32 devices in a mesh: groups: 2 (over x), render: 4 (over y, core), view: 4 (over z).
Axes of the slice: x: 2, y: 2, z: 4, core: 2. Of those that a mesh axis runs over, the one named last changes fastest.
Arguments:
- params: float32 [59, 32768], P(None, ('groups', 'render')), parts along dimension 1, may hold values from -6 to 1.5, as said below
- cameras: float32 [32, 7], P(('groups', 'view')), parts along dimension 0, may hold values from -0.2 to 170, as said below
- send_index: int32 [8, 4, 4, 512], P(('groups', 'render'), 'view'), parts along dimension 0, may hold values from 0 to 4095, as said below
- tile_id: int32 [8, 4, 8], P(('groups', 'render'), 'view'), parts along dimension 0, may hold values from 0 to 15
- tile_count: int32 [8, 4, 8], P(('groups', 'render'), 'view'), parts along dimension 0, may hold values from 1 to 512, as said below
- tile_slot: int32 [8, 4, 8, 512], P(('groups', 'render'), 'view'), parts along dimension 0, may hold values from 0 to 2047, as said below
- targets: float32 [8, 4, 8, 3, 256], P(('groups', 'render'), 'view'), parts along dimension 0, may hold values from 0 to 1
Outputs:
- image: float32 [8, 4, 8, 3, 256], P(('groups', 'render'), 'view'), parts along dimension 0
- gradients: float32 [59, 32768], P(None, ('groups', 'render', 'view')), parts along dimension 1
The draws below stay inside these ranges and needn't reach their ends.
There are 2 independent parts, one for each index of `groups`. The reference program is written for one: setup_inputs(seed, part) draws one part's arguments, and reference() takes and returns one part's arrays. A program takes and returns all parts, laid end to end along the dimension named above; each array names one. Nothing has to cross between parts.
Inputs may be any that keep to these rules, and one draw needn't show every extreme that they name: `params`: row ranges: 0-2 in -0.1 to 0.1, 3-5 in log 0.2 to log 0.6, 6 in 0.5 to 1.5, 7-9 in -1 to 1, 10 in -6 to -4, colour rows of basis index 0 in -1 to 1, the others in -0.5 to 0.5. `cameras`: columns 0-2 in -0.2 to 0.2, 3-4 in -0.05 to 0.05, 5 in 3.5 to 4.5, 6 in 130 to 170. `send_index`: the 512 rows of one slab, view column and renderer are distinct. `tile_count`: every device has a tile with exactly 512 live entries. `tile_slot`: the 512 entries of one tile are distinct.
All inputs are finite; a program needn't handle non-finite values.
Results may differ from the reference program's by a relative error of at most 0.0003.
Values sent between devices are 32-bit elements; how exact they have to be, the bound alone decides.
No kernel may reach another device: no remote copies, remote signals or barrier semaphores. Data moves between devices by JAX's collectives and lax.ppermute only.
A program may use at most 64 MiB of HBM per device.

```python
import math
import jax
import jax.numpy as jnp
from jax import lax

GS_DEV = 4096
CAP = 512
TILE_DEV = 8
VIEW_DEV = 4
LIST_MAX = 512
CROP = 2
GAUSSIANS = 16384
SLOTS = 2048
VIEWS = 16
N_RENDER = 4
N_VIEW = 4


def draw_params(key, part):
    key = jax.random.fold_in(key, 11)
    lower_end = [-0.1] * 3 + [math.log(0.2)] * 3 + [0.5, -1.0, -1.0, -1.0] + [-6.0] + ([-1.0] + [-0.5] * 15) * 3
    upper_end = [0.1] * 3 + [math.log(0.6)] * 3 + [1.5, 1.0, 1.0, 1.0] + [-4.0] + ([1.0] + [0.5] * 15) * 3
    bottom = jnp.array(lower_end, jnp.float32)[:, None]
    upper = jnp.array(upper_end, jnp.float32)[:, None]
    spread = jax.random.uniform(key, (59, GAUSSIANS), jnp.float32)
    return bottom + (upper - bottom) * spread


def draw_cameras(key, part):
    key = jax.random.fold_in(key, 17)
    bottom = jnp.array([-0.2, -0.2, -0.2, -0.05, -0.05, 3.5, 130.0], jnp.float32)[None, :]
    upper = jnp.array([0.2, 0.2, 0.2, 0.05, 0.05, 4.5, 170.0], jnp.float32)[None, :]
    spread = jax.random.uniform(key, (VIEWS, 7), jnp.float32)
    return bottom + (upper - bottom) * spread


def draw_send_index(key, part):
    key = jax.random.fold_in(key, 23)
    total_lists = N_RENDER * N_VIEW * N_RENDER
    keys_all = jax.random.split(key, total_lists)
    chosen = jax.vmap(lambda one_key: jax.random.permutation(one_key, GS_DEV)[:CAP])(keys_all)
    return chosen.reshape(N_RENDER, N_VIEW, N_RENDER, CAP).astype(jnp.int32)


def draw_tile_slot(key, part):
    key = jax.random.fold_in(key, 29)
    total_lists = N_RENDER * N_VIEW * TILE_DEV
    keys_all = jax.random.split(key, total_lists)
    chosen = jax.vmap(lambda one_key: jax.random.permutation(one_key, SLOTS)[:LIST_MAX])(keys_all)
    return chosen.reshape(N_RENDER, N_VIEW, TILE_DEV, LIST_MAX).astype(jnp.int32)


def draw_tile_count(key, part):
    key = jax.random.fold_in(key, 37)
    first_key, second_key, third_key = jax.random.split(key, 3)
    floor_dev = jax.random.randint(first_key, (N_RENDER, N_VIEW, 1), LIST_MAX // 8, LIST_MAX)
    counts = jax.random.randint(second_key, (N_RENDER, N_VIEW, TILE_DEV), floor_dev, LIST_MAX + 1)
    full_at = jax.random.randint(third_key, (N_RENDER, N_VIEW, 1), 0, TILE_DEV)
    position = jnp.arange(TILE_DEV, dtype=jnp.int32)[None, None, :]
    return jnp.where(position == full_at, LIST_MAX, counts).astype(jnp.int32)


def plant(values, rng, smallest, top_value):
    spot = [jax.random.randint(jax.random.fold_in(rng, axis), (), 0, length) for axis, length in enumerate(values.shape)]
    main_axis = values.shape.index(max(values.shape))
    beside = spot[:main_axis] + [(spot[main_axis] + 1) % values.shape[main_axis]] + spot[main_axis + 1:]
    return values.at[tuple(spot)].set(smallest).at[tuple(beside)].set(top_value)


def steps_of(own_key, shape, cuts, least, top_value):
    level = 1.0
    for dim, parts in cuts:
        heights = jax.random.uniform(jax.random.fold_in(jax.random.fold_in(own_key, 6), dim), (parts,), jnp.float32, least / len(cuts), top_value / len(cuts))
        level = level * jnp.repeat(jnp.exp(heights), shape[dim] // parts).reshape((-1,) + (1,) * (len(shape) - 1 - dim))
    return level


def setup_inputs(seed: int = 0, part: int = 0) -> dict:
    splits = jax.random.split(jax.random.key(seed), 8)
    own_keys = jax.random.split(jax.random.fold_in(splits[7], part), 8)
    params = draw_params(jax.random.fold_in(jax.random.fold_in(splits[7], part), 71), part)
    cameras = draw_cameras(jax.random.fold_in(jax.random.fold_in(splits[7], part), 71), part)
    send_index = draw_send_index(jax.random.fold_in(jax.random.fold_in(splits[7], part), 71), part)
    tile_id = plant(jax.random.randint(own_keys[3], (N_RENDER, N_VIEW, TILE_DEV), 0, VIEW_DEV * CROP * CROP), jax.random.fold_in(own_keys[3], 1), 0, (VIEW_DEV * CROP * CROP) - 1).astype(jnp.int32)
    tile_count = draw_tile_count(jax.random.fold_in(jax.random.fold_in(splits[7], part), 71), part)
    tile_slot = draw_tile_slot(jax.random.fold_in(jax.random.fold_in(splits[7], part), 71), part)
    targets = jnp.clip(1.0 * jax.random.uniform(own_keys[6], (N_RENDER, N_VIEW, TILE_DEV, 3, 256), jnp.float32) ** steps_of(own_keys[6], (N_RENDER, N_VIEW, TILE_DEV, 3, 256), ((0, 4), (1, 4)), -0.2, 0.2), 0.0, 1.0)
    return {"params": params, "cameras": cameras, "send_index": send_index, "tile_id": tile_id, "tile_count": tile_count, "tile_slot": tile_slot, "targets": targets}


dilation = 0.3
backdrop = 1.0
band_zero = 0.28209479177387814
band_one = 0.4886025119029199
band_two = [1.0925484305920792, -1.0925484305920792, 0.31539156525252005, -1.0925484305920792, 0.5462742152960396]
band_three = [-0.5900435899266435, 2.890611442640554, -0.4570457994644658, 0.3731763325901154, -0.4570457994644658, 1.445305721320277, -0.5900435899266435]

def harmonic_basis(direction):
    along_x, along_y, along_z = (direction[0], direction[1], direction[2])
    square_x = along_x * along_x
    square_y = along_y * along_y
    square_z = along_z * along_z
    constant = band_zero + 0.0 * along_x
    return [constant, -band_one * along_y, band_one * along_z, -band_one * along_x, band_two[0] * along_x * along_y, band_two[1] * along_y * along_z, band_two[2] * (2.0 * square_z - square_x - square_y), band_two[3] * along_x * along_z, band_two[4] * (square_x - square_y), band_three[0] * along_y * (3.0 * square_x - square_y), band_three[1] * along_x * along_y * along_z, band_three[2] * along_y * (4.0 * square_z - square_x - square_y), band_three[3] * along_z * (2.0 * square_z - 3.0 * square_x - 3.0 * square_y), band_three[4] * along_x * (4.0 * square_z - square_x - square_y), band_three[5] * along_z * (square_x - square_y), band_three[6] * along_x * (square_x - 3.0 * square_y)]

def project(raw_rows, frame):
    position = [raw_rows[0], raw_rows[1], raw_rows[2]]
    extent = [jnp.exp(raw_rows[3]), jnp.exp(raw_rows[4]), jnp.exp(raw_rows[5])]
    quat_raw = [raw_rows[6], raw_rows[7], raw_rows[8], raw_rows[9]]
    quat_norm = jnp.sqrt(sum((member * member for member in quat_raw)))
    quat = [member / quat_norm for member in quat_raw]
    opacity = jax.nn.sigmoid(raw_rows[10])
    cosine = [jnp.cos(frame[0]), jnp.cos(frame[1]), jnp.cos(frame[2])]
    sine = [jnp.sin(frame[0]), jnp.sin(frame[1]), jnp.sin(frame[2])]
    rotation = [[cosine[1] * cosine[2], sine[0] * sine[1] * cosine[2] - cosine[0] * sine[2], cosine[0] * sine[1] * cosine[2] + sine[0] * sine[2]], [cosine[1] * sine[2], sine[0] * sine[1] * sine[2] + cosine[0] * cosine[2], cosine[0] * sine[1] * sine[2] - sine[0] * cosine[2]], [-sine[1], sine[0] * cosine[1], cosine[0] * cosine[1]]]
    camera_pt = [rotation[across][0] * position[0] + rotation[across][1] * position[1] + rotation[across][2] * position[2] + frame[3 + across] for across in range(3)]
    inv_depth = 1.0 / camera_pt[2]
    focal = frame[6]
    centre = CROP * 8.0
    screen_u = focal * camera_pt[0] * inv_depth + centre
    screen_v = focal * camera_pt[1] * inv_depth + centre
    quat_rot = [[1.0 - 2.0 * (quat[2] * quat[2] + quat[3] * quat[3]), 2.0 * (quat[1] * quat[2] - quat[0] * quat[3]), 2.0 * (quat[1] * quat[3] + quat[0] * quat[2])], [2.0 * (quat[1] * quat[2] + quat[0] * quat[3]), 1.0 - 2.0 * (quat[1] * quat[1] + quat[3] * quat[3]), 2.0 * (quat[2] * quat[3] - quat[0] * quat[1])], [2.0 * (quat[1] * quat[3] - quat[0] * quat[2]), 2.0 * (quat[2] * quat[3] + quat[0] * quat[1]), 1.0 - 2.0 * (quat[1] * quat[1] + quat[2] * quat[2])]]
    spread = [[quat_rot[across][within] * extent[within] for within in range(3)] for across in range(3)]
    depth_term = [focal * camera_pt[0] * inv_depth * inv_depth, focal * camera_pt[1] * inv_depth * inv_depth]
    screen_rot = [[focal * inv_depth * rotation[across][within] - depth_term[across] * rotation[2][within] for within in range(3)] for across in range(2)]
    footprint = [[sum((screen_rot[across][middle] * spread[middle][within] for middle in range(3))) for within in range(3)] for across in range(2)]
    cov_a = sum((footprint[0][within] * footprint[0][within] for within in range(3))) + dilation
    cov_b = sum((footprint[0][within] * footprint[1][within] for within in range(3)))
    cov_c = sum((footprint[1][within] * footprint[1][within] for within in range(3))) + dilation
    determinant = cov_a * cov_c - cov_b * cov_b
    conic_a = cov_c / determinant
    conic_b = -cov_b / determinant
    conic_c = cov_a / determinant
    distance = jnp.sqrt(sum((member * member for member in camera_pt)))
    direction = [sum((rotation[middle][across] * camera_pt[middle] for middle in range(3))) / distance for across in range(3)]
    basis = harmonic_basis(direction)
    colour = [0.5 + sum((basis[level] * raw_rows[11 + 16 * channel + level] for level in range(16))) for channel in range(3)]
    pieces = jnp.broadcast_arrays(screen_u, screen_v, conic_a, conic_b, conic_c, colour[0], colour[1], colour[2], opacity)
    return jnp.stack(pieces)

def exclusive_sum(log_keep):
    return jnp.cumsum(log_keep, axis=0) - log_keep

def blend_tile(tile_feat, tile_code, live_count):
    list_len = tile_feat.shape[1]
    crop_cell = tile_code % (CROP * CROP)
    tile_row = crop_cell // CROP
    tile_col = crop_cell % CROP
    pixel = jnp.arange(256, dtype=jnp.int32)
    pixel_x = (tile_col * 16 + pixel % 16).astype(jnp.float32) + 0.5
    pixel_y = (tile_row * 16 + pixel // 16).astype(jnp.float32) + 0.5
    offset_x = pixel_x[None, :] - tile_feat[0][:, None]
    offset_y = pixel_y[None, :] - tile_feat[1][:, None]
    power = -0.5 * (tile_feat[2][:, None] * offset_x * offset_x + tile_feat[4][:, None] * offset_y * offset_y) - tile_feat[3][:, None] * offset_x * offset_y
    live = (jnp.arange(list_len, dtype=jnp.int32) < live_count).astype(jnp.float32)
    alpha = tile_feat[8][:, None] * jnp.exp(power) * live[:, None]
    log_keep = jnp.log1p(-alpha)
    before = exclusive_sum(log_keep)
    weight = jnp.exp(before) * alpha
    colour = jnp.dot(tile_feat[5:8], weight, precision=lax.Precision.HIGHEST)
    remain = jnp.exp(lax.optimization_barrier(jnp.sum(log_keep, axis=0)))
    return colour + backdrop * remain[None, :]

def reference(params, cameras, send_index, tile_id, tile_count, tile_slot, targets):

    def device_image(weights, flat_index):
        renderer_rank = flat_index // N_VIEW
        column = flat_index % N_VIEW
        chosen = send_index[:, column, renderer_rank, :]
        owners = jnp.arange(N_RENDER, dtype=jnp.int32)[:, None] * GS_DEV
        global_ids = (owners + chosen).reshape(-1)
        entries = global_ids[tile_slot[renderer_rank, column]]
        raw_rows = weights[:, entries]
        view_cams = lax.dynamic_slice_in_dim(cameras, (column * VIEW_DEV).astype(jnp.int32), VIEW_DEV, 0)
        tile_codes = tile_id[renderer_rank, column]
        live_counts = tile_count[renderer_rank, column]
        tile_cams = view_cams[tile_codes // (CROP * CROP)]

        def per_tile(raw_tile, cam_tile, tile_code, live_count):
            return blend_tile(project(raw_tile, cam_tile[:, None]), tile_code, live_count)
        return jax.vmap(per_tile, in_axes=(1, 0, 0, 0))(raw_rows, tile_cams, tile_codes, live_counts)
    checked = jax.checkpoint(device_image)

    def photometric(weights):
        images = lax.map(lambda flat_index: checked(weights, flat_index), jnp.arange(N_RENDER * N_VIEW, dtype=jnp.int32))
        images = images.reshape(N_RENDER, N_VIEW, TILE_DEV, 3, 256)
        residual = images - targets
        return (0.5 * jnp.sum(residual * residual), images)
    gradient_rows, images = jax.grad(photometric, has_aux=True)(params)
    return (images, gradient_rows)
```

```python
from functools import partial

import jax
import jax.numpy as jnp
from jax import lax
from jax.experimental import pallas as pl
from jax.experimental.pallas import tpu as pltpu
from jax.sharding import PartitionSpec as P

CROP = 2
PIXELS = 256
GEOMETRY = 11
COLOUR_ROW = 12
SPAN = 256
LOG2_E = 1.4426950408889634
DEAD = -1e30

dilation = 0.3
backdrop = 1.0
band_zero = 0.28209479177387814
band_one = 0.4886025119029199
band_two = [
    1.0925484305920792,
    -1.0925484305920792,
    0.31539156525252005,
    -1.0925484305920792,
    0.5462742152960396,
]
band_three = [
    -0.5900435899266435,
    2.890611442640554,
    -0.4570457994644658,
    0.3731763325901154,
    -0.4570457994644658,
    1.445305721320277,
    -0.5900435899266435,
]

F32 = jnp.float32
BF16 = jnp.bfloat16


def harmonic_basis(along_x, along_y, along_z):
    square_x = along_x * along_x
    square_y = along_y * along_y
    square_z = along_z * along_z
    return [
        jnp.full_like(along_x, band_zero),
        -band_one * along_y,
        band_one * along_z,
        -band_one * along_x,
        band_two[0] * along_x * along_y,
        band_two[1] * along_y * along_z,
        band_two[2] * (2.0 * square_z - square_x - square_y),
        band_two[3] * along_x * along_z,
        band_two[4] * (square_x - square_y),
        band_three[0] * along_y * (3.0 * square_x - square_y),
        band_three[1] * along_x * along_y * along_z,
        band_three[2] * along_y * (4.0 * square_z - square_x - square_y),
        band_three[3] * along_z * (2.0 * square_z - 3.0 * square_x - 3.0 * square_y),
        band_three[4] * along_x * (4.0 * square_z - square_x - square_y),
        band_three[5] * along_z * (square_x - square_y),
        band_three[6] * along_x * (square_x - 3.0 * square_y),
    ]


def high_low(value):
    high = value.astype(BF16).astype(F32)
    return high, value - high


def dot_plain(left, right):
    return lax.dot_general(left, right, (((1,), (0,)), ((), ())), preferred_element_type=F32)


def dot_lanes(left, right):
    return lax.dot_general(left, right, (((1,), (1,)), ((), ())), preferred_element_type=F32)


def camera_table(cameras):
    cosine, sine = jnp.cos(cameras[:, :3]), jnp.sin(cameras[:, :3])
    c0, c1, c2 = cosine[:, 0], cosine[:, 1], cosine[:, 2]
    s0, s1, s2 = sine[:, 0], sine[:, 1], sine[:, 2]
    rotation = [
        [c1 * c2, s0 * s1 * c2 - c0 * s2, c0 * s1 * c2 + s0 * s2],
        [c1 * s2, s0 * s1 * s2 + c0 * c2, c0 * s1 * s2 - s0 * c2],
        [-s1, s0 * c1, c0 * c1],
    ]
    shift = [cameras[:, 3], cameras[:, 4], cameras[:, 5]]
    origin = [sum(rotation[m][a] * shift[m] for m in range(3)) for a in range(3)]
    return jnp.stack([e for row in rotation for e in row] + shift + [cameras[:, 6]] + origin, 1)


def lane_pick(source, lanes):
    return jnp.take_along_axis(source, lanes, axis=1, mode="promise_in_bounds")


def slab_kernel(n_render, views, params_ref, table_ref, index_ref, *rest):
    outs, dense_ref = rest[:n_render], rest[n_render]
    rows, gaussians = dense_ref.shape
    cap = index_ref.shape[1]
    width = 256

    def shade(step, _):
        lanes = pl.ds(pl.multiple_of(step * width, width), width)
        dense_ref[0:16, lanes] = params_ref[0:16, lanes]
        away = [params_ref[a : a + 1, lanes] + table_ref[:, 13 + a : 14 + a] for a in range(3)]
        inverse = lax.rsqrt(away[0] * away[0] + away[1] * away[1] + away[2] * away[2])
        basis = harmonic_basis(*[part * inverse for part in away])
        for channel in range(3):
            base = GEOMETRY + 16 * channel
            colour = 0.5 + basis[0] * params_ref[base : base + 1, lanes]
            for level in range(1, 16):
                colour += basis[level] * params_ref[base + level : base + level + 1, lanes]
            first = COLOUR_ROW + channel * views
            dense_ref[first : first + views, lanes] = colour
        return 0

    lax.fori_loop(0, gaussians // width, shade, 0)

    for turn in range(n_render):

        def pick(step, _):
            lanes = pl.ds(pl.multiple_of(step * 128, 128), 128)
            index = jnp.broadcast_to(index_ref[turn : turn + 1, lanes], (8, 128))
            lane, block = index & 127, index >> 7
            found = [jnp.zeros((8, 128), F32) for _ in range(rows // 8)]
            for b in range(gaussians // 128):
                here = block == b
                for s in range(rows // 8):
                    piece = dense_ref[8 * s : 8 * s + 8, 128 * b : 128 * b + 128]
                    found[s] = jnp.where(here, lane_pick(piece, lane), found[s])
            for s in range(rows // 8):
                outs[turn][8 * s : 8 * s + 8, lanes] = found[s]
            return 0

        lax.fori_loop(0, cap // 128, pick, 0)


def entry_coefficients(raw, cam):
    px, py, pz = raw[0], raw[1], raw[2]
    extent = [jnp.exp(raw[3 + a]) for a in range(3)]
    norm = lax.rsqrt(raw[6] * raw[6] + raw[7] * raw[7] + raw[8] * raw[8] + raw[9] * raw[9])
    qw, qx, qy, qz = [raw[6 + a] * norm for a in range(4)]
    turn = [[cam[3 * a + b] for b in range(3)] for a in range(3)]
    x, y, z = [turn[a][0] * px + turn[a][1] * py + turn[a][2] * pz + cam[9 + a] for a in range(3)]
    scale = cam[12] / z
    slope_x, slope_y = x / z, y / z
    u = cam[12] * slope_x + cam[13]
    v = cam[12] * slope_y + cam[14]
    quat = [
        [1.0 - 2.0 * (qy * qy + qz * qz), 2.0 * (qx * qy - qw * qz), 2.0 * (qx * qz + qw * qy)],
        [2.0 * (qx * qy + qw * qz), 1.0 - 2.0 * (qx * qx + qz * qz), 2.0 * (qy * qz - qw * qx)],
        [2.0 * (qx * qz - qw * qy), 2.0 * (qy * qz + qw * qx), 1.0 - 2.0 * (qx * qx + qy * qy)],
    ]
    screen = [
        [scale * (turn[a][b] - slope * turn[2][b]) for b in range(3)]
        for a, slope in ((0, slope_x), (1, slope_y))
    ]
    foot = [
        [sum(screen[a][m] * quat[m][b] for m in range(3)) * extent[b] for b in range(3)]
        for a in range(2)
    ]
    cov_a = sum(foot[0][b] * foot[0][b] for b in range(3)) + dilation
    cov_b = sum(foot[0][b] * foot[1][b] for b in range(3))
    cov_c = sum(foot[1][b] * foot[1][b] for b in range(3)) + dilation
    inverse = 1.0 / (cov_a * cov_c - cov_b * cov_b)
    conic_a, conic_b, conic_c = cov_c * inverse, -cov_b * inverse, cov_a * inverse
    log_opacity = -jnp.log(1.0 + jnp.exp(-raw[10]))
    pull_x = conic_a * u + conic_b * v
    pull_y = conic_c * v + conic_b * u
    return [
        -0.5 * conic_a,
        -conic_b,
        -0.5 * conic_c,
        pull_x,
        pull_y,
        log_opacity - 0.5 * (pull_x * u + pull_y * v),
    ]


def monomials(rows):
    row = lax.broadcasted_iota(jnp.int32, (rows, PIXELS), 0) & 7
    pixel = lax.broadcasted_iota(jnp.int32, (rows, PIXELS), 1)
    x = (pixel & 15).astype(F32) - 7.5
    y = (pixel >> 4).astype(F32) - 7.5
    value = jnp.where(row == 0, x * x, 0.0)
    for number, term in ((1, x * y), (2, y * y), (3, x), (4, y), (5, jnp.ones_like(x))):
        value = jnp.where(row == number, term, value)
    return value


def render_kernel(n_render, views, where_ref, *refs):
    blocks, refs = refs[:n_render], refs[n_render:]
    slot_ref, cam_ref, target_ref, refs = refs[0], refs[1], refs[2], refs[3:]
    image_ref, outs, refs = refs[0], refs[1 : 1 + n_render], refs[1 + n_render :]
    raw_ref, stack_ref, wide_ref, tall_ref, alpha_ref, weight_ref, high_ref, low_ref, lhs_ref, acc_ref = refs
    tiles = target_ref.shape[0]
    entry_rows = slot_ref.shape[0]
    entries = entry_rows * 128
    cap = blocks[0].shape[1]
    rows = blocks[0].shape[0]
    per_block = cap // 128
    me = where_ref[0]
    groups = entry_rows // 8

    def fetch(group, _):
        here = pl.ds(pl.multiple_of(group * 8, 8), 8)
        slot = slot_ref[here, :]
        lane, block = slot & 127, slot >> 7
        view = jnp.broadcast_to(cam_ref[15:16, :], (8, 128)).astype(jnp.int32)
        found = [jnp.zeros((8, 128), F32) for _ in range(GEOMETRY + 3)]
        for turn in range(n_render):
            first = (me ^ turn) * per_block
            for j in range(per_block):
                hit = block == first + j
                cut = slice(128 * j, 128 * j + 128)
                for p in range(GEOMETRY):
                    piece = jnp.broadcast_to(blocks[turn][p : p + 1, cut], (8, 128))
                    found[p] = jnp.where(hit, lane_pick(piece, lane), found[p])
                for w in range(views):
                    seen = hit & (view == w)
                    for channel in range(3):
                        p = COLOUR_ROW + channel * views + w
                        piece = jnp.broadcast_to(blocks[turn][p : p + 1, cut], (8, 128))
                        at = GEOMETRY + channel
                        found[at] = jnp.where(seen, lane_pick(piece, lane), found[at])
        for p in range(GEOMETRY + 3):
            raw_ref[p, here, :] = found[p]
        return 0

    lax.fori_loop(0, groups, fetch, 0)

    def cam_rows():
        return [jnp.broadcast_to(cam_ref[i : i + 1, :], (8, 128)) for i in range(15)]

    stack_ref[...] = jnp.zeros_like(stack_ref)

    def forward_entries(group, _):
        here = pl.ds(pl.multiple_of(group * 8, 8), 8)
        coefficient = entry_coefficients([raw_ref[p, here, :] for p in range(GEOMETRY)], cam_rows())
        row = lax.broadcasted_iota(jnp.int32, (8, 128), 0) + group * 8
        lane = lax.broadcasted_iota(jnp.int32, (8, 128), 1)
        order = (row * 128 + lane) // tiles
        live = order < jnp.broadcast_to(cam_ref[16:17, :], (8, 128)).astype(jnp.int32)
        for c in range(6):
            value = coefficient[c] * LOG2_E
            if c == 5:
                value = jnp.where(live, value, DEAD)
            at = pl.ds(pl.multiple_of(c * entry_rows + group * 8, 8), 8)
            stack_ref[at, :] = value
        for channel in range(3):
            at = pl.ds(pl.multiple_of((8 + channel) * entry_rows + group * 8, 8), 8)
            stack_ref[at, :] = raw_ref[GEOMETRY + channel, here, :]
        return 0

    lax.fori_loop(0, groups, forward_entries, 0)

    wide_ref[96:128, :] = jnp.zeros((32, entries), BF16)
    own_tile = (lax.broadcasted_iota(jnp.int32, (8, 128), 1) & (tiles - 1)) == lax.broadcasted_iota(
        jnp.int32, (8, 128), 0
    )

    def widen(row, _):
        value = stack_ref[pl.ds(row, 16, stride=entry_rows), :]
        high, rest = high_low(value)
        middle, low = high_low(rest)

        def spread(part):
            return [
                jnp.where(own_tile, jnp.broadcast_to(part[8 + ch : 9 + ch, :], (8, 128)), 0.0)
                for ch in range(3)
            ]

        pieces = [high[0:8], middle[0:8], low[0:8]] + spread(high) * 2 + spread(middle)
        lanes = pl.ds(pl.multiple_of(row * 128, 128), 128)
        wide_ref[0:96, lanes] = jnp.concatenate(pieces, axis=0).astype(BF16)
        return 0

    lax.fori_loop(0, entry_rows, widen, 0)

    eye = (
        lax.broadcasted_iota(jnp.int32, (256, 256), 0) == lax.broadcasted_iota(jnp.int32, (256, 256), 1)
    ).astype(F32).astype(BF16)
    left = jnp.concatenate([monomials(24), jnp.zeros((104, PIXELS), F32)], axis=0).astype(BF16)
    moment_rows = monomials(16)
    moment_rows = jnp.where(
        lax.broadcasted_iota(jnp.int32, (16, PIXELS), 0) < 8, moment_rows, 0.0
    ).astype(BF16)
    steps = 256 // tiles

    def forward(chunk, carry):
        passing, image = carry
        at = pl.ds(pl.multiple_of(chunk * 256, 256), 256)
        tall = dot_lanes(eye, wide_ref[:, at]).astype(BF16)
        tall_ref[at, :] = tall
        alpha = jnp.exp2(dot_plain(tall, left))
        alpha_ref[at, :] = alpha
        weights = []
        for k in range(steps):
            weight = passing * alpha[tiles * k : tiles * k + tiles, :]
            passing = passing - weight
            weights.append(weight)
        weight = jnp.concatenate(weights, axis=0)
        weight_ref[at, :] = weight
        high, low = high_low(weight)
        high, low = high.astype(BF16), low.astype(BF16)
        high_ref[at, :] = high
        low_ref[at, :] = low
        colours = wide_ref[48:96, at]
        image = image + (dot_plain(colours, high) + dot_plain(colours, low))
        return passing, image

    remain, image = lax.fori_loop(
        0,
        entries // 256,
        forward,
        (jnp.ones((tiles, PIXELS), F32), jnp.zeros((48, PIXELS), F32)),
    )
    image = image[0:24] + image[24:48]
    residual = []
    for channel in range(3):
        shown = image[8 * channel : 8 * channel + 8] + backdrop * remain
        image_ref[:, channel, :] = shown
        residual.append(shown - target_ref[:, channel, :])
    behind = backdrop * (residual[0] + residual[1] + residual[2])
    high, low = high_low(jnp.concatenate(residual, axis=0))
    zeros = jnp.zeros((24, PIXELS), F32)
    right = jnp.concatenate([zeros, high, low, high, jnp.zeros((32, PIXELS), F32)], axis=0).astype(BF16)
    both = jnp.concatenate([high, low], axis=0).astype(BF16)
    own_wide = (lax.broadcasted_iota(jnp.int32, (8, 256), 1) & (tiles - 1)) == lax.broadcasted_iota(
        jnp.int32, (8, 256), 0
    )

    def backward(step, behind):
        chunk = entries // 256 - 1 - step
        at = pl.ds(pl.multiple_of(chunk * 256, 256), 256)
        shade = dot_plain(tall_ref[at, :], right)
        alpha, weight = alpha_ref[at, :], weight_ref[at, :]
        slopes = [None] * steps
        for k in reversed(range(steps)):
            cut = slice(tiles * k, tiles * k + tiles)
            gap = shade[cut, :] - behind
            slopes[k] = weight[cut, :] * gap
            behind = behind + alpha[cut, :] * gap
        high, low = high_low(jnp.concatenate(slopes, axis=0))
        moments = dot_lanes(moment_rows, high.astype(BF16)) + dot_lanes(moment_rows, low.astype(BF16))
        tint = dot_lanes(both, high_ref[at, :]) + dot_lanes(both, low_ref[at, :])
        tint = tint[0:24] + tint[24:48]
        for half in range(2):
            row = chunk * 2 + half
            cut = slice(128 * half, 128 * half + 128)
            stack_ref[pl.ds(row, 8, stride=entry_rows), :] = moments[0:8, cut]
            for channel in range(3):
                part = jnp.where(own_tile, tint[8 * channel : 8 * channel + 8, cut], 0.0)
                stack_ref[pl.ds((8 + channel) * entry_rows + row, 1), :] = jnp.sum(
                    part, axis=0, keepdims=True
                )
        return behind

    lax.fori_loop(0, entries // 256, backward, behind)

    def backward_entries(group, _):
        here = pl.ds(pl.multiple_of(group * 8, 8), 8)
        cam = cam_rows()
        given = [
            stack_ref[pl.ds(pl.multiple_of(c * entry_rows + group * 8, 8), 8), :] for c in range(6)
        ]
        _, pull = jax.vjp(
            lambda raw: entry_coefficients(raw, cam), [raw_ref[p, here, :] for p in range(GEOMETRY)]
        )
        (grads,) = pull(given)
        for channel in range(3):
            at = pl.ds(pl.multiple_of((8 + channel) * entry_rows + group * 8, 8), 8)
            grads.append(stack_ref[at, :])
        for p in range(GEOMETRY + 3):
            high, low = high_low(grads[p])
            raw_ref[p, here, :] = high
            raw_ref[GEOMETRY + 3 + p, here, :] = low
        return 0

    lax.fori_loop(0, groups, backward_entries, 0)

    spans = n_render * cap // SPAN
    acc_ref[...] = jnp.zeros_like(acc_ref)
    view = cam_ref[15:16, :].astype(jnp.int32)
    view = jnp.concatenate([view] * 4, axis=1)

    def scatter(step, _):
        def line(ref, *lead):
            return jnp.concatenate(
                [ref[lead + (pl.ds(step * 4 + i, 1), slice(None))] for i in range(4)], axis=1
            )

        slot = line(slot_ref)
        span, lane = slot // SPAN, slot & (SPAN - 1)
        lanes_of = jnp.where(
            lax.broadcasted_iota(jnp.int32, (SPAN, 512), 0) == jnp.broadcast_to(lane, (SPAN, 512)), 1.0, 0.0
        ).astype(BF16)
        in_span = lax.broadcasted_iota(jnp.int32, (spans, 512), 0) == jnp.broadcast_to(span, (spans, 512))
        key = view * spans + span
        in_view = lax.broadcasted_iota(jnp.int32, (views * spans, 512), 0) == jnp.broadcast_to(
            key, (views * spans, 512)
        )
        half_rows = rows * spans
        for part in range(2):
            base = part * half_rows
            pieces = []
            for p in range(COLOUR_ROW):
                if p < GEOMETRY:
                    value = line(raw_ref, part * (GEOMETRY + 3) + p)
                    value = jnp.broadcast_to(value, (spans, 512))
                    pieces.append(jnp.where(in_span, value, 0.0))
                else:
                    pieces.append(jnp.zeros((spans, 512), F32))
                if len(pieces) == 2:
                    at = base + (p - 1) * spans
                    lhs_ref[at : at + 2 * spans, :] = jnp.concatenate(pieces, axis=0).astype(BF16)
                    pieces = []
            for channel in range(3):
                value = line(raw_ref, part * (GEOMETRY + 3) + GEOMETRY + channel)
                value = jnp.where(in_view, jnp.broadcast_to(value, (views * spans, 512)), 0.0)
                at = base + (COLOUR_ROW + channel * views) * spans
                lhs_ref[at : at + views * spans, :] = value.astype(BF16)
        product = dot_lanes(lhs_ref[...], lanes_of)
        for half in range(SPAN // 128):
            at = slice(half * 2 * half_rows, (half + 1) * 2 * half_rows)
            acc_ref[at, :] += product[:, 128 * half : 128 * half + 128]
        return 0

    lax.fori_loop(0, entry_rows // 4, scatter, 0)
    for turn in range(n_render):
        for part in range(cap // SPAN):
            span = (me ^ turn) * (cap // SPAN) + part
            for half in range(SPAN // 128):
                cut = slice(128 * half, 128 * half + 128)
                total = (
                    acc_ref[pl.ds(half * 2 * rows * spans + span, rows, stride=spans), :]
                    + acc_ref[pl.ds(half * 2 * rows * spans + rows * spans + span, rows, stride=spans), :]
                )
                first = part * SPAN + 128 * half
                outs[turn][:, first : first + 128] = total


def collect_kernel(n_render, n_view, where_ref, *refs):
    blocks, refs = refs[:n_render], refs[n_render:]
    index_ref, origin_ref, refs = refs[0], refs[1], refs[2:]
    outs, (lhs_ref, acc_ref) = refs[:n_view], refs[n_view:]
    rows, cap = blocks[0].shape
    own = outs[0].shape[0] // rows * 128
    gaussians = own * n_view
    spans = gaussians // SPAN
    column = where_ref[1]
    for turn in range(n_render):
        index = index_ref[turn : turn + 1, :]
        span, lane = index // SPAN, index & (SPAN - 1)
        lanes_of = jnp.where(
            lax.broadcasted_iota(jnp.int32, (SPAN, cap), 0) == jnp.broadcast_to(lane, (SPAN, cap)), 1.0, 0.0
        ).astype(BF16)
        in_span = lax.broadcasted_iota(jnp.int32, (spans, cap), 0) == jnp.broadcast_to(span, (spans, cap))
        high, low = high_low(blocks[turn][...])
        for part, value in ((0, high), (1, low)):
            for p in range(rows):
                at = (part * rows + p) * spans
                piece = jnp.broadcast_to(value[p : p + 1, :], (spans, cap))
                lhs_ref[at : at + spans, :] = jnp.where(in_span, piece, 0.0).astype(BF16)
        product = dot_lanes(lhs_ref[...], lanes_of)
        for half in range(2):
            at = slice(half * 2 * rows * spans, (half + 1) * 2 * rows * spans)
            piece = product[:, 128 * half : 128 * half + 128]
            if turn == 0:
                acc_ref[at, :] = piece
            else:
                acc_ref[at, :] += piece
    strips = own // 128
    for turn in range(n_view):
        for strip in range(strips):
            span = (column ^ turn) * (own // SPAN) + strip // 2
            first = (strip % 2) * 2 * rows * spans
            total = (
                acc_ref[pl.ds(first + span, rows, stride=spans), :]
                + acc_ref[pl.ds(first + rows * spans + span, rows, stride=spans), :]
            )
            outs[turn][pl.ds(strip, rows, stride=strips), :] = total
        outs[turn][GEOMETRY * strips : GEOMETRY * strips + 1, :] = origin_ref[...]


def owner_kernel(n_view, views, *refs):
    blocks, (own_ref, out_ref, sum_ref) = refs[:n_view], refs[n_view:]
    strips = out_ref.shape[1] // 128

    def of(ref, p):
        return ref[p * strips : (p + 1) * strips, :]

    position = [of(own_ref, a) for a in range(3)]
    levels = [[None] * 16 for _ in range(3)]
    moved = [0.0, 0.0, 0.0]
    for block in blocks:
        for w in range(views):
            away = []
            for a in range(3):
                at = 3 * w + a
                offset = block[GEOMETRY * strips : GEOMETRY * strips + 1, at : at + 1]
                away.append(position[a] + jnp.broadcast_to(offset, (strips, 128)))
            inverse = lax.rsqrt(away[0] * away[0] + away[1] * away[1] + away[2] * away[2])
            direction = [part * inverse for part in away]
            basis, pull = jax.vjp(harmonic_basis, *direction)
            tint = [of(block, COLOUR_ROW + ch * views + w) for ch in range(3)]
            for ch in range(3):
                for b in range(16):
                    term = tint[ch] * basis[b]
                    levels[ch][b] = term if levels[ch][b] is None else levels[ch][b] + term
            given = [
                sum(tint[ch] * of(own_ref, GEOMETRY + 16 * ch + b) for ch in range(3)) for b in range(16)
            ]
            turned = pull(given)
            along = sum(turned[a] * direction[a] for a in range(3))
            for a in range(3):
                moved[a] = moved[a] + inverse * (turned[a] - direction[a] * along)
    for p in range(GEOMETRY):
        total = sum(of(block, p) for block in blocks)
        sum_ref[p * strips : (p + 1) * strips, :] = total + moved[p] if p < 3 else total
    for ch in range(3):
        for b in range(16):
            p = GEOMETRY + 16 * ch + b
            sum_ref[p * strips : (p + 1) * strips, :] = levels[ch][b]
    count = out_ref.shape[0]
    for strip in range(strips):
        out_ref[:, 128 * strip : 128 * strip + 128] = sum_ref[pl.ds(strip, count, stride=strips), :]


def swap(blocks, axis):
    n = len(blocks)
    return [blocks[0]] + [
        lax.ppermute(blocks[turn], axis, [(i, i ^ turn) for i in range(n)]) for turn in range(1, n)
    ]


def call(kernel, out_shape, scratch, in_smem, *args):
    specs = [
        pl.BlockSpec(memory_space=pltpu.SMEM) if i < in_smem else pl.BlockSpec(memory_space=pltpu.VMEM)
        for i in range(len(args))
    ]
    return pl.pallas_call(
        kernel,
        out_shape=out_shape,
        in_specs=specs,
        out_specs=[pl.BlockSpec(memory_space=pltpu.VMEM)] * len(out_shape),
        scratch_shapes=scratch,
        compiler_params=pltpu.CompilerParams(vmem_limit_bytes=48 * 1024 * 1024),
    )(*args)


def body(n_render, n_view, params, cameras, send_index, tile_id, tile_count, tile_slot, targets):
    index = send_index[0, 0]
    slot = tile_slot[0, 0]
    code = tile_id[0, 0]
    live = tile_count[0, 0]
    wanted = targets[0, 0]
    views = cameras.shape[0]
    gaussians = params.shape[1]
    cap = index.shape[1]
    tiles, length = slot.shape
    own = gaussians // n_view
    rows = -(-(COLOUR_ROW + 3 * views) // 8) * 8
    order = lax.axis_index("render") ^ jnp.arange(n_render, dtype=jnp.int32)
    index = sum(jnp.where((order == o)[:, None], index[o][None], 0) for o in range(n_render))
    where = jnp.stack([lax.axis_index("render"), lax.axis_index("view")]).astype(jnp.int32)

    table = camera_table(cameras)
    view = code // (CROP * CROP)
    cell = code % (CROP * CROP)
    tile_table = sum(
        jnp.where((view == w)[:, None], table[w : w + 1, :13], 0.0) for w in range(views)
    )
    extra = jnp.stack(
        [
            (8 * CROP - 8 - 16 * (cell % CROP)).astype(F32),
            (8 * CROP - 8 - 16 * (cell // CROP)).astype(F32),
            view.astype(F32),
            live.astype(F32),
        ],
        axis=1,
    )
    lane_table = jnp.concatenate([tile_table, extra, jnp.zeros((tiles, 7), F32)], axis=1).T
    lane_table = jnp.tile(lane_table, (1, 128 // tiles))
    slot_lanes = slot.T.reshape(-1, 128)
    origin = jnp.pad(table[:, 13:16].reshape(1, 3 * views), ((0, 0), (0, 128 - 3 * views)))
    mine = lax.dynamic_slice_in_dim(params, lax.axis_index("view") * own, own, 1).reshape(-1, 128)

    block = jax.ShapeDtypeStruct((rows, cap), F32)
    sent = call(
        partial(slab_kernel, n_render, views),
        [block] * n_render,
        [pltpu.VMEM((rows, gaussians), F32)],
        0,
        params,
        table,
        index,
    )
    arrived = swap(list(sent), "render")
    entries = tiles * length
    entry_rows = entries // 128
    spans = n_render * cap // SPAN
    image, *returned = call(
        partial(render_kernel, n_render, views),
        [jax.ShapeDtypeStruct(wanted.shape, F32)] + [block] * n_render,
        [
            pltpu.VMEM((2 * (GEOMETRY + 3), entry_rows, 128), F32),
            pltpu.VMEM((16 * entry_rows, 128), F32),
            pltpu.VMEM((128, entries), BF16),
            pltpu.VMEM((entries, 128), BF16),
            pltpu.VMEM((entries, PIXELS), F32),
            pltpu.VMEM((entries, PIXELS), F32),
            pltpu.VMEM((entries, PIXELS), BF16),
            pltpu.VMEM((entries, PIXELS), BF16),
            pltpu.VMEM((2 * rows * spans, 512), BF16),
            pltpu.VMEM((4 * rows * spans, 128), F32),
        ],
        1,
        where,
        *arrived,
        slot_lanes,
        lane_table,
        wanted,
    )
    homed = swap(list(returned), "render")
    slab_spans = gaussians // SPAN
    shares = call(
        partial(collect_kernel, n_render, n_view),
        [jax.ShapeDtypeStruct((rows * own // 128, 128), F32)] * n_view,
        [
            pltpu.VMEM((2 * rows * slab_spans, cap), BF16),
            pltpu.VMEM((4 * rows * slab_spans, 128), F32),
        ],
        1,
        where,
        *homed,
        index,
        origin,
    )
    owned = swap(list(shares), "view")
    (gradients,) = call(
        partial(owner_kernel, n_view, views),
        [jax.ShapeDtypeStruct((params.shape[0], own), F32)],
        [pltpu.VMEM((params.shape[0] * own // 128, 128), F32)],
        0,
        *owned,
        mine,
    )
    return (image[None, None], gradients)


def solution(mesh):
    in_specs = (
        P(None, ("groups", "render")),
        P(("groups", "view"), None),
        P(("groups", "render"), "view", None, None),
        P(("groups", "render"), "view", None),
        P(("groups", "render"), "view", None),
        P(("groups", "render"), "view", None, None),
        P(("groups", "render"), "view", None, None, None),
    )
    out_specs = (
        P(("groups", "render"), "view", None, None, None),
        P(None, ("groups", "render", "view")),
    )
    work = partial(body, mesh.shape["render"], mesh.shape["view"])
    return jax.shard_map(work, mesh=mesh, in_specs=in_specs, out_specs=out_specs, check_vma=False)
```

```python
from functools import partial

import jax
import jax.numpy as jnp
from jax import lax
from jax.experimental import pallas as pl
from jax.experimental.pallas import tpu as pltpu
from jax.sharding import PartitionSpec as P

CROP = 2
PIXELS = 256
GEOMETRY = 11
COLOUR_ROW = 12
SPAN = 256
CHUNK = 2048
LOG2_E = 1.4426950408889634
DEAD = -1e30

dilation = 0.3
backdrop = 1.0
band_zero = 0.28209479177387814
band_one = 0.4886025119029199
band_two = [
    1.0925484305920792,
    -1.0925484305920792,
    0.31539156525252005,
    -1.0925484305920792,
    0.5462742152960396,
]
band_three = [
    -0.5900435899266435,
    2.890611442640554,
    -0.4570457994644658,
    0.3731763325901154,
    -0.4570457994644658,
    1.445305721320277,
    -0.5900435899266435,
]

F32 = jnp.float32
BF16 = jnp.bfloat16


def harmonic_basis(along_x, along_y, along_z):
    square_x = along_x * along_x
    square_y = along_y * along_y
    square_z = along_z * along_z
    return [
        jnp.full_like(along_x, band_zero),
        -band_one * along_y,
        band_one * along_z,
        -band_one * along_x,
        band_two[0] * along_x * along_y,
        band_two[1] * along_y * along_z,
        band_two[2] * (2.0 * square_z - square_x - square_y),
        band_two[3] * along_x * along_z,
        band_two[4] * (square_x - square_y),
        band_three[0] * along_y * (3.0 * square_x - square_y),
        band_three[1] * along_x * along_y * along_z,
        band_three[2] * along_y * (4.0 * square_z - square_x - square_y),
        band_three[3] * along_z * (2.0 * square_z - 3.0 * square_x - 3.0 * square_y),
        band_three[4] * along_x * (4.0 * square_z - square_x - square_y),
        band_three[5] * along_z * (square_x - square_y),
        band_three[6] * along_x * (square_x - 3.0 * square_y),
    ]


def high_low(value):
    high = value.astype(BF16).astype(F32)
    return high, value - high


def dot_plain(left, right):
    return lax.dot_general(left, right, (((1,), (0,)), ((), ())), preferred_element_type=F32)


def dot_lanes(left, right):
    return lax.dot_general(left, right, (((1,), (1,)), ((), ())), preferred_element_type=F32)


def camera_table(cameras):
    cosine, sine = jnp.cos(cameras[:, :3]), jnp.sin(cameras[:, :3])
    c0, c1, c2 = cosine[:, 0], cosine[:, 1], cosine[:, 2]
    s0, s1, s2 = sine[:, 0], sine[:, 1], sine[:, 2]
    rotation = [
        [c1 * c2, s0 * s1 * c2 - c0 * s2, c0 * s1 * c2 + s0 * s2],
        [c1 * s2, s0 * s1 * s2 + c0 * c2, c0 * s1 * s2 - s0 * c2],
        [-s1, s0 * c1, c0 * c1],
    ]
    shift = [cameras[:, 3], cameras[:, 4], cameras[:, 5]]
    origin = [sum(rotation[m][a] * shift[m] for m in range(3)) for a in range(3)]
    return jnp.stack([e for row in rotation for e in row] + shift + [cameras[:, 6]] + origin, 1)


def lane_pick(source, lanes):
    return jnp.take_along_axis(source, lanes, axis=1, mode="promise_in_bounds")


def slab_kernel(n_render, views, params_ref, table_ref, index_ref, *rest):
    outs, dense_ref = rest[:n_render], rest[n_render]
    rows, gaussians = outs[0].shape[0], params_ref.shape[1]
    cap = index_ref.shape[1]
    width = 512
    picks = [(turn, step) for turn in range(n_render) for step in range(cap // 128)]
    shades = gaussians // width

    def shade(step):
        lanes = slice(step * width, step * width + width)
        dense_ref[0:8, lanes] = params_ref[8:16, lanes]
        away = [params_ref[a : a + 1, lanes] + table_ref[:, 13 + a : 14 + a] for a in range(3)]
        inverse = lax.rsqrt(away[0] * away[0] + away[1] * away[1] + away[2] * away[2])
        basis = harmonic_basis(*[part * inverse for part in away])
        for channel in range(3):
            base = GEOMETRY + 16 * channel
            colour = 0.5 + basis[0] * params_ref[base : base + 1, lanes]
            for level in range(1, 16):
                colour += basis[level] * params_ref[base + level : base + level + 1, lanes]
            first = COLOUR_ROW + channel * views - 8
            dense_ref[first : first + views, lanes] = colour

    def pick(source, groups, skip, turn, step):
        lanes = slice(128 * step, 128 * step + 128)
        index = jnp.broadcast_to(index_ref[turn : turn + 1, lanes], (8, 128))
        lane, block = index & 127, index >> 7
        found = [jnp.zeros((8, 128), F32) for _ in range(groups)]
        for b in range(gaussians // 128):
            here = block == b
            for s in range(groups):
                piece = source[8 * s : 8 * s + 8, 128 * b : 128 * b + 128]
                found[s] = jnp.where(here, lane_pick(piece, lane), found[s])
        for s in range(groups):
            outs[turn][8 * (s + skip) : 8 * (s + skip) + 8, lanes] = found[s]

    for step in range(shades):
        shade(step)
        for turn, at in picks[step * len(picks) // shades : (step + 1) * len(picks) // shades]:
            pick(params_ref, 1, 0, turn, at)
    for turn, at in picks:
        pick(dense_ref, rows // 8 - 1, 1, turn, at)


def entry_coefficients(raw, cam):
    px, py, pz = raw[0], raw[1], raw[2]
    extent = [jnp.exp(raw[3 + a]) for a in range(3)]
    norm = lax.rsqrt(raw[6] * raw[6] + raw[7] * raw[7] + raw[8] * raw[8] + raw[9] * raw[9])
    qw, qx, qy, qz = [raw[6 + a] * norm for a in range(4)]
    turn = [[cam[3 * a + b] for b in range(3)] for a in range(3)]
    x, y, z = [turn[a][0] * px + turn[a][1] * py + turn[a][2] * pz + cam[9 + a] for a in range(3)]
    scale = cam[12] / z
    slope_x, slope_y = x / z, y / z
    u = cam[12] * slope_x + cam[13]
    v = cam[12] * slope_y + cam[14]
    quat = [
        [1.0 - 2.0 * (qy * qy + qz * qz), 2.0 * (qx * qy - qw * qz), 2.0 * (qx * qz + qw * qy)],
        [2.0 * (qx * qy + qw * qz), 1.0 - 2.0 * (qx * qx + qz * qz), 2.0 * (qy * qz - qw * qx)],
        [2.0 * (qx * qz - qw * qy), 2.0 * (qy * qz + qw * qx), 1.0 - 2.0 * (qx * qx + qy * qy)],
    ]
    screen = [
        [scale * (turn[a][b] - slope * turn[2][b]) for b in range(3)]
        for a, slope in ((0, slope_x), (1, slope_y))
    ]
    foot = [
        [sum(screen[a][m] * quat[m][b] for m in range(3)) * extent[b] for b in range(3)]
        for a in range(2)
    ]
    cov_a = sum(foot[0][b] * foot[0][b] for b in range(3)) + dilation
    cov_b = sum(foot[0][b] * foot[1][b] for b in range(3))
    cov_c = sum(foot[1][b] * foot[1][b] for b in range(3)) + dilation
    inverse = 1.0 / (cov_a * cov_c - cov_b * cov_b)
    conic_a, conic_b, conic_c = cov_c * inverse, -cov_b * inverse, cov_a * inverse
    log_opacity = -jnp.log(1.0 + jnp.exp(-raw[10]))
    pull_x = conic_a * u + conic_b * v
    pull_y = conic_c * v + conic_b * u
    return [
        -0.5 * conic_a,
        -conic_b,
        -0.5 * conic_c,
        pull_x,
        pull_y,
        log_opacity - 0.5 * (pull_x * u + pull_y * v),
    ]


def monomials(shape, axis):
    number = lax.broadcasted_iota(jnp.int32, shape, axis)
    pixel = lax.broadcasted_iota(jnp.int32, shape, 1 - axis)
    x = (pixel & 15).astype(F32) - 7.5
    y = (pixel >> 4).astype(F32) - 7.5
    value = jnp.zeros(shape, F32)
    for at, term in enumerate((x * x, x * y, y * y, x, y, jnp.ones_like(x))):
        value = jnp.where((number & 7) == at, term, value)
    return value, number


def render_kernel(n_render, views, where_ref, *refs):
    blocks, refs = refs[:n_render], refs[n_render:]
    slot_ref, cam_ref, target_ref, refs = refs[0], refs[1], refs[2], refs[3:]
    image_ref, outs, refs = refs[0], refs[1 : 1 + n_render], refs[1 + n_render :]
    raw_ref, stack_ref, wide_ref, alpha_ref, weight_ref, shade_ref, high_ref, low_ref, pass_ref, enter_ref, behind_ref, lhs_ref, hot_ref, acc_ref = refs
    tiles = target_ref.shape[0]
    entry_rows = slot_ref.shape[0]
    entries = entry_rows * 128
    cap = blocks[0].shape[1]
    rows = blocks[0].shape[0]
    per_block = cap // 128
    me = where_ref[0]
    groups = entry_rows // 8

    def fetch(group, _):
        here = pl.ds(pl.multiple_of(group * 8, 8), 8)
        slot = slot_ref[here, :]
        lane, block = slot & 127, slot >> 7
        view = jnp.broadcast_to(cam_ref[15:16, :], (8, 128)).astype(jnp.int32)
        found = [jnp.zeros((8, 128), F32) for _ in range(GEOMETRY + 3)]
        for turn in range(n_render):
            first = (me ^ turn) * per_block
            for j in range(per_block):
                hit = block == first + j
                cut = slice(128 * j, 128 * j + 128)
                for p in range(GEOMETRY):
                    piece = jnp.broadcast_to(blocks[turn][p : p + 1, cut], (8, 128))
                    found[p] = jnp.where(hit, lane_pick(piece, lane), found[p])
                for w in range(views):
                    seen = hit & (view == w)
                    for channel in range(3):
                        p = COLOUR_ROW + channel * views + w
                        piece = jnp.broadcast_to(blocks[turn][p : p + 1, cut], (8, 128))
                        at = GEOMETRY + channel
                        found[at] = jnp.where(seen, lane_pick(piece, lane), found[at])
        for p in range(GEOMETRY + 3):
            raw_ref[p, here, :] = found[p]
        return 0

    lax.fori_loop(0, groups, fetch, 0)

    def cam_rows():
        return [jnp.broadcast_to(cam_ref[i : i + 1, :], (8, 128)) for i in range(15)]

    stack_ref[...] = jnp.zeros_like(stack_ref)

    def forward_entries(group, _):
        here = pl.ds(pl.multiple_of(group * 8, 8), 8)
        coefficient = entry_coefficients([raw_ref[p, here, :] for p in range(GEOMETRY)], cam_rows())
        row = lax.broadcasted_iota(jnp.int32, (8, 128), 0) + group * 8
        lane = lax.broadcasted_iota(jnp.int32, (8, 128), 1)
        order = (lane // tiles) * entry_rows + row
        live = order < jnp.broadcast_to(cam_ref[16:17, :], (8, 128)).astype(jnp.int32)
        for c in range(6):
            value = coefficient[c] * LOG2_E
            if c == 5:
                value = jnp.where(live, value, DEAD)
            at = pl.ds(pl.multiple_of(c * entry_rows + group * 8, 8), 8)
            stack_ref[at, :] = value
        for channel in range(3):
            at = pl.ds(pl.multiple_of((8 + channel) * entry_rows + group * 8, 8), 8)
            stack_ref[at, :] = raw_ref[GEOMETRY + channel, here, :]
        return 0

    lax.fori_loop(0, groups, forward_entries, 0)

    wide_ref[...] = jnp.zeros_like(wide_ref)
    lane = lax.broadcasted_iota(jnp.int32, (8, 128), 1)
    own_tile = (lane & (tiles - 1)) == lax.broadcasted_iota(jnp.int32, (8, 128), 0)
    chunks = entries // CHUNK

    def chunk_of(chunk):
        return pl.ds(pl.multiple_of(chunk * CHUNK, CHUNK), CHUNK)

    def widen(row, _):
        value = stack_ref[pl.ds(row, 16, stride=entry_rows), :]
        high, rest = high_low(value)
        middle, low = high_low(rest)

        def spread(part):
            return [
                jnp.where(own_tile, jnp.broadcast_to(part[8 + ch : 9 + ch, :], (8, 128)), 0.0)
                for ch in range(3)
            ]

        zero = jnp.zeros((8, 128), F32)
        bright = spread(high)
        pieces = [high[0:8], middle[0:8], low[0:8], zero] + bright + spread(middle) + bright + [zero]
        lanes = pl.ds(pl.multiple_of(row * 128, 128), 128)
        wide_ref[:, lanes] = jnp.concatenate(pieces, axis=0).astype(BF16)
        return 0

    lax.fori_loop(0, entry_rows, widen, 0)

    value, number = monomials((PIXELS, 32), 1)
    left = jnp.where(number < 24, value, 0.0).astype(BF16)
    value, number = monomials((16, PIXELS), 0)
    moment_rows = jnp.where(number < 8, value, 0.0).astype(BF16)
    segment = lax.broadcasted_iota(jnp.int32, (PIXELS, 128), 1) // tiles
    last = 128 // tiles - 1

    def attenuate(chunk, _):
        alpha = jnp.exp2(dot_plain(left, wide_ref[0:32, chunk_of(chunk)]))
        alpha_ref[:, chunk_of(chunk)] = alpha
        passing = pass_ref[...]
        weights = []
        for k in range(CHUNK // 128):
            weight = passing * alpha[:, 128 * k : 128 * k + 128]
            passing = passing - weight
            weights.append(weight)
        weight_ref[:, chunk_of(chunk)] = jnp.concatenate(weights, axis=1)
        pass_ref[...] = passing
        return 0

    pass_ref[...] = jnp.ones_like(pass_ref)
    lax.fori_loop(0, chunks, attenuate, 0)

    through = pass_ref[...]
    hop = 1
    while hop <= last:
        through = through * jnp.where(segment >= hop, pltpu.roll(through, tiles * hop, 1), 1.0)
        hop *= 2
    enter_ref[...] = jnp.where(segment >= 1, pltpu.roll(through, tiles, 1), 1.0)
    remain = through.T[tiles * last : tiles * last + tiles, :]

    def paint(chunk, image):
        weight = weight_ref[:, chunk_of(chunk)] * jnp.concatenate([enter_ref[...]] * (CHUNK // 128), axis=1)
        weight_ref[:, chunk_of(chunk)] = weight
        high = weight.astype(BF16)
        low = (weight - high.astype(F32)).astype(BF16)
        high_ref[:, chunk_of(chunk)] = high
        low_ref[:, chunk_of(chunk)] = low
        colours = wide_ref[32:80, chunk_of(chunk)]
        return image + (dot_lanes(colours, high) + dot_lanes(colours, low))

    image = lax.fori_loop(0, chunks, paint, jnp.zeros((48, PIXELS), F32))
    image = image[0:24] + image[24:48]
    residual = []
    for channel in range(3):
        shown = image[8 * channel : 8 * channel + 8] + backdrop * remain
        image_ref[:, channel, :] = shown
        residual.append(shown - target_ref[:, channel, :])
    high, low = high_low(jnp.concatenate(residual, axis=0))
    both = jnp.concatenate([high, low], axis=0).astype(BF16)
    right = jnp.concatenate([high, high, low, jnp.zeros((56, PIXELS), F32)], axis=0).T.astype(BF16)
    right = right[:, 0:80]
    number = lax.broadcasted_iota(jnp.int32, (80, 128), 0)
    unit = (number & (tiles - 1)) == (lax.broadcasted_iota(jnp.int32, (80, 128), 1) & (tiles - 1))
    unit = jnp.where(unit & ((number < 24) | ((number >= 48) & (number < 72))), backdrop, 0.0)
    open_end = dot_plain(right, unit.astype(BF16))

    def shade(step, _):
        chunk = chunks - 1 - step
        colour = dot_plain(right, wide_ref[32:112, chunk_of(chunk)])
        shade_ref[:, chunk_of(chunk)] = colour
        alpha = alpha_ref[:, chunk_of(chunk)]
        behind = behind_ref[...]
        for k in reversed(range(CHUNK // 128)):
            cut = slice(128 * k, 128 * k + 128)
            behind = behind + alpha[:, cut] * (colour[:, cut] - behind)
        behind_ref[...] = behind
        return 0

    behind_ref[...] = jnp.zeros_like(behind_ref)
    lax.fori_loop(0, chunks, shade, 0)

    keep, add = pass_ref[...], behind_ref[...]
    hop = 1
    while hop <= last:
        inside = segment + hop <= last
        add = add + keep * jnp.where(inside, pltpu.roll(add, 128 - tiles * hop, 1), 0.0)
        keep = keep * jnp.where(inside, pltpu.roll(keep, 128 - tiles * hop, 1), 1.0)
        hop *= 2
    behind_ref[...] = jnp.where(
        segment < last, pltpu.roll(add + keep * open_end, 128 - tiles, 1), open_end
    )

    def descend(step, _):
        chunk = chunks - 1 - step
        behind = behind_ref[...]
        slopes = [None] * (CHUNK // 128)
        for k in reversed(range(CHUNK // 128)):
            cut = pl.ds(pl.multiple_of(chunk * CHUNK + 128 * k, 128), 128)
            gap = shade_ref[:, cut] - behind
            behind = behind + alpha_ref[:, cut] * gap
            slopes[k] = weight_ref[:, cut] * gap
        behind_ref[...] = behind
        slope = jnp.concatenate(slopes, axis=1)
        high = slope.astype(BF16)
        low = (slope - high.astype(F32)).astype(BF16)
        moments = dot_plain(moment_rows, high) + dot_plain(moment_rows, low)
        tint = dot_plain(both, high_ref[:, chunk_of(chunk)]) + dot_plain(both, low_ref[:, chunk_of(chunk)])
        tint = tint[0:24] + tint[24:48]
        for k in range(CHUNK // 128):
            row = chunk * (CHUNK // 128) + k
            cut = slice(128 * k, 128 * k + 128)
            stack_ref[pl.ds(row, 8, stride=entry_rows), :] = moments[0:8, cut]
            for channel in range(3):
                part = jnp.where(own_tile, tint[8 * channel : 8 * channel + 8, cut], 0.0)
                stack_ref[pl.ds((8 + channel) * entry_rows + row, 1), :] = jnp.sum(
                    part, axis=0, keepdims=True
                )
        return 0

    lax.fori_loop(0, chunks, descend, 0)

    def backward_entries(group, _):
        here = pl.ds(pl.multiple_of(group * 8, 8), 8)
        cam = cam_rows()
        given = [
            stack_ref[pl.ds(pl.multiple_of(c * entry_rows + group * 8, 8), 8), :] for c in range(6)
        ]
        _, pull = jax.vjp(
            lambda raw: entry_coefficients(raw, cam), [raw_ref[p, here, :] for p in range(GEOMETRY)]
        )
        (grads,) = pull(given)
        for channel in range(3):
            at = pl.ds(pl.multiple_of((8 + channel) * entry_rows + group * 8, 8), 8)
            grads.append(stack_ref[at, :])
        for p in range(GEOMETRY + 3):
            high, low = high_low(grads[p])
            raw_ref[p, here, :] = high
            raw_ref[GEOMETRY + 3 + p, here, :] = low
        return 0

    lax.fori_loop(0, groups, backward_entries, 0)

    spans = n_render * cap // SPAN
    half_rows = rows * spans
    view = cam_ref[15:16, :].astype(jnp.int32)

    def spread_out(row, _):
        at_lanes = pl.ds(pl.multiple_of(row * 128, 128), 128)
        slot = slot_ref[pl.ds(row, 1), :]
        span, lane = slot // SPAN, slot & (SPAN - 1)
        lanes_of = lax.broadcasted_iota(jnp.int32, (SPAN, 128), 0) == jnp.broadcast_to(lane, (SPAN, 128))
        hot_ref[:, at_lanes] = jnp.where(lanes_of, 1.0, 0.0).astype(BF16)
        in_span = lax.broadcasted_iota(jnp.int32, (spans, 128), 0) == jnp.broadcast_to(span, (spans, 128))
        key = view * spans + span
        in_view = lax.broadcasted_iota(jnp.int32, (views * spans, 128), 0) == jnp.broadcast_to(
            key, (views * spans, 128)
        )
        for part in range(2):
            base = part * half_rows
            pieces = []
            for p in range(COLOUR_ROW):
                if p < GEOMETRY:
                    value = raw_ref[part * (GEOMETRY + 3) + p, pl.ds(row, 1), :]
                    pieces.append(jnp.where(in_span, jnp.broadcast_to(value, (spans, 128)), 0.0))
                else:
                    pieces.append(jnp.zeros((spans, 128), F32))
                if len(pieces) == 2:
                    at = base + (p - 1) * spans
                    lhs_ref[at : at + 2 * spans, at_lanes] = jnp.concatenate(pieces, axis=0).astype(BF16)
                    pieces = []
            for channel in range(3):
                value = raw_ref[part * (GEOMETRY + 3) + GEOMETRY + channel, pl.ds(row, 1), :]
                value = jnp.where(in_view, jnp.broadcast_to(value, (views * spans, 128)), 0.0)
                at = base + (COLOUR_ROW + channel * views) * spans
                lhs_ref[at : at + views * spans, at_lanes] = value.astype(BF16)

    def spread_rows(step, _):
        for i in range(4):
            spread_out(step * 4 + i, 0)
        return 0

    lax.fori_loop(0, entry_rows // 4, spread_rows, 0)
    product = dot_lanes(lhs_ref[...], hot_ref[...])
    for half in range(SPAN // 128):
        at = slice(half * 2 * half_rows, (half + 1) * 2 * half_rows)
        acc_ref[at, :] = product[:, 128 * half : 128 * half + 128]
    for turn in range(n_render):
        for part in range(cap // SPAN):
            span = (me ^ turn) * (cap // SPAN) + part
            for half in range(SPAN // 128):
                cut = slice(128 * half, 128 * half + 128)
                total = (
                    acc_ref[pl.ds(half * 2 * rows * spans + span, rows, stride=spans), :]
                    + acc_ref[pl.ds(half * 2 * rows * spans + rows * spans + span, rows, stride=spans), :]
                )
                first = part * SPAN + 128 * half
                outs[turn][:, first : first + 128] = total


def collect_kernel(n_render, n_view, where_ref, *refs):
    blocks, refs = refs[:n_render], refs[n_render:]
    index_ref, origin_ref, refs = refs[0], refs[1], refs[2:]
    outs, (lhs_ref, hot_ref, acc_ref) = refs[:n_view], refs[n_view:]
    rows, cap = blocks[0].shape
    own = outs[0].shape[0] // rows * 128
    gaussians = own * n_view
    spans = gaussians // SPAN
    column = where_ref[1]
    for turn in range(n_render):
        lanes = slice(turn * cap, (turn + 1) * cap)
        index = index_ref[turn : turn + 1, :]
        span, lane = index // SPAN, index & (SPAN - 1)
        hot = lax.broadcasted_iota(jnp.int32, (SPAN, cap), 0) == jnp.broadcast_to(lane, (SPAN, cap))
        hot_ref[:, lanes] = jnp.where(hot, 1.0, 0.0).astype(BF16)
        in_span = lax.broadcasted_iota(jnp.int32, (spans, cap), 0) == jnp.broadcast_to(span, (spans, cap))
        high, low = high_low(blocks[turn][...])
        for part, value in ((0, high), (1, low)):
            for p in range(rows):
                at = (part * rows + p) * spans
                piece = jnp.broadcast_to(value[p : p + 1, :], (spans, cap))
                lhs_ref[at : at + spans, lanes] = jnp.where(in_span, piece, 0.0).astype(BF16)
    product = dot_lanes(lhs_ref[...], hot_ref[...])
    for half in range(2):
        at = slice(half * 2 * rows * spans, (half + 1) * 2 * rows * spans)
        acc_ref[at, :] = product[:, 128 * half : 128 * half + 128]
    strips = own // 128
    for turn in range(n_view):
        for strip in range(strips):
            span = (column ^ turn) * (own // SPAN) + strip // 2
            first = (strip % 2) * 2 * rows * spans
            total = (
                acc_ref[pl.ds(first + span, rows, stride=spans), :]
                + acc_ref[pl.ds(first + rows * spans + span, rows, stride=spans), :]
            )
            outs[turn][pl.ds(strip, rows, stride=strips), :] = total
        outs[turn][GEOMETRY * strips : GEOMETRY * strips + 1, :] = origin_ref[...]


def owner_kernel(n_view, views, *refs):
    blocks, (own_ref, out_ref, sum_ref) = refs[:n_view], refs[n_view:]
    strips = out_ref.shape[1] // 128

    def of(ref, p):
        return ref[p * strips : (p + 1) * strips, :]

    position = [of(own_ref, a) for a in range(3)]
    levels = [[None] * 16 for _ in range(3)]
    moved = [0.0, 0.0, 0.0]
    for block in blocks:
        for w in range(views):
            away = []
            for a in range(3):
                at = 3 * w + a
                offset = block[GEOMETRY * strips : GEOMETRY * strips + 1, at : at + 1]
                away.append(position[a] + jnp.broadcast_to(offset, (strips, 128)))
            inverse = lax.rsqrt(away[0] * away[0] + away[1] * away[1] + away[2] * away[2])
            direction = [part * inverse for part in away]
            basis, pull = jax.vjp(harmonic_basis, *direction)
            tint = [of(block, COLOUR_ROW + ch * views + w) for ch in range(3)]
            for ch in range(3):
                for b in range(16):
                    term = tint[ch] * basis[b]
                    levels[ch][b] = term if levels[ch][b] is None else levels[ch][b] + term
            given = [
                sum(tint[ch] * of(own_ref, GEOMETRY + 16 * ch + b) for ch in range(3)) for b in range(16)
            ]
            turned = pull(given)
            along = sum(turned[a] * direction[a] for a in range(3))
            for a in range(3):
                moved[a] = moved[a] + inverse * (turned[a] - direction[a] * along)
    for p in range(GEOMETRY):
        total = sum(of(block, p) for block in blocks)
        sum_ref[p * strips : (p + 1) * strips, :] = total + moved[p] if p < 3 else total
    for ch in range(3):
        for b in range(16):
            p = GEOMETRY + 16 * ch + b
            sum_ref[p * strips : (p + 1) * strips, :] = levels[ch][b]
    count = out_ref.shape[0]
    for strip in range(strips):
        out_ref[:, 128 * strip : 128 * strip + 128] = sum_ref[pl.ds(strip, count, stride=strips), :]


def swap(blocks, axis):
    n = len(blocks)
    return [blocks[0]] + [
        lax.ppermute(blocks[turn], axis, [(i, i ^ turn) for i in range(n)]) for turn in range(1, n)
    ]


def call(kernel, out_shape, scratch, in_smem, *args):
    specs = [
        pl.BlockSpec(memory_space=pltpu.SMEM) if i < in_smem else pl.BlockSpec(memory_space=pltpu.VMEM)
        for i in range(len(args))
    ]
    return pl.pallas_call(
        kernel,
        out_shape=out_shape,
        in_specs=specs,
        out_specs=[pl.BlockSpec(memory_space=pltpu.VMEM)] * len(out_shape),
        scratch_shapes=scratch,
        compiler_params=pltpu.CompilerParams(vmem_limit_bytes=48 * 1024 * 1024),
    )(*args)


def render(n_render, views, where, arrived, table, code, live, slot, wanted):
    tiles, length = slot.shape
    rows, cap = arrived[0].shape
    view = code // (CROP * CROP)
    cell = code % (CROP * CROP)
    tile_table = sum(
        jnp.where((view == w)[:, None], table[w : w + 1, :13], 0.0) for w in range(views)
    )
    extra = jnp.stack(
        [
            (8 * CROP - 8 - 16 * (cell % CROP)).astype(F32),
            (8 * CROP - 8 - 16 * (cell // CROP)).astype(F32),
            view.astype(F32),
            live.astype(F32),
        ],
        axis=1,
    )
    lane_table = jnp.concatenate([tile_table, extra, jnp.zeros((tiles, 7), F32)], axis=1).T
    lane_table = jnp.tile(lane_table, (1, 128 // tiles))
    slot_lanes = slot.reshape(tiles, 128 // tiles, -1).transpose(2, 1, 0).reshape(-1, 128)
    entries = tiles * length
    entry_rows = entries // 128
    spans = n_render * cap // SPAN
    return call(
        partial(render_kernel, n_render, views),
        [jax.ShapeDtypeStruct(wanted.shape, F32)]
        + [jax.ShapeDtypeStruct((rows, cap), F32)] * n_render,
        [
            pltpu.VMEM((2 * (GEOMETRY + 3), entry_rows, 128), F32),
            pltpu.VMEM((16 * entry_rows, 128), F32),
            pltpu.VMEM((112, entries), BF16),
            pltpu.VMEM((PIXELS, entries), F32),
            pltpu.VMEM((PIXELS, entries), F32),
            pltpu.VMEM((PIXELS, entries), F32),
            pltpu.VMEM((PIXELS, entries), BF16),
            pltpu.VMEM((PIXELS, entries), BF16),
            pltpu.VMEM((PIXELS, 128), F32),
            pltpu.VMEM((PIXELS, 128), F32),
            pltpu.VMEM((PIXELS, 128), F32),
            pltpu.VMEM((2 * rows * spans, entries), BF16),
            pltpu.VMEM((SPAN, entries), BF16),
            pltpu.VMEM((4 * rows * spans, 128), F32),
        ],
        1,
        where,
        *arrived,
        slot_lanes,
        lane_table,
        wanted,
    )


def slab(n_render, views, params, table, index):
    rows = -(-(COLOUR_ROW + 3 * views) // 8) * 8
    return call(
        partial(slab_kernel, n_render, views),
        [jax.ShapeDtypeStruct((rows, index.shape[1]), F32)] * n_render,
        [pltpu.VMEM((rows - 8, params.shape[1]), F32)],
        0,
        params,
        table,
        index,
    )


def collect(n_render, n_view, where, homed, index, origin, own):
    rows, cap = homed[0].shape
    spans = n_view * own // SPAN
    return call(
        partial(collect_kernel, n_render, n_view),
        [jax.ShapeDtypeStruct((rows * own // 128, 128), F32)] * n_view,
        [
            pltpu.VMEM((2 * rows * spans, n_render * cap), BF16),
            pltpu.VMEM((SPAN, n_render * cap), BF16),
            pltpu.VMEM((4 * rows * spans, 128), F32),
        ],
        1,
        where,
        *homed,
        index,
        origin,
    )


def body(n_render, n_view, params, cameras, send_index, tile_id, tile_count, tile_slot, targets):
    index = send_index[0, 0]
    views = cameras.shape[0]
    own = params.shape[1] // n_view
    order = lax.axis_index("render") ^ jnp.arange(n_render, dtype=jnp.int32)
    index = sum(jnp.where((order == o)[:, None], index[o][None], 0) for o in range(n_render))
    where = jnp.stack([lax.axis_index("render"), lax.axis_index("view")]).astype(jnp.int32)
    table = camera_table(cameras)
    origin = jnp.pad(table[:, 13:16].reshape(1, 3 * views), ((0, 0), (0, 128 - 3 * views)))
    mine = lax.dynamic_slice_in_dim(params, lax.axis_index("view") * own, own, 1).reshape(-1, 128)

    arrived = swap(list(slab(n_render, views, params, table, index)), "render")
    image, *returned = render(
        n_render,
        views,
        where,
        arrived,
        table,
        tile_id[0, 0],
        tile_count[0, 0],
        tile_slot[0, 0],
        targets[0, 0],
    )
    homed = swap(returned, "render")
    owned = swap(list(collect(n_render, n_view, where, homed, index, origin, own)), "view")
    (gradients,) = call(
        partial(owner_kernel, n_view, views),
        [jax.ShapeDtypeStruct((params.shape[0], own), F32)],
        [pltpu.VMEM((params.shape[0] * own // 128, 128), F32)],
        0,
        *owned,
        mine,
    )
    return (image[None, None], gradients)


def solution(mesh):
    in_specs = (
        P(None, ("groups", "render")),
        P(("groups", "view"), None),
        P(("groups", "render"), "view", None, None),
        P(("groups", "render"), "view", None),
        P(("groups", "render"), "view", None),
        P(("groups", "render"), "view", None, None),
        P(("groups", "render"), "view", None, None, None),
    )
    out_specs = (
        P(("groups", "render"), "view", None, None, None),
        P(None, ("groups", "render", "view")),
    )
    work = partial(body, mesh.shape["render"], mesh.shape["view"])
    return jax.shard_map(work, mesh=mesh, in_specs=in_specs, out_specs=out_specs, check_vma=False)
```

```python
from functools import partial

import jax
import jax.numpy as jnp
from jax import lax
from jax.experimental import pallas as pl
from jax.experimental.pallas import tpu as pltpu
from jax.sharding import PartitionSpec as P

CROP = 2
PIXELS = 256
GEOMETRY = 11
COLOUR_ROW = 12
SPAN = 256
CHUNK = 2048
STRIP = 128
LOG2_E = 1.4426950408889634
DEAD = -1e30

dilation = 0.3
backdrop = 1.0
band_zero = 0.28209479177387814
band_one = 0.4886025119029199
band_two = [
    1.0925484305920792,
    -1.0925484305920792,
    0.31539156525252005,
    -1.0925484305920792,
    0.5462742152960396,
]
band_three = [
    -0.5900435899266435,
    2.890611442640554,
    -0.4570457994644658,
    0.3731763325901154,
    -0.4570457994644658,
    1.445305721320277,
    -0.5900435899266435,
]

F32 = jnp.float32
BF16 = jnp.bfloat16


def harmonic_basis(along_x, along_y, along_z):
    square_x = along_x * along_x
    square_y = along_y * along_y
    square_z = along_z * along_z
    return [
        jnp.full_like(along_x, band_zero),
        -band_one * along_y,
        band_one * along_z,
        -band_one * along_x,
        band_two[0] * along_x * along_y,
        band_two[1] * along_y * along_z,
        band_two[2] * (2.0 * square_z - square_x - square_y),
        band_two[3] * along_x * along_z,
        band_two[4] * (square_x - square_y),
        band_three[0] * along_y * (3.0 * square_x - square_y),
        band_three[1] * along_x * along_y * along_z,
        band_three[2] * along_y * (4.0 * square_z - square_x - square_y),
        band_three[3] * along_z * (2.0 * square_z - 3.0 * square_x - 3.0 * square_y),
        band_three[4] * along_x * (4.0 * square_z - square_x - square_y),
        band_three[5] * along_z * (square_x - square_y),
        band_three[6] * along_x * (square_x - 3.0 * square_y),
    ]


def high_low(value):
    high = value.astype(BF16).astype(F32)
    return high, value - high


def dot_plain(left, right):
    return lax.dot_general(left, right, (((1,), (0,)), ((), ())), preferred_element_type=F32)


def dot_lanes(left, right):
    return lax.dot_general(left, right, (((1,), (1,)), ((), ())), preferred_element_type=F32)


def camera_columns(cameras):
    cosine, sine = jnp.cos(cameras), jnp.sin(cameras)
    c0, c1, c2 = [cosine[:, a : a + 1] for a in range(3)]
    s0, s1, s2 = [sine[:, a : a + 1] for a in range(3)]
    rotation = [
        [c1 * c2, s0 * s1 * c2 - c0 * s2, c0 * s1 * c2 + s0 * s2],
        [c1 * s2, s0 * s1 * s2 + c0 * c2, c0 * s1 * s2 - s0 * c2],
        [-s1, s0 * c1, c0 * c1],
    ]
    shift = [cameras[:, a : a + 1] for a in (3, 4, 5)]
    origin = [sum(rotation[m][a] * shift[m] for m in range(3)) for a in range(3)]
    return [e for row in rotation for e in row] + shift + [cameras[:, 6:7]] + origin


def camera_table(cameras):
    return jnp.concatenate(camera_columns(cameras), axis=1)


def lane_pick(source, lanes):
    return jnp.take_along_axis(source, lanes, axis=1, mode="promise_in_bounds")


def partner_rows(index_ref, n_render):
    me = lax.axis_index("render")
    rows = [index_ref[o : o + 1, :] for o in range(n_render)]
    return [
        sum(jnp.where((me ^ turn) == o, rows[o], 0) for o in range(n_render)) for turn in range(n_render)
    ]


def slab_kernel(n_render, views, params_hbm, cameras_hbm, index_hbm, *rest):
    outs, refs = rest[:n_render], rest[n_render:]
    params_ref, cameras_ref, index_ref, order_ref, dense_ref, arrival = refs
    rows, gaussians = outs[0].shape[0], params_ref.shape[1]
    cap = index_ref.shape[1]
    width = 512
    shades = gaussians // width
    count = params_ref.shape[0]
    copies = [
        pltpu.make_async_copy(cameras_hbm, cameras_ref, arrival.at[0]),
        pltpu.make_async_copy(index_hbm, index_ref, arrival.at[1]),
        pltpu.make_async_copy(params_hbm.at[0:8, :], params_ref.at[0:8, :], arrival.at[2]),
    ]
    for step in range(shades):
        lanes = pl.ds(step * width, width)
        copies.append(
            pltpu.make_async_copy(
                params_hbm.at[8:count, lanes], params_ref.at[8:count, lanes], arrival.at[3 + step]
            )
        )
    for copy in copies:
        copy.start()
    copies[0].wait()
    origin = camera_columns(cameras_ref[...])[13:16]
    copies[1].wait()
    for turn, row in enumerate(partner_rows(index_ref, n_render)):
        order_ref[turn : turn + 1, :] = row
    copies[2].wait()

    picks = [(turn, step) for turn in range(n_render) for step in range(cap // 128)]

    def shade(step):
        lanes = slice(step * width, step * width + width)
        copies[3 + step].wait()
        dense_ref[0:8, lanes] = params_ref[8:16, lanes]
        away = [params_ref[a : a + 1, lanes] + origin[a] for a in range(3)]
        inverse = lax.rsqrt(away[0] * away[0] + away[1] * away[1] + away[2] * away[2])
        basis = harmonic_basis(*[part * inverse for part in away])
        for channel in range(3):
            base = GEOMETRY + 16 * channel
            colour = 0.5 + basis[0] * params_ref[base : base + 1, lanes]
            for level in range(1, 16):
                colour += basis[level] * params_ref[base + level : base + level + 1, lanes]
            first = COLOUR_ROW + channel * views - 8
            dense_ref[first : first + views, lanes] = colour

    def pick(source, groups, skip, turn, step):
        lanes = slice(128 * step, 128 * step + 128)
        index = jnp.broadcast_to(order_ref[turn : turn + 1, lanes], (8, 128))
        lane, block = index & 127, index >> 7
        found = [jnp.zeros((8, 128), F32) for _ in range(groups)]
        for b in range(gaussians // 128):
            here = block == b
            for s in range(groups):
                piece = source[8 * s : 8 * s + 8, 128 * b : 128 * b + 128]
                found[s] = jnp.where(here, lane_pick(piece, lane), found[s])
        for s in range(groups):
            outs[turn][8 * (s + skip) : 8 * (s + skip) + 8, lanes] = found[s]

    for step in range(shades):
        shade(step)
        for turn, at in picks[step * len(picks) // shades : (step + 1) * len(picks) // shades]:
            pick(params_ref, 1, 0, turn, at)
    for turn, at in picks:
        pick(dense_ref, rows // 8 - 1, 1, turn, at)


def entry_coefficients(raw, cam):
    px, py, pz = raw[0], raw[1], raw[2]
    extent = [jnp.exp(raw[3 + a]) for a in range(3)]
    norm = lax.rsqrt(raw[6] * raw[6] + raw[7] * raw[7] + raw[8] * raw[8] + raw[9] * raw[9])
    qw, qx, qy, qz = [raw[6 + a] * norm for a in range(4)]
    turn = [[cam[3 * a + b] for b in range(3)] for a in range(3)]
    x, y, z = [turn[a][0] * px + turn[a][1] * py + turn[a][2] * pz + cam[9 + a] for a in range(3)]
    scale = cam[12] / z
    slope_x, slope_y = x / z, y / z
    u = cam[12] * slope_x + cam[13]
    v = cam[12] * slope_y + cam[14]
    quat = [
        [1.0 - 2.0 * (qy * qy + qz * qz), 2.0 * (qx * qy - qw * qz), 2.0 * (qx * qz + qw * qy)],
        [2.0 * (qx * qy + qw * qz), 1.0 - 2.0 * (qx * qx + qz * qz), 2.0 * (qy * qz - qw * qx)],
        [2.0 * (qx * qz - qw * qy), 2.0 * (qy * qz + qw * qx), 1.0 - 2.0 * (qx * qx + qy * qy)],
    ]
    screen = [
        [scale * (turn[a][b] - slope * turn[2][b]) for b in range(3)]
        for a, slope in ((0, slope_x), (1, slope_y))
    ]
    foot = [
        [sum(screen[a][m] * quat[m][b] for m in range(3)) * extent[b] for b in range(3)]
        for a in range(2)
    ]
    cov_a = sum(foot[0][b] * foot[0][b] for b in range(3)) + dilation
    cov_b = sum(foot[0][b] * foot[1][b] for b in range(3))
    cov_c = sum(foot[1][b] * foot[1][b] for b in range(3)) + dilation
    inverse = 1.0 / (cov_a * cov_c - cov_b * cov_b)
    conic_a, conic_b, conic_c = cov_c * inverse, -cov_b * inverse, cov_a * inverse
    log_opacity = -jnp.log(1.0 + jnp.exp(-raw[10]))
    pull_x = conic_a * u + conic_b * v
    pull_y = conic_c * v + conic_b * u
    return [
        -0.5 * conic_a,
        -conic_b,
        -0.5 * conic_c,
        pull_x,
        pull_y,
        log_opacity - 0.5 * (pull_x * u + pull_y * v),
    ]


def monomials(shape, axis):
    number = lax.broadcasted_iota(jnp.int32, shape, axis)
    pixel = lax.broadcasted_iota(jnp.int32, shape, 1 - axis)
    x = (pixel & 15).astype(F32) - 7.5
    y = (pixel >> 4).astype(F32) - 7.5
    value = jnp.zeros(shape, F32)
    for at, term in enumerate((x * x, x * y, y * y, x, y, jnp.ones_like(x))):
        value = jnp.where((number & 7) == at, term, value)
    return value, number


def render_kernel(n_render, views, *refs):
    blocks, refs = refs[:n_render], refs[n_render:]
    slot_ref, cam_ref, target_ref, refs = refs[0], refs[1], refs[2], refs[3:]
    image_ref, outs, refs = refs[0], refs[1 : 1 + n_render], refs[1 + n_render :]
    raw_ref, stack_ref, wide_ref, alpha_ref, weight_ref, shown_ref, pass_ref, enter_ref, behind_ref, right_ref, sums_ref, lhs_ref, hot_ref, acc_ref = refs
    tiles = target_ref.shape[0]
    entry_rows = slot_ref.shape[0]
    entries = entry_rows * 128
    cap = blocks[0].shape[1]
    rows = blocks[0].shape[0]
    per_block = cap // 128
    me = lax.axis_index("render")
    groups = entry_rows // 8

    def fetch(group, _):
        here = pl.ds(pl.multiple_of(group * 8, 8), 8)
        slot = slot_ref[here, :]
        lane, block = slot & 127, slot >> 7
        view = jnp.broadcast_to(cam_ref[15:16, :], (8, 128)).astype(jnp.int32)
        found = [jnp.zeros((8, 128), F32) for _ in range(GEOMETRY + 3)]
        for turn in range(n_render):
            first = (me ^ turn) * per_block
            for j in range(per_block):
                hit = block == first + j
                cut = slice(128 * j, 128 * j + 128)
                for p in range(GEOMETRY):
                    piece = jnp.broadcast_to(blocks[turn][p : p + 1, cut], (8, 128))
                    found[p] = jnp.where(hit, lane_pick(piece, lane), found[p])
                for w in range(views):
                    seen = hit & (view == w)
                    for channel in range(3):
                        p = COLOUR_ROW + channel * views + w
                        piece = jnp.broadcast_to(blocks[turn][p : p + 1, cut], (8, 128))
                        at = GEOMETRY + channel
                        found[at] = jnp.where(seen, lane_pick(piece, lane), found[at])
        for p in range(GEOMETRY + 3):
            raw_ref[p, here, :] = found[p]
        return 0

    lax.fori_loop(0, groups, fetch, 0)

    def cam_rows():
        return [jnp.broadcast_to(cam_ref[i : i + 1, :], (8, 128)) for i in range(15)]

    stack_ref[...] = jnp.zeros_like(stack_ref)

    def forward_entries(group, _):
        here = pl.ds(pl.multiple_of(group * 8, 8), 8)
        coefficient = entry_coefficients([raw_ref[p, here, :] for p in range(GEOMETRY)], cam_rows())
        row = lax.broadcasted_iota(jnp.int32, (8, 128), 0) + group * 8
        lane = lax.broadcasted_iota(jnp.int32, (8, 128), 1)
        order = (lane // tiles) * entry_rows + row
        live = order < jnp.broadcast_to(cam_ref[16:17, :], (8, 128)).astype(jnp.int32)
        for c in range(6):
            value = coefficient[c] * LOG2_E
            if c == 5:
                value = jnp.where(live, value, DEAD)
            at = pl.ds(pl.multiple_of(c * entry_rows + group * 8, 8), 8)
            stack_ref[at, :] = value
        for channel in range(3):
            at = pl.ds(pl.multiple_of((8 + channel) * entry_rows + group * 8, 8), 8)
            stack_ref[at, :] = raw_ref[GEOMETRY + channel, here, :]
        return 0

    lax.fori_loop(0, groups, forward_entries, 0)

    chunks = entries // CHUNK

    def chunk_of(chunk):
        return pl.ds(pl.multiple_of(chunk * CHUNK, CHUNK), CHUNK)

    lane = lax.broadcasted_iota(jnp.int32, (8, 128), 1)
    own_tile = (lane & (tiles - 1)) == lax.broadcasted_iota(jnp.int32, (8, 128), 0)

    def widen(row, _):
        value = stack_ref[pl.ds(row, 16, stride=entry_rows), :]
        high, rest = high_low(value)
        middle, low = high_low(rest)

        def spread(part):
            return [
                jnp.where(own_tile, jnp.broadcast_to(part[8 + ch : 9 + ch, :], (8, 128)), 0.0)
                for ch in range(3)
            ]

        zero = jnp.zeros((8, 128), F32)
        bright = spread(high)
        pieces = [high[0:8], middle[0:8], low[0:8], zero] + bright + spread(middle) + bright + [zero]
        lanes = pl.ds(pl.multiple_of(row * 128, 128), 128)
        wide_ref[:, lanes] = jnp.concatenate(pieces, axis=0).astype(BF16)
        return 0

    lax.fori_loop(0, entry_rows, widen, 0)

    value, number = monomials((PIXELS, 32), 1)
    left = jnp.where(number < 24, value, 0.0).astype(BF16)
    segment = lax.broadcasted_iota(jnp.int32, (PIXELS, 128), 1) // tiles
    last = 128 // tiles - 1

    def expose(chunk, _):
        alpha_ref[:, chunk_of(chunk)] = jnp.exp2(dot_plain(left, wide_ref[0:32, chunk_of(chunk)]))
        return 0

    lax.fori_loop(0, chunks, expose, 0)

    def colour_rows(row):
        return [
            jnp.broadcast_to(stack_ref[(8 + ch) * entry_rows + row : (8 + ch) * entry_rows + row + 1, :], (8, 128))
            for ch in range(3)
        ]

    def strip_of(strip, part):
        return pl.ds(pl.multiple_of(strip * STRIP + 8 * part, 8), 8)

    parts = STRIP // 8

    def attenuate(strip, _):
        passing = [jnp.ones((8, 128), F32) for _ in range(parts)]
        shown = [[None] * parts for _ in range(3)]
        for row in range(entry_rows):
            cut = slice(128 * row, 128 * row + 128)
            colours = colour_rows(row)
            for part in range(parts):
                weight = passing[part] * alpha_ref[strip_of(strip, part), cut]
                passing[part] = passing[part] - weight
                weight_ref[strip_of(strip, part), cut] = weight
                for ch in range(3):
                    term = weight * colours[ch]
                    shown[ch][part] = term if row == 0 else shown[ch][part] + term
        for part in range(parts):
            pass_ref[strip_of(strip, part), :] = passing[part]
            for ch in range(3):
                shown_ref[ch, strip_of(strip, part), :] = shown[ch][part]
        return 0

    lax.fori_loop(0, PIXELS // STRIP, attenuate, 0)

    through = pass_ref[...]
    hop = 1
    while hop <= last:
        through = through * jnp.where(segment >= hop, pltpu.roll(through, tiles * hop, 1), 1.0)
        hop *= 2
    enter = jnp.where(segment >= 1, pltpu.roll(through, tiles, 1), 1.0)
    enter_ref[...] = enter
    remain = jnp.where(segment == last, backdrop * through, 0.0)
    open_end = jnp.zeros((PIXELS, 128), F32)
    add = jnp.zeros((PIXELS, 128), F32)
    right = jnp.zeros((PIXELS, 128), F32)
    for channel in range(3):
        alone = shown_ref[channel]
        total = alone * enter + remain
        hop = 1
        while hop <= last:
            total = total + pltpu.roll(total, tiles * hop, 1)
            hop *= 2
        image_ref[:, channel, :] = total.T[0:tiles, :]
        wanted = jnp.concatenate([target_ref[:, channel, :]] * (last + 1), axis=0).T
        residual = total - wanted
        high, low = high_low(residual)
        right = jnp.where((segment == channel) | (segment == 3 + channel), high, right)
        right = jnp.where(segment == 6 + channel, low, right)
        shown_ref[channel] = residual
        open_end = open_end + backdrop * residual
        add = add + residual * alone

    right_ref[...] = right.astype(BF16)

    keep = pass_ref[...]
    hop = 1
    while hop <= last:
        inside = segment + hop <= last
        add = add + keep * jnp.where(inside, pltpu.roll(add, 128 - tiles * hop, 1), 0.0)
        keep = keep * jnp.where(inside, pltpu.roll(keep, 128 - tiles * hop, 1), 1.0)
        hop *= 2
    behind_ref[...] = jnp.where(
        segment < last, pltpu.roll(add + keep * open_end, 128 - tiles, 1), open_end
    )

    def sums_at(strip, number, row):
        return pl.ds(pl.multiple_of(((strip * 9 + number) * entry_rows + row) * 8, 8), 8)

    def descend(strip, _):
        behind = [behind_ref[strip_of(strip, part), :] for part in range(parts)]
        enter = [enter_ref[strip_of(strip, part), :] for part in range(parts)]
        residual = [[shown_ref[ch, strip_of(strip, part), :] for part in range(parts)] for ch in range(3)]
        facing = right_ref[pl.ds(pl.multiple_of(strip * STRIP, STRIP), STRIP), 0:80]
        for row in reversed(range(entry_rows)):
            cut = slice(128 * row, 128 * row + 128)
            if row % 2:
                shade = dot_plain(facing, wide_ref[32:112, 128 * row - 128 : 128 * row + 128])
            side = slice(128 * (row % 2), 128 * (row % 2) + 128)
            tint = [None] * 3
            tall = [[None] * 3, [None] * 3]
            for part in range(parts):
                here = [residual[ch][part] for ch in range(3)]
                gap = shade[8 * part : 8 * part + 8, side] - behind[part]
                behind[part] = behind[part] + alpha_ref[strip_of(strip, part), cut] * gap
                weight = weight_ref[strip_of(strip, part), cut] * enter[part]
                slope = weight * gap
                for ch in range(3):
                    term = weight * here[ch]
                    tint[ch] = term if part == 0 else tint[ch] + term
                half, up = part % 2, float(part // 2)
                terms = [slope, slope * up, slope * (up * up)] if up else [slope, None, None]
                for power in range(3):
                    if terms[power] is None:
                        continue
                    known = tall[half][power]
                    tall[half][power] = terms[power] if known is None else known + terms[power]
            base = (strip * (STRIP // 16)).astype(F32) - 7.5
            for half in range(2):
                level, rise, bend = tall[half]
                bend = bend + (2.0 * base) * rise + (base * base) * level
                rise = rise + base * level
                for power, value in ((0, level), (1, rise), (2, bend)):
                    at = 3 * half + power
                    sums_ref[sums_at(strip, at, row), :] = value
            for ch in range(3):
                sums_ref[sums_at(strip, 6 + ch, row), :] = tint[ch]
        return 0

    lax.fori_loop(0, PIXELS // STRIP, descend, 0)

    def gather_sums(group, _):
        def summed(number, sub):
            return sum(
                sums_ref[pl.ds((strip * 9 + number) * 8 * entry_rows + group * 64 + sub, 8, stride=8), :]
                for strip in range(PIXELS // STRIP)
            )

        values = [0.0] * 9
        for sub in range(8):
            for half in range(2):
                x = 8.0 * half + sub - 7.5
                level, rise, bend = [summed(3 * half + power, sub) for power in range(3)]
                terms = [(x * x) * level, x * rise, bend, x * level, rise, level]
                for c in range(6):
                    values[c] = values[c] + terms[c]
            for ch in range(3):
                values[6 + ch] = values[6 + ch] + summed(6 + ch, sub)
        for c, value in enumerate(values):
            line = c * entry_rows if c < 6 else (c + 2) * entry_rows
            stack_ref[pl.ds(pl.multiple_of(line + group * 8, 8), 8), :] = value
        return 0

    lax.fori_loop(0, groups, gather_sums, 0)

    def backward_entries(group, _):
        here = pl.ds(pl.multiple_of(group * 8, 8), 8)
        cam = cam_rows()
        given = [
            stack_ref[pl.ds(pl.multiple_of(c * entry_rows + group * 8, 8), 8), :] for c in range(6)
        ]
        _, pull = jax.vjp(
            lambda raw: entry_coefficients(raw, cam), [raw_ref[p, here, :] for p in range(GEOMETRY)]
        )
        (grads,) = pull(given)
        for channel in range(3):
            at = pl.ds(pl.multiple_of((8 + channel) * entry_rows + group * 8, 8), 8)
            grads.append(stack_ref[at, :])
        for p in range(GEOMETRY + 3):
            high, low = high_low(grads[p])
            raw_ref[p, here, :] = high
            raw_ref[GEOMETRY + 3 + p, here, :] = low
        return 0

    lax.fori_loop(0, groups, backward_entries, 0)

    spans = n_render * cap // SPAN
    half_rows = rows * spans
    view = cam_ref[15:16, :].astype(jnp.int32)

    def spread_out(row, _):
        at_lanes = pl.ds(pl.multiple_of(row * 128, 128), 128)
        slot = slot_ref[pl.ds(row, 1), :]
        span, lane = slot // SPAN, slot & (SPAN - 1)
        lanes_of = lax.broadcasted_iota(jnp.int32, (SPAN, 128), 0) == jnp.broadcast_to(lane, (SPAN, 128))
        hot_ref[:, at_lanes] = jnp.where(lanes_of, 1.0, 0.0).astype(BF16)
        in_span = lax.broadcasted_iota(jnp.int32, (spans, 128), 0) == jnp.broadcast_to(span, (spans, 128))
        key = view * spans + span
        in_view = lax.broadcasted_iota(jnp.int32, (views * spans, 128), 0) == jnp.broadcast_to(
            key, (views * spans, 128)
        )
        for part in range(2):
            base = part * half_rows
            pieces = []
            for p in range(COLOUR_ROW):
                if p < GEOMETRY:
                    value = raw_ref[part * (GEOMETRY + 3) + p, pl.ds(row, 1), :]
                    pieces.append(jnp.where(in_span, jnp.broadcast_to(value, (spans, 128)), 0.0))
                else:
                    pieces.append(jnp.zeros((spans, 128), F32))
                if len(pieces) == 2:
                    at = base + (p - 1) * spans
                    lhs_ref[at : at + 2 * spans, at_lanes] = jnp.concatenate(pieces, axis=0).astype(BF16)
                    pieces = []
            for channel in range(3):
                value = raw_ref[part * (GEOMETRY + 3) + GEOMETRY + channel, pl.ds(row, 1), :]
                value = jnp.where(in_view, jnp.broadcast_to(value, (views * spans, 128)), 0.0)
                at = base + (COLOUR_ROW + channel * views) * spans
                lhs_ref[at : at + views * spans, at_lanes] = value.astype(BF16)

    def spread_rows(step, _):
        for i in range(4):
            spread_out(step * 4 + i, 0)
        return 0

    lax.fori_loop(0, entry_rows // 4, spread_rows, 0)
    product = dot_lanes(lhs_ref[...], hot_ref[...])
    for half in range(SPAN // 128):
        at = slice(half * 2 * half_rows, (half + 1) * 2 * half_rows)
        acc_ref[at, :] = product[:, 128 * half : 128 * half + 128]
    for turn in range(n_render):
        for part in range(cap // SPAN):
            span = (me ^ turn) * (cap // SPAN) + part
            for half in range(SPAN // 128):
                cut = slice(128 * half, 128 * half + 128)
                total = (
                    acc_ref[pl.ds(half * 2 * rows * spans + span, rows, stride=spans), :]
                    + acc_ref[pl.ds(half * 2 * rows * spans + rows * spans + span, rows, stride=spans), :]
                )
                first = part * SPAN + 128 * half
                outs[turn][:, first : first + 128] = total


def collect_kernel(n_render, n_view, *refs):
    blocks, refs = refs[:n_render], refs[n_render:]
    index_ref, origin_ref, refs = refs[0], refs[1], refs[2:]
    outs, (lhs_ref, hot_ref, acc_ref) = refs[:n_view], refs[n_view:]
    rows, cap = blocks[0].shape
    own = outs[0].shape[0] // rows * 128
    gaussians = own * n_view
    spans = gaussians // SPAN
    column = lax.axis_index("view")
    for turn, index in enumerate(partner_rows(index_ref, n_render)):
        lanes = slice(turn * cap, (turn + 1) * cap)
        span, lane = index // SPAN, index & (SPAN - 1)
        hot = lax.broadcasted_iota(jnp.int32, (SPAN, cap), 0) == jnp.broadcast_to(lane, (SPAN, cap))
        hot_ref[:, lanes] = jnp.where(hot, 1.0, 0.0).astype(BF16)
        in_span = lax.broadcasted_iota(jnp.int32, (spans, cap), 0) == jnp.broadcast_to(span, (spans, cap))
        high, low = high_low(blocks[turn][...])
        for part, value in ((0, high), (1, low)):
            for p in range(rows):
                at = (part * rows + p) * spans
                piece = jnp.broadcast_to(value[p : p + 1, :], (spans, cap))
                lhs_ref[at : at + spans, lanes] = jnp.where(in_span, piece, 0.0).astype(BF16)
    product = dot_lanes(lhs_ref[...], hot_ref[...])
    for half in range(2):
        at = slice(half * 2 * rows * spans, (half + 1) * 2 * rows * spans)
        acc_ref[at, :] = product[:, 128 * half : 128 * half + 128]
    strips = own // 128
    for turn in range(n_view):
        for strip in range(strips):
            span = (column ^ turn) * (own // SPAN) + strip // 2
            first = (strip % 2) * 2 * rows * spans
            total = (
                acc_ref[pl.ds(first + span, rows, stride=spans), :]
                + acc_ref[pl.ds(first + rows * spans + span, rows, stride=spans), :]
            )
            outs[turn][pl.ds(strip, rows, stride=strips), :] = total
        outs[turn][GEOMETRY * strips : GEOMETRY * strips + 1, :] = origin_ref[...]


def owner_kernel(n_view, views, *refs):
    blocks, (own_ref, out_ref, sum_ref) = refs[:n_view], refs[n_view:]
    strips = out_ref.shape[1] // 128

    def of(ref, p):
        return ref[p * strips : (p + 1) * strips, :]

    position = [of(own_ref, a) for a in range(3)]
    levels = [[None] * 16 for _ in range(3)]
    moved = [0.0, 0.0, 0.0]
    for block in blocks:
        for w in range(views):
            away = []
            for a in range(3):
                at = 3 * w + a
                offset = block[GEOMETRY * strips : GEOMETRY * strips + 1, at : at + 1]
                away.append(position[a] + jnp.broadcast_to(offset, (strips, 128)))
            inverse = lax.rsqrt(away[0] * away[0] + away[1] * away[1] + away[2] * away[2])
            direction = [part * inverse for part in away]
            basis, pull = jax.vjp(harmonic_basis, *direction)
            tint = [of(block, COLOUR_ROW + ch * views + w) for ch in range(3)]
            for ch in range(3):
                for b in range(16):
                    term = tint[ch] * basis[b]
                    levels[ch][b] = term if levels[ch][b] is None else levels[ch][b] + term
            given = [
                sum(tint[ch] * of(own_ref, GEOMETRY + 16 * ch + b) for ch in range(3)) for b in range(16)
            ]
            turned = pull(given)
            along = sum(turned[a] * direction[a] for a in range(3))
            for a in range(3):
                moved[a] = moved[a] + inverse * (turned[a] - direction[a] * along)
    for p in range(GEOMETRY):
        total = sum(of(block, p) for block in blocks)
        sum_ref[p * strips : (p + 1) * strips, :] = total + moved[p] if p < 3 else total
    for ch in range(3):
        for b in range(16):
            p = GEOMETRY + 16 * ch + b
            sum_ref[p * strips : (p + 1) * strips, :] = levels[ch][b]
    count = out_ref.shape[0]
    for strip in range(strips):
        out_ref[:, 128 * strip : 128 * strip + 128] = sum_ref[pl.ds(strip, count, stride=strips), :]


def swap(blocks, axis):
    n = len(blocks)
    return [blocks[0]] + [
        lax.ppermute(blocks[turn], axis, [(i, i ^ turn) for i in range(n)]) for turn in range(1, n)
    ]


def call(kernel, out_shape, scratch, space, *args):
    return pl.pallas_call(
        kernel,
        out_shape=out_shape,
        in_specs=[pl.BlockSpec(memory_space=space)] * len(args),
        out_specs=[pl.BlockSpec(memory_space=pltpu.VMEM)] * len(out_shape),
        scratch_shapes=scratch,
        compiler_params=pltpu.CompilerParams(vmem_limit_bytes=(64 if space == pl.ANY else 48) * 1024 * 1024),
    )(*args)


def render(n_render, views, arrived, table, code, live, slot, wanted):
    tiles, length = slot.shape
    rows, cap = arrived[0].shape
    view = code // (CROP * CROP)
    cell = code % (CROP * CROP)
    tile_table = sum(
        jnp.where((view == w)[:, None], table[w : w + 1, :13], 0.0) for w in range(views)
    )
    extra = jnp.stack(
        [
            (8 * CROP - 8 - 16 * (cell % CROP)).astype(F32),
            (8 * CROP - 8 - 16 * (cell // CROP)).astype(F32),
            view.astype(F32),
            live.astype(F32),
        ],
        axis=1,
    )
    lane_table = jnp.concatenate([tile_table, extra, jnp.zeros((tiles, 7), F32)], axis=1).T
    lane_table = jnp.tile(lane_table, (1, 128 // tiles))
    slot_lanes = slot.reshape(tiles, 128 // tiles, -1).transpose(2, 1, 0).reshape(-1, 128)
    entries = tiles * length
    entry_rows = entries // 128
    spans = n_render * cap // SPAN
    return call(
        partial(render_kernel, n_render, views),
        [jax.ShapeDtypeStruct(wanted.shape, F32)]
        + [jax.ShapeDtypeStruct((rows, cap), F32)] * n_render,
        [
            pltpu.VMEM((2 * (GEOMETRY + 3), entry_rows, 128), F32),
            pltpu.VMEM((16 * entry_rows, 128), F32),
            pltpu.VMEM((112, entries), BF16),
            pltpu.VMEM((PIXELS, entries), F32),
            pltpu.VMEM((PIXELS, entries), F32),
            pltpu.VMEM((3, PIXELS, 128), F32),
            pltpu.VMEM((PIXELS, 128), F32),
            pltpu.VMEM((PIXELS, 128), F32),
            pltpu.VMEM((PIXELS, 128), F32),
            pltpu.VMEM((PIXELS, 128), BF16),
            pltpu.VMEM((9 * PIXELS // STRIP * 8 * entry_rows, 128), F32),
            pltpu.VMEM((2 * rows * spans, entries), BF16),
            pltpu.VMEM((SPAN, entries), BF16),
            pltpu.VMEM((4 * rows * spans, 128), F32),
        ],
        pltpu.VMEM,
        *arrived,
        slot_lanes,
        lane_table,
        wanted,
    )


def slab(n_render, params, cameras, index):
    views, (count, gaussians), cap = cameras.shape[0], params.shape, index.shape[1]
    rows = -(-(COLOUR_ROW + 3 * views) // 8) * 8
    return call(
        partial(slab_kernel, n_render, views),
        [jax.ShapeDtypeStruct((rows, cap), F32)] * n_render,
        [
            pltpu.VMEM((count, gaussians), F32),
            pltpu.VMEM(cameras.shape, F32),
            pltpu.VMEM((n_render, cap), jnp.int32),
            pltpu.VMEM((n_render, cap), jnp.int32),
            pltpu.VMEM((rows - 8, gaussians), F32),
            pltpu.SemaphoreType.DMA((3 + gaussians // 512,)),
        ],
        pl.ANY,
        params,
        cameras,
        index,
    )


def collect(n_render, n_view, homed, index, origin, own):
    rows, cap = homed[0].shape
    spans = n_view * own // SPAN
    return call(
        partial(collect_kernel, n_render, n_view),
        [jax.ShapeDtypeStruct((rows * own // 128, 128), F32)] * n_view,
        [
            pltpu.VMEM((2 * rows * spans, n_render * cap), BF16),
            pltpu.VMEM((SPAN, n_render * cap), BF16),
            pltpu.VMEM((4 * rows * spans, 128), F32),
        ],
        pltpu.VMEM,
        *homed,
        index,
        origin,
    )


def body(n_render, n_view, params, cameras, send_index, tile_id, tile_count, tile_slot, targets):
    index = send_index[0, 0]
    views = cameras.shape[0]
    own = params.shape[1] // n_view
    table = camera_table(cameras)
    origin = jnp.pad(table[:, 13:16].reshape(1, 3 * views), ((0, 0), (0, 128 - 3 * views)))
    mine = lax.dynamic_slice_in_dim(params, lax.axis_index("view") * own, own, 1).reshape(-1, 128)

    arrived = swap(list(slab(n_render, params, cameras, index)), "render")
    image, *returned = render(
        n_render,
        views,
        arrived,
        table,
        tile_id[0, 0],
        tile_count[0, 0],
        tile_slot[0, 0],
        targets[0, 0],
    )
    homed = swap(returned, "render")
    owned = swap(list(collect(n_render, n_view, homed, index, origin, own)), "view")
    (gradients,) = call(
        partial(owner_kernel, n_view, views),
        [jax.ShapeDtypeStruct((params.shape[0], own), F32)],
        [pltpu.VMEM((params.shape[0] * own // 128, 128), F32)],
        pltpu.VMEM,
        *owned,
        mine,
    )
    return (image[None, None], gradients)


def solution(mesh):
    in_specs = (
        P(None, ("groups", "render")),
        P(("groups", "view"), None),
        P(("groups", "render"), "view", None, None),
        P(("groups", "render"), "view", None),
        P(("groups", "render"), "view", None),
        P(("groups", "render"), "view", None, None),
        P(("groups", "render"), "view", None, None, None),
    )
    out_specs = (
        P(("groups", "render"), "view", None, None, None),
        P(None, ("groups", "render", "view")),
    )
    work = partial(body, mesh.shape["render"], mesh.shape["view"])
    return jax.shard_map(work, mesh=mesh, in_specs=in_specs, out_specs=out_specs, check_vma=False)
```

```python
from functools import partial

import jax
import jax.numpy as jnp
from jax import lax
from jax.experimental import pallas as pl
from jax.experimental.pallas import tpu as pltpu
from jax.sharding import PartitionSpec as P

CROP = 2
PIXELS = 256
GEOMETRY = 11
COLOUR_ROW = 12
SPAN = 256
CHUNK = 2048
STRIP = 256
NEAR = 2
LOG2_E = 1.4426950408889634
DEAD = -1e30

dilation = 0.3
backdrop = 1.0
band_zero = 0.28209479177387814
band_one = 0.4886025119029199
band_two = [
    1.0925484305920792,
    -1.0925484305920792,
    0.31539156525252005,
    -1.0925484305920792,
    0.5462742152960396,
]
band_three = [
    -0.5900435899266435,
    2.890611442640554,
    -0.4570457994644658,
    0.3731763325901154,
    -0.4570457994644658,
    1.445305721320277,
    -0.5900435899266435,
]

F32 = jnp.float32
BF16 = jnp.bfloat16


def harmonic_basis(along_x, along_y, along_z):
    square_x = along_x * along_x
    square_y = along_y * along_y
    square_z = along_z * along_z
    return [
        jnp.full_like(along_x, band_zero),
        -band_one * along_y,
        band_one * along_z,
        -band_one * along_x,
        band_two[0] * along_x * along_y,
        band_two[1] * along_y * along_z,
        band_two[2] * (2.0 * square_z - square_x - square_y),
        band_two[3] * along_x * along_z,
        band_two[4] * (square_x - square_y),
        band_three[0] * along_y * (3.0 * square_x - square_y),
        band_three[1] * along_x * along_y * along_z,
        band_three[2] * along_y * (4.0 * square_z - square_x - square_y),
        band_three[3] * along_z * (2.0 * square_z - 3.0 * square_x - 3.0 * square_y),
        band_three[4] * along_x * (4.0 * square_z - square_x - square_y),
        band_three[5] * along_z * (square_x - square_y),
        band_three[6] * along_x * (square_x - 3.0 * square_y),
    ]


def high_low(value):
    high = value.astype(BF16).astype(F32)
    return high, value - high


def dot_plain(left, right):
    return lax.dot_general(left, right, (((1,), (0,)), ((), ())), preferred_element_type=F32)


def dot_lanes(left, right):
    return lax.dot_general(left, right, (((1,), (1,)), ((), ())), preferred_element_type=F32)


def camera_parts(angles, shift, focal):
    c0, c1, c2 = [jnp.cos(angle) for angle in angles]
    s0, s1, s2 = [jnp.sin(angle) for angle in angles]
    rotation = [
        [c1 * c2, s0 * s1 * c2 - c0 * s2, c0 * s1 * c2 + s0 * s2],
        [c1 * s2, s0 * s1 * s2 + c0 * c2, c0 * s1 * s2 - s0 * c2],
        [-s1, s0 * c1, c0 * c1],
    ]
    origin = [sum(rotation[m][a] * shift[m] for m in range(3)) for a in range(3)]
    return [e for row in rotation for e in row] + shift + [focal] + origin


def lane_pick(source, lanes):
    return jnp.take_along_axis(source, lanes, axis=1, mode="promise_in_bounds")


def partner_rows(index_ref, n_render):
    me = lax.axis_index("render")
    rows = [index_ref[o : o + 1, :] for o in range(n_render)]
    return [
        sum(jnp.where((me ^ turn) == o, rows[o], 0) for o in range(n_render)) for turn in range(n_render)
    ]


def slab_kernel(n_render, views, params_hbm, cameras_hbm, index_hbm, *rest):
    outs, refs = rest[:n_render], rest[n_render:]
    params_ref, cameras_ref, index_ref, order_ref, dense_ref, arrival = refs
    rows, gaussians = outs[0].shape[0], params_ref.shape[1]
    cap = index_ref.shape[1]
    width = 512
    shades = gaussians // width
    count = params_ref.shape[0]
    copies = [
        pltpu.make_async_copy(cameras_hbm, cameras_ref, arrival.at[0]),
        pltpu.make_async_copy(index_hbm, index_ref, arrival.at[1]),
        pltpu.make_async_copy(params_hbm.at[0:8, :], params_ref.at[0:8, :], arrival.at[2]),
    ]
    for step in range(shades):
        lanes = pl.ds(step * width, width)
        copies.append(
            pltpu.make_async_copy(
                params_hbm.at[8:count, lanes], params_ref.at[8:count, lanes], arrival.at[3 + step]
            )
        )
    for copy in copies:
        copy.start()
    copies[0].wait()
    cameras = [cameras_ref[:, a : a + 1] for a in range(7)]
    origin = camera_parts(cameras[0:3], cameras[3:6], cameras[6])[13:16]
    copies[1].wait()
    for turn, row in enumerate(partner_rows(index_ref, n_render)):
        order_ref[turn : turn + 1, :] = row
    copies[2].wait()

    picks = [(turn, step) for turn in range(n_render) for step in range(cap // 128)]

    def shade(step):
        lanes = slice(step * width, step * width + width)
        copies[3 + step].wait()
        dense_ref[0:8, lanes] = params_ref[8:16, lanes]
        away = [params_ref[a : a + 1, lanes] + origin[a] for a in range(3)]
        inverse = lax.rsqrt(away[0] * away[0] + away[1] * away[1] + away[2] * away[2])
        basis = harmonic_basis(*[part * inverse for part in away])
        for channel in range(3):
            base = GEOMETRY + 16 * channel
            colour = 0.5 + basis[0] * params_ref[base : base + 1, lanes]
            for level in range(1, 16):
                colour += basis[level] * params_ref[base + level : base + level + 1, lanes]
            first = COLOUR_ROW + channel * views - 8
            dense_ref[first : first + views, lanes] = colour

    def pick(source, groups, skip, turn, step):
        lanes = slice(128 * step, 128 * step + 128)
        index = jnp.broadcast_to(order_ref[turn : turn + 1, lanes], (8, 128))
        lane, block = index & 127, index >> 7
        found = [jnp.zeros((8, 128), F32) for _ in range(groups)]
        for b in range(gaussians // 128):
            here = block == b
            for s in range(groups):
                piece = source[8 * s : 8 * s + 8, 128 * b : 128 * b + 128]
                found[s] = jnp.where(here, lane_pick(piece, lane), found[s])
        for s in range(groups):
            outs[turn][8 * (s + skip) : 8 * (s + skip) + 8, lanes] = found[s]

    for step in range(shades):
        shade(step)
        for turn, at in picks[step * len(picks) // shades : (step + 1) * len(picks) // shades]:
            pick(params_ref, 1, 0, turn, at)
    for turn, at in picks:
        pick(dense_ref, rows // 8 - 1, 1, turn, at)


def entry_coefficients(raw, cam):
    px, py, pz = raw[0], raw[1], raw[2]
    extent = [jnp.exp(raw[3 + a]) for a in range(3)]
    norm = lax.rsqrt(raw[6] * raw[6] + raw[7] * raw[7] + raw[8] * raw[8] + raw[9] * raw[9])
    qw, qx, qy, qz = [raw[6 + a] * norm for a in range(4)]
    turn = [[cam[3 * a + b] for b in range(3)] for a in range(3)]
    x, y, z = [turn[a][0] * px + turn[a][1] * py + turn[a][2] * pz + cam[9 + a] for a in range(3)]
    scale = cam[12] / z
    slope_x, slope_y = x / z, y / z
    u = cam[12] * slope_x + cam[13]
    v = cam[12] * slope_y + cam[14]
    quat = [
        [1.0 - 2.0 * (qy * qy + qz * qz), 2.0 * (qx * qy - qw * qz), 2.0 * (qx * qz + qw * qy)],
        [2.0 * (qx * qy + qw * qz), 1.0 - 2.0 * (qx * qx + qz * qz), 2.0 * (qy * qz - qw * qx)],
        [2.0 * (qx * qz - qw * qy), 2.0 * (qy * qz + qw * qx), 1.0 - 2.0 * (qx * qx + qy * qy)],
    ]
    screen = [
        [scale * (turn[a][b] - slope * turn[2][b]) for b in range(3)]
        for a, slope in ((0, slope_x), (1, slope_y))
    ]
    foot = [
        [sum(screen[a][m] * quat[m][b] for m in range(3)) * extent[b] for b in range(3)]
        for a in range(2)
    ]
    cov_a = sum(foot[0][b] * foot[0][b] for b in range(3)) + dilation
    cov_b = sum(foot[0][b] * foot[1][b] for b in range(3))
    cov_c = sum(foot[1][b] * foot[1][b] for b in range(3)) + dilation
    inverse = 1.0 / (cov_a * cov_c - cov_b * cov_b)
    conic_a, conic_b, conic_c = cov_c * inverse, -cov_b * inverse, cov_a * inverse
    log_opacity = -jnp.log(1.0 + jnp.exp(-raw[10]))
    pull_x = conic_a * u + conic_b * v
    pull_y = conic_c * v + conic_b * u
    return [
        -0.5 * conic_a,
        -conic_b,
        -0.5 * conic_c,
        pull_x,
        pull_y,
        log_opacity - 0.5 * (pull_x * u + pull_y * v),
    ]


def monomials(shape, axis):
    number = lax.broadcasted_iota(jnp.int32, shape, axis)
    pixel = lax.broadcasted_iota(jnp.int32, shape, 1 - axis)
    x = (pixel & 15).astype(F32) - 7.5
    y = (pixel >> 4).astype(F32) - 7.5
    value = jnp.zeros(shape, F32)
    for at, term in enumerate((x * x, x * y, y * y, x, y, jnp.ones_like(x))):
        value = jnp.where((number & 7) == at, term, value)
    return value, number


def fetch(slot, view, views, blocks, turns, found):
    me = lax.axis_index("render")
    per_block = blocks[0].shape[1] // 128
    lane, block = slot & 127, slot >> 7
    found = list(found)
    for ref, turn in zip(blocks, turns):
        first = (me ^ turn) * per_block
        for j in range(per_block):
            hit = block == first + j
            cut = slice(128 * j, 128 * j + 128)
            for p in range(GEOMETRY):
                piece = jnp.broadcast_to(ref[p : p + 1, cut], (8, 128))
                found[p] = jnp.where(hit, lane_pick(piece, lane), found[p])
            for w in range(views):
                seen = hit & (view == w)
                for channel in range(3):
                    p = COLOUR_ROW + channel * views + w
                    piece = jnp.broadcast_to(ref[p : p + 1, cut], (8, 128))
                    at = GEOMETRY + channel
                    found[at] = jnp.where(seen, lane_pick(piece, lane), found[at])
    return found


def meet_kernel(views, small_ref, list_ref, *refs):
    blocks, (slot_ref, cam_ref, part_ref, origin_ref) = refs[:NEAR], refs[NEAR:]
    tiles, length = list_ref.shape
    segments = 128 // tiles
    steps = length // segments
    lists = list_ref[...].astype(F32)
    turned = []
    for segment in range(segments):
        begin = segment * steps
        base = lists[:, begin // 128 * 128 : begin // 128 * 128 + 128]
        turned.append(pltpu.roll(base, 128 - begin % 128, 1) if begin % 128 else base)
    slot_ref[...] = jnp.concatenate(turned, axis=0).T[0:steps, :].astype(jnp.int32)

    def small(row):
        return jnp.broadcast_to(small_ref[row : row + 1, :], (8, 128))

    lane = lax.broadcasted_iota(jnp.int32, (8, 128), 1)
    tile = lane & (tiles - 1)
    code = lane_pick(small(7), tile).astype(jnp.int32)
    view = code // (CROP * CROP)
    cell = code - view * (CROP * CROP)
    down = cell // CROP
    parts = camera_parts([small(a) for a in range(3)], [small(a) for a in (3, 4, 5)], small(6))
    for c in range(13):
        cam_ref[c : c + 1, :] = lane_pick(parts[c], view)[0:1, :]
    cam_ref[13:14, :] = (8 * CROP - 8 - 16 * (cell - down * CROP)).astype(F32)[0:1, :]
    cam_ref[14:15, :] = (8 * CROP - 8 - 16 * down).astype(F32)[0:1, :]
    cam_ref[15:16, :] = view.astype(F32)[0:1, :]
    cam_ref[16:17, :] = lane_pick(small(8), tile)[0:1, :]
    row = jnp.where(lane < 32, parts[13], 0.0)
    for a in (1, 2):
        row = row + pltpu.roll(jnp.where(lane < 32, parts[13 + a], 0.0), 32 * a, 1)
    origin_ref[...] = row[0:1, :]

    def group_work(group, _):
        here = pl.ds(pl.multiple_of(group * 8, 8), 8)
        found = [jnp.zeros((8, 128), F32) for _ in range(GEOMETRY + 3)]
        found = fetch(slot_ref[here, :], view, views, blocks, range(NEAR), found)
        for p in range(GEOMETRY + 3):
            part_ref[p, here, :] = found[p]
        return 0

    lax.fori_loop(0, steps // 8, group_work, 0)


def render_kernel(n_render, views, *refs):
    blocks, refs = refs[: n_render - NEAR], refs[n_render - NEAR :]
    slot_ref, cam_ref, part_ref, target_ref, refs = *refs[0:4], refs[4:]
    image_ref, outs, refs = refs[0], refs[1 : 1 + n_render], refs[1 + n_render :]
    raw_ref, stack_ref, wide_ref, alpha_ref, weight_ref, shown_ref, pass_ref, enter_ref, behind_ref, right_ref, sums_ref, lhs_ref, hot_ref, acc_ref = refs
    tiles = target_ref.shape[0]
    entry_rows = slot_ref.shape[0]
    entries = entry_rows * 128
    rows, cap = blocks[0].shape
    me = lax.axis_index("render")
    groups = entry_rows // 8

    def complete(group, _):
        here = pl.ds(pl.multiple_of(group * 8, 8), 8)
        view = jnp.broadcast_to(cam_ref[15:16, :], (8, 128)).astype(jnp.int32)
        found = [part_ref[p, here, :] for p in range(GEOMETRY + 3)]
        found = fetch(slot_ref[here, :], view, views, blocks, range(NEAR, n_render), found)
        for p in range(GEOMETRY + 3):
            raw_ref[p, here, :] = found[p]
        return 0

    lax.fori_loop(0, groups, complete, 0)

    def cam_rows():
        return [jnp.broadcast_to(cam_ref[i : i + 1, :], (8, 128)) for i in range(15)]

    stack_ref[...] = jnp.zeros_like(stack_ref)

    def forward_entries(group, _):
        here = pl.ds(pl.multiple_of(group * 8, 8), 8)
        coefficient = entry_coefficients([raw_ref[p, here, :] for p in range(GEOMETRY)], cam_rows())
        row = lax.broadcasted_iota(jnp.int32, (8, 128), 0) + group * 8
        lane = lax.broadcasted_iota(jnp.int32, (8, 128), 1)
        order = (lane // tiles) * entry_rows + row
        live = order < jnp.broadcast_to(cam_ref[16:17, :], (8, 128)).astype(jnp.int32)
        for c in range(6):
            value = coefficient[c] * LOG2_E
            if c == 5:
                value = jnp.where(live, value, DEAD)
            at = pl.ds(pl.multiple_of(c * entry_rows + group * 8, 8), 8)
            stack_ref[at, :] = value
        for channel in range(3):
            at = pl.ds(pl.multiple_of((8 + channel) * entry_rows + group * 8, 8), 8)
            stack_ref[at, :] = raw_ref[GEOMETRY + channel, here, :]
        return 0

    lax.fori_loop(0, groups, forward_entries, 0)

    chunks = entries // CHUNK

    def chunk_of(chunk):
        return pl.ds(pl.multiple_of(chunk * CHUNK, CHUNK), CHUNK)

    lane = lax.broadcasted_iota(jnp.int32, (8, 128), 1)
    own_tile = (lane & (tiles - 1)) == lax.broadcasted_iota(jnp.int32, (8, 128), 0)

    def widen(row, _):
        value = stack_ref[pl.ds(row, 16, stride=entry_rows), :]
        high, rest = high_low(value)
        middle, low = high_low(rest)

        def spread(part):
            return [
                jnp.where(own_tile, jnp.broadcast_to(part[8 + ch : 9 + ch, :], (8, 128)), 0.0)
                for ch in range(3)
            ]

        zero = jnp.zeros((8, 128), F32)
        bright = spread(high)
        pieces = [high[0:8], middle[0:8], low[0:8], zero] + bright + spread(middle) + bright + [zero]
        lanes = pl.ds(pl.multiple_of(row * 128, 128), 128)
        wide_ref[:, lanes] = jnp.concatenate(pieces, axis=0).astype(BF16)
        return 0

    lax.fori_loop(0, entry_rows, widen, 0)

    value, number = monomials((PIXELS, 32), 1)
    left = jnp.where(number < 24, value, 0.0).astype(BF16)
    segment = lax.broadcasted_iota(jnp.int32, (PIXELS, 128), 1) // tiles
    last = 128 // tiles - 1

    def expose(chunk, _):
        alpha = jnp.exp2(dot_plain(left, wide_ref[0:32, chunk_of(chunk)]))
        for k in range(CHUNK // 128):
            alpha_ref[chunk * (CHUNK // 128) + k] = alpha[:, 128 * k : 128 * k + 128]
        return 0

    lax.fori_loop(0, chunks, expose, 0)

    def colour_rows(row):
        return [
            jnp.broadcast_to(stack_ref[(8 + ch) * entry_rows + row : (8 + ch) * entry_rows + row + 1, :], (8, 128))
            for ch in range(3)
        ]

    def strip_of(strip, part):
        return pl.ds(pl.multiple_of(strip * STRIP + 8 * part, 8), 8)

    parts = STRIP // 8

    def attenuate(strip, _):
        passing = [jnp.ones((8, 128), F32) for _ in range(parts)]
        shown = [[None] * parts for _ in range(3)]
        for row in range(entry_rows):
            colours = colour_rows(row)
            for part in range(parts):
                weight = passing[part] * alpha_ref[row, strip_of(strip, part), :]
                passing[part] = passing[part] - weight
                weight_ref[row, strip_of(strip, part), :] = weight
                for ch in range(3):
                    term = weight * colours[ch]
                    shown[ch][part] = term if row == 0 else shown[ch][part] + term
        for part in range(parts):
            pass_ref[strip_of(strip, part), :] = passing[part]
            for ch in range(3):
                shown_ref[ch, strip_of(strip, part), :] = shown[ch][part]
        return 0

    lax.fori_loop(0, PIXELS // STRIP, attenuate, 0)

    through = pass_ref[...]
    hop = 1
    while hop <= last:
        through = through * jnp.where(segment >= hop, pltpu.roll(through, tiles * hop, 1), 1.0)
        hop *= 2
    enter = jnp.where(segment >= 1, pltpu.roll(through, tiles, 1), 1.0)
    enter_ref[...] = enter
    remain = jnp.where(segment == last, backdrop * through, 0.0)
    open_end = jnp.zeros((PIXELS, 128), F32)
    add = jnp.zeros((PIXELS, 128), F32)
    right = jnp.zeros((PIXELS, 128), F32)
    for channel in range(3):
        alone = shown_ref[channel]
        total = alone * enter + remain
        hop = 1
        while hop <= last:
            total = total + pltpu.roll(total, tiles * hop, 1)
            hop *= 2
        image_ref[:, channel, :] = total.T[0:tiles, :]
        wanted = jnp.concatenate([target_ref[:, channel, :]] * (last + 1), axis=0).T
        residual = total - wanted
        high, low = high_low(residual)
        right = jnp.where((segment == channel) | (segment == 3 + channel), high, right)
        right = jnp.where(segment == 6 + channel, low, right)
        shown_ref[channel] = residual
        open_end = open_end + backdrop * residual
        add = add + residual * alone

    right_ref[...] = right.astype(BF16)

    keep = pass_ref[...]
    hop = 1
    while hop <= last:
        inside = segment + hop <= last
        add = add + keep * jnp.where(inside, pltpu.roll(add, 128 - tiles * hop, 1), 0.0)
        keep = keep * jnp.where(inside, pltpu.roll(keep, 128 - tiles * hop, 1), 1.0)
        hop *= 2
    behind_ref[...] = jnp.where(
        segment < last, pltpu.roll(add + keep * open_end, 128 - tiles, 1), open_end
    )

    def sums_at(strip, number, row):
        return pl.ds(pl.multiple_of(((strip * 9 + number) * entry_rows + row) * 8, 8), 8)

    def descend(strip, _):
        behind = [behind_ref[strip_of(strip, part), :] for part in range(parts)]
        enter = [enter_ref[strip_of(strip, part), :] for part in range(parts)]
        residual = [[shown_ref[ch, strip_of(strip, part), :] for part in range(parts)] for ch in range(3)]
        facing = right_ref[pl.ds(pl.multiple_of(strip * STRIP, STRIP), STRIP), 0:80]
        for row in reversed(range(entry_rows)):
            if row % 2:
                shade = dot_plain(facing, wide_ref[32:112, 128 * row - 128 : 128 * row + 128])
            side = slice(128 * (row % 2), 128 * (row % 2) + 128)
            tint = [None] * 3
            tall = [[None] * 3, [None] * 3]
            for part in range(parts):
                here = [residual[ch][part] for ch in range(3)]
                gap = shade[8 * part : 8 * part + 8, side] - behind[part]
                behind[part] = behind[part] + alpha_ref[row, strip_of(strip, part), :] * gap
                weight = weight_ref[row, strip_of(strip, part), :] * enter[part]
                slope = weight * gap
                for ch in range(3):
                    term = weight * here[ch]
                    tint[ch] = term if part == 0 else tint[ch] + term
                half, up = part % 2, float(part // 2)
                terms = [slope, slope * up, slope * (up * up)] if up else [slope, None, None]
                for power in range(3):
                    if terms[power] is None:
                        continue
                    known = tall[half][power]
                    tall[half][power] = terms[power] if known is None else known + terms[power]
            base = (strip * (STRIP // 16)).astype(F32) - 7.5
            for half in range(2):
                level, rise, bend = tall[half]
                bend = bend + (2.0 * base) * rise + (base * base) * level
                rise = rise + base * level
                for power, value in ((0, level), (1, rise), (2, bend)):
                    at = 3 * half + power
                    sums_ref[sums_at(strip, at, row), :] = value
            for ch in range(3):
                sums_ref[sums_at(strip, 6 + ch, row), :] = tint[ch]
        return 0

    lax.fori_loop(0, PIXELS // STRIP, descend, 0)

    def gather_sums(group, _):
        def summed(number, sub):
            return sum(
                sums_ref[pl.ds((strip * 9 + number) * 8 * entry_rows + group * 64 + sub, 8, stride=8), :]
                for strip in range(PIXELS // STRIP)
            )

        values = [0.0] * 9
        for sub in range(8):
            for half in range(2):
                x = 8.0 * half + sub - 7.5
                level, rise, bend = [summed(3 * half + power, sub) for power in range(3)]
                terms = [(x * x) * level, x * rise, bend, x * level, rise, level]
                for c in range(6):
                    values[c] = values[c] + terms[c]
            for ch in range(3):
                values[6 + ch] = values[6 + ch] + summed(6 + ch, sub)
        for c, value in enumerate(values):
            line = c * entry_rows if c < 6 else (c + 2) * entry_rows
            stack_ref[pl.ds(pl.multiple_of(line + group * 8, 8), 8), :] = value
        return 0

    lax.fori_loop(0, groups, gather_sums, 0)

    def backward_entries(group, _):
        here = pl.ds(pl.multiple_of(group * 8, 8), 8)
        cam = cam_rows()
        given = [
            stack_ref[pl.ds(pl.multiple_of(c * entry_rows + group * 8, 8), 8), :] for c in range(6)
        ]
        _, pull = jax.vjp(
            lambda raw: entry_coefficients(raw, cam), [raw_ref[p, here, :] for p in range(GEOMETRY)]
        )
        (grads,) = pull(given)
        for channel in range(3):
            at = pl.ds(pl.multiple_of((8 + channel) * entry_rows + group * 8, 8), 8)
            grads.append(stack_ref[at, :])
        for p in range(GEOMETRY + 3):
            high, low = high_low(grads[p])
            raw_ref[p, here, :] = high
            raw_ref[GEOMETRY + 3 + p, here, :] = low
        return 0

    lax.fori_loop(0, groups, backward_entries, 0)

    spans = n_render * cap // SPAN
    half_rows = rows * spans
    view = cam_ref[15:16, :].astype(jnp.int32)

    def spread_out(row, _):
        at_lanes = pl.ds(pl.multiple_of(row * 128, 128), 128)
        slot = slot_ref[pl.ds(row, 1), :]
        span, lane = slot // SPAN, slot & (SPAN - 1)
        lanes_of = lax.broadcasted_iota(jnp.int32, (SPAN, 128), 0) == jnp.broadcast_to(lane, (SPAN, 128))
        hot_ref[:, at_lanes] = jnp.where(lanes_of, 1.0, 0.0).astype(BF16)
        in_span = lax.broadcasted_iota(jnp.int32, (spans, 128), 0) == jnp.broadcast_to(span, (spans, 128))
        key = view * spans + span
        in_view = lax.broadcasted_iota(jnp.int32, (views * spans, 128), 0) == jnp.broadcast_to(
            key, (views * spans, 128)
        )
        for part in range(2):
            base = part * half_rows
            pieces = []
            for p in range(COLOUR_ROW):
                if p < GEOMETRY:
                    value = raw_ref[part * (GEOMETRY + 3) + p, pl.ds(row, 1), :]
                    pieces.append(jnp.where(in_span, jnp.broadcast_to(value, (spans, 128)), 0.0))
                else:
                    pieces.append(jnp.zeros((spans, 128), F32))
                if len(pieces) == 2:
                    at = base + (p - 1) * spans
                    lhs_ref[at : at + 2 * spans, at_lanes] = jnp.concatenate(pieces, axis=0).astype(BF16)
                    pieces = []
            for channel in range(3):
                value = raw_ref[part * (GEOMETRY + 3) + GEOMETRY + channel, pl.ds(row, 1), :]
                value = jnp.where(in_view, jnp.broadcast_to(value, (views * spans, 128)), 0.0)
                at = base + (COLOUR_ROW + channel * views) * spans
                lhs_ref[at : at + views * spans, at_lanes] = value.astype(BF16)

    def spread_rows(step, _):
        for i in range(4):
            spread_out(step * 4 + i, 0)
        return 0

    lax.fori_loop(0, entry_rows // 4, spread_rows, 0)
    product = dot_lanes(lhs_ref[...], hot_ref[...])
    for half in range(SPAN // 128):
        at = slice(half * 2 * half_rows, (half + 1) * 2 * half_rows)
        acc_ref[at, :] = product[:, 128 * half : 128 * half + 128]
    for turn in range(n_render):
        for part in range(cap // SPAN):
            span = (me ^ turn) * (cap // SPAN) + part
            for half in range(SPAN // 128):
                cut = slice(128 * half, 128 * half + 128)
                total = (
                    acc_ref[pl.ds(half * 2 * rows * spans + span, rows, stride=spans), :]
                    + acc_ref[pl.ds(half * 2 * rows * spans + rows * spans + span, rows, stride=spans), :]
                )
                first = part * SPAN + 128 * half
                outs[turn][:, first : first + 128] = total


def collect_kernel(n_render, n_view, own, turns, *refs):
    final = turns[-1] == n_render - 1
    blocks, refs = refs[: len(turns)], refs[len(turns) :]
    index_ref, refs = refs[0], refs[1:]
    rows, cap = blocks[0].shape
    spans = own * n_view // SPAN
    if final:
        origin_ref, before_ref, refs = refs[0], refs[1], refs[2:]
        outs, (lhs_ref, hot_ref, acc_ref) = refs[:n_view], refs[n_view:]
    else:
        acc_ref, lhs_ref, hot_ref = refs
    column = lax.axis_index("view")
    order = partner_rows(index_ref, n_render)
    for place, turn in enumerate(turns):
        lanes = slice(place * cap, (place + 1) * cap)
        index = order[turn]
        span, lane = index // SPAN, index & (SPAN - 1)
        hot = lax.broadcasted_iota(jnp.int32, (SPAN, cap), 0) == jnp.broadcast_to(lane, (SPAN, cap))
        hot_ref[:, lanes] = jnp.where(hot, 1.0, 0.0).astype(BF16)
        in_span = lax.broadcasted_iota(jnp.int32, (spans, cap), 0) == jnp.broadcast_to(span, (spans, cap))
        high, low = high_low(blocks[place][...])
        for part, value in ((0, high), (1, low)):
            for p in range(rows):
                at = (part * rows + p) * spans
                piece = jnp.broadcast_to(value[p : p + 1, :], (spans, cap))
                lhs_ref[at : at + spans, lanes] = jnp.where(in_span, piece, 0.0).astype(BF16)
    product = dot_lanes(lhs_ref[...], hot_ref[...])
    for half in range(2):
        at = slice(half * 2 * rows * spans, (half + 1) * 2 * rows * spans)
        piece = product[:, 128 * half : 128 * half + 128]
        acc_ref[at, :] = piece + before_ref[at, :] if final else piece
    if not final:
        return
    strips = own // 128
    for turn in range(n_view):
        for strip in range(strips):
            span = (column ^ turn) * (own // SPAN) + strip // 2
            first = (strip % 2) * 2 * rows * spans
            total = (
                acc_ref[pl.ds(first + span, rows, stride=spans), :]
                + acc_ref[pl.ds(first + rows * spans + span, rows, stride=spans), :]
            )
            outs[turn][pl.ds(strip, rows, stride=strips), :] = total
        outs[turn][GEOMETRY * strips : GEOMETRY * strips + 1, :] = origin_ref[...]


def owner_kernel(views, n_blocks, final, *refs):
    blocks, refs = refs[:n_blocks], refs[n_blocks:]
    own_ref, refs = refs[0], refs[1:]
    if final:
        before_ref, out_ref, sum_ref = refs
        strips = out_ref.shape[1] // 128
    else:
        (sum_ref,) = refs
        strips = sum_ref.shape[0] // (GEOMETRY + 48)

    def of(ref, p):
        return ref[p * strips : (p + 1) * strips, :]

    def known(p):
        return of(before_ref, p) if final else None

    def plus(total, term):
        return term if total is None else total + term

    position = [of(own_ref, a) for a in range(3)]
    levels = [[known(GEOMETRY + 16 * ch + b) for b in range(16)] for ch in range(3)]
    moved = [known(a) for a in range(3)]
    for block in blocks:
        for w in range(views):
            away = []
            for a in range(3):
                at = 32 * a + w
                offset = block[GEOMETRY * strips : GEOMETRY * strips + 1, at : at + 1]
                away.append(position[a] + jnp.broadcast_to(offset, (strips, 128)))
            inverse = lax.rsqrt(away[0] * away[0] + away[1] * away[1] + away[2] * away[2])
            direction = [part * inverse for part in away]
            basis, pull = jax.vjp(harmonic_basis, *direction)
            tint = [of(block, COLOUR_ROW + ch * views + w) for ch in range(3)]
            for ch in range(3):
                for b in range(16):
                    levels[ch][b] = plus(levels[ch][b], tint[ch] * basis[b])
            given = [
                sum(tint[ch] * of(own_ref, GEOMETRY + 16 * ch + b) for ch in range(3)) for b in range(16)
            ]
            turned = pull(given)
            along = sum(turned[a] * direction[a] for a in range(3))
            for a in range(3):
                moved[a] = plus(moved[a], inverse * (turned[a] - direction[a] * along))
    for p in range(GEOMETRY):
        total = moved[p] if p < 3 else known(p)
        for block in blocks:
            total = plus(total, of(block, p))
        sum_ref[p * strips : (p + 1) * strips, :] = total
    for ch in range(3):
        for b in range(16):
            p = GEOMETRY + 16 * ch + b
            sum_ref[p * strips : (p + 1) * strips, :] = levels[ch][b]
    if final:
        count = out_ref.shape[0]
        for strip in range(strips):
            out_ref[:, 128 * strip : 128 * strip + 128] = sum_ref[pl.ds(strip, count, stride=strips), :]


def swap(blocks, axis):
    n = len(blocks)
    return [blocks[0]] + [
        lax.ppermute(blocks[turn], axis, [(i, i ^ turn) for i in range(n)]) for turn in range(1, n)
    ]


def call(kernel, out_shape, scratch, space, *args):
    return pl.pallas_call(
        kernel,
        out_shape=out_shape,
        in_specs=[pl.BlockSpec(memory_space=space)] * len(args),
        out_specs=[pl.BlockSpec(memory_space=pltpu.VMEM)] * len(out_shape),
        scratch_shapes=scratch,
        compiler_params=pltpu.CompilerParams(vmem_limit_bytes=(64 if space == pl.ANY else 48) * 1024 * 1024),
    )(*args)


def meet(arrived, cameras, code, live, lists):
    views, (tiles, length) = cameras.shape[0], lists.shape
    rows = [jnp.pad(cameras.T, ((0, 0), (0, 128 - views)))]
    for ids in (code, live):
        rows.append(jnp.pad(ids.astype(F32)[None], ((0, 0), (0, 128 - tiles))))
    small = jnp.concatenate(rows + [jnp.zeros((7, 128), F32)], axis=0)
    entry_rows = tiles * length // 128
    return call(
        partial(meet_kernel, views),
        [
            jax.ShapeDtypeStruct((entry_rows, 128), jnp.int32),
            jax.ShapeDtypeStruct((24, 128), F32),
            jax.ShapeDtypeStruct((GEOMETRY + 3, entry_rows, 128), F32),
            jax.ShapeDtypeStruct((1, 128), F32),
        ],
        [],
        pltpu.VMEM,
        small,
        lists,
        *arrived[:NEAR],
    )


def render(n_render, views, arrived, slot_lanes, lane_table, part, wanted):
    rows, cap = arrived[0].shape
    entry_rows = slot_lanes.shape[0]
    entries = entry_rows * 128
    spans = n_render * cap // SPAN
    return call(
        partial(render_kernel, n_render, views),
        [jax.ShapeDtypeStruct(wanted.shape, F32)]
        + [jax.ShapeDtypeStruct((rows, cap), F32)] * n_render,
        [
            pltpu.VMEM((2 * (GEOMETRY + 3), entry_rows, 128), F32),
            pltpu.VMEM((16 * entry_rows, 128), F32),
            pltpu.VMEM((112, entries), BF16),
            pltpu.VMEM((entry_rows, PIXELS, 128), F32),
            pltpu.VMEM((entry_rows, PIXELS, 128), F32),
            pltpu.VMEM((3, PIXELS, 128), F32),
            pltpu.VMEM((PIXELS, 128), F32),
            pltpu.VMEM((PIXELS, 128), F32),
            pltpu.VMEM((PIXELS, 128), F32),
            pltpu.VMEM((PIXELS, 128), BF16),
            pltpu.VMEM((9 * PIXELS // STRIP * 8 * entry_rows, 128), F32),
            pltpu.VMEM((2 * rows * spans, entries), BF16),
            pltpu.VMEM((SPAN, entries), BF16),
            pltpu.VMEM((4 * rows * spans, 128), F32),
        ],
        pltpu.VMEM,
        *arrived[NEAR:],
        slot_lanes,
        lane_table,
        part,
        wanted,
    )


def slab(n_render, params, cameras, index):
    views, (count, gaussians), cap = cameras.shape[0], params.shape, index.shape[1]
    rows = -(-(COLOUR_ROW + 3 * views) // 8) * 8
    return call(
        partial(slab_kernel, n_render, views),
        [jax.ShapeDtypeStruct((rows, cap), F32)] * n_render,
        [
            pltpu.VMEM((count, gaussians), F32),
            pltpu.VMEM(cameras.shape, F32),
            pltpu.VMEM((n_render, cap), jnp.int32),
            pltpu.VMEM((n_render, cap), jnp.int32),
            pltpu.VMEM((rows - 8, gaussians), F32),
            pltpu.SemaphoreType.DMA((3 + gaussians // 512,)),
        ],
        pl.ANY,
        params,
        cameras,
        index,
    )


def collect(n_render, n_view, homed, index, origin, own):
    rows, cap = homed[0].shape
    spans = n_view * own // SPAN
    total = jax.ShapeDtypeStruct((4 * rows * spans, 128), F32)

    def scratch(turns):
        return [
            pltpu.VMEM((2 * rows * spans, len(turns) * cap), BF16),
            pltpu.VMEM((SPAN, len(turns) * cap), BF16),
        ]

    near, far = tuple(range(2)), tuple(range(2, n_render))
    (early,) = call(
        partial(collect_kernel, n_render, n_view, own, near),
        [total],
        scratch(near),
        pltpu.VMEM,
        *homed[:2],
        index,
    )
    return call(
        partial(collect_kernel, n_render, n_view, own, far),
        [jax.ShapeDtypeStruct((rows * own // 128, 128), F32)] * n_view,
        scratch(far) + [pltpu.VMEM(total.shape, F32)],
        pltpu.VMEM,
        *homed[2:],
        index,
        origin,
        early,
    )


def body(n_render, n_view, params, cameras, send_index, tile_id, tile_count, tile_slot, targets):
    index = send_index[0, 0]
    views = cameras.shape[0]
    own = params.shape[1] // n_view
    mine = lax.dynamic_slice_in_dim(params, lax.axis_index("view") * own, own, 1).reshape(-1, 128)

    arrived = swap(list(slab(n_render, params, cameras, index)), "render")
    slot_lanes, lane_table, part, origin = meet(
        arrived, cameras, tile_id[0, 0], tile_count[0, 0], tile_slot[0, 0]
    )
    image, *returned = render(n_render, views, arrived, slot_lanes, lane_table, part, targets[0, 0])
    homed = swap(returned, "render")
    owned = swap(list(collect(n_render, n_view, homed, index, origin, own)), "view")
    (early,) = call(
        partial(owner_kernel, views, 2, False),
        [jax.ShapeDtypeStruct(mine.shape, F32)],
        [],
        pltpu.VMEM,
        *owned[:2],
        mine,
    )
    (gradients,) = call(
        partial(owner_kernel, views, n_view - 2, True),
        [jax.ShapeDtypeStruct((params.shape[0], own), F32)],
        [pltpu.VMEM(mine.shape, F32)],
        pltpu.VMEM,
        *owned[2:],
        mine,
        early,
    )
    return (image[None, None], gradients)


def solution(mesh):
    in_specs = (
        P(None, ("groups", "render")),
        P(("groups", "view"), None),
        P(("groups", "render"), "view", None, None),
        P(("groups", "render"), "view", None),
        P(("groups", "render"), "view", None),
        P(("groups", "render"), "view", None, None),
        P(("groups", "render"), "view", None, None, None),
    )
    out_specs = (
        P(("groups", "render"), "view", None, None, None),
        P(None, ("groups", "render", "view")),
    )
    work = partial(body, mesh.shape["render"], mesh.shape["view"])
    return jax.shard_map(work, mesh=mesh, in_specs=in_specs, out_specs=out_specs, check_vma=False)
```

```python
from functools import partial

import jax
import jax.numpy as jnp
from jax import lax
from jax.experimental import pallas as pl
from jax.experimental.pallas import tpu as pltpu
from jax.sharding import PartitionSpec as P

CROP = 2
PIXELS = 256
GEOMETRY = 11
COLOUR_ROW = 12
TURN_ROW = 6
SPAN = 256
CHUNK = 2048
STRIP = 256
NEAR = 2
LOG2_E = 1.4426950408889634
DEAD = -1e30

dilation = 0.3
backdrop = 1.0
band_zero = 0.28209479177387814
band_one = 0.4886025119029199
band_two = [
    1.0925484305920792,
    -1.0925484305920792,
    0.31539156525252005,
    -1.0925484305920792,
    0.5462742152960396,
]
band_three = [
    -0.5900435899266435,
    2.890611442640554,
    -0.4570457994644658,
    0.3731763325901154,
    -0.4570457994644658,
    1.445305721320277,
    -0.5900435899266435,
]

F32 = jnp.float32
BF16 = jnp.bfloat16


def harmonic_basis(along_x, along_y, along_z):
    square_x = along_x * along_x
    square_y = along_y * along_y
    square_z = along_z * along_z
    return [
        jnp.full_like(along_x, band_zero),
        -band_one * along_y,
        band_one * along_z,
        -band_one * along_x,
        band_two[0] * along_x * along_y,
        band_two[1] * along_y * along_z,
        band_two[2] * (2.0 * square_z - square_x - square_y),
        band_two[3] * along_x * along_z,
        band_two[4] * (square_x - square_y),
        band_three[0] * along_y * (3.0 * square_x - square_y),
        band_three[1] * along_x * along_y * along_z,
        band_three[2] * along_y * (4.0 * square_z - square_x - square_y),
        band_three[3] * along_z * (2.0 * square_z - 3.0 * square_x - 3.0 * square_y),
        band_three[4] * along_x * (4.0 * square_z - square_x - square_y),
        band_three[5] * along_z * (square_x - square_y),
        band_three[6] * along_x * (square_x - 3.0 * square_y),
    ]


def high_low(value):
    high = value.astype(BF16).astype(F32)
    return high, value - high


def dot_plain(left, right):
    return lax.dot_general(left, right, (((1,), (0,)), ((), ())), preferred_element_type=F32)


def dot_lanes(left, right):
    return lax.dot_general(left, right, (((1,), (1,)), ((), ())), preferred_element_type=F32)


def camera_parts(angles, shift, focal):
    c0, c1, c2 = [jnp.cos(angle) for angle in angles]
    s0, s1, s2 = [jnp.sin(angle) for angle in angles]
    rotation = [
        [c1 * c2, s0 * s1 * c2 - c0 * s2, c0 * s1 * c2 + s0 * s2],
        [c1 * s2, s0 * s1 * s2 + c0 * c2, c0 * s1 * s2 - s0 * c2],
        [-s1, s0 * c1, c0 * c1],
    ]
    origin = [sum(rotation[m][a] * shift[m] for m in range(3)) for a in range(3)]
    return [e for row in rotation for e in row] + shift + [focal] + origin


def lane_pick(source, lanes):
    return jnp.take_along_axis(source, lanes, axis=1, mode="promise_in_bounds")


def partner_rows(index_ref, n_render):
    me = lax.axis_index("render")
    rows = [index_ref[o : o + 1, :] for o in range(n_render)]
    return [
        sum(jnp.where((me ^ turn) == o, rows[o], 0) for o in range(n_render)) for turn in range(n_render)
    ]


def slab_kernel(n_render, views, params_hbm, cameras_hbm, index_hbm, *rest):
    outs, refs = rest[:n_render], rest[n_render:]
    params_ref, cameras_ref, index_ref, order_ref, dense_ref, arrival = refs
    rows, gaussians = outs[0].shape[0], params_ref.shape[1]
    cap = index_ref.shape[1]
    width = 512
    shades = gaussians // width
    count = params_ref.shape[0]
    copies = [
        pltpu.make_async_copy(cameras_hbm, cameras_ref, arrival.at[0]),
        pltpu.make_async_copy(index_hbm, index_ref, arrival.at[1]),
        pltpu.make_async_copy(params_hbm.at[0:8, :], params_ref.at[0:8, :], arrival.at[2]),
    ]
    for step in range(shades):
        lanes = pl.ds(step * width, width)
        copies.append(
            pltpu.make_async_copy(
                params_hbm.at[8:count, lanes], params_ref.at[8:count, lanes], arrival.at[3 + step]
            )
        )
    for copy in copies:
        copy.start()
    copies[0].wait()
    cameras = [cameras_ref[:, a : a + 1] for a in range(7)]
    origin = camera_parts(cameras[0:3], cameras[3:6], cameras[6])[13:16]
    copies[1].wait()
    for turn, row in enumerate(partner_rows(index_ref, n_render)):
        order_ref[turn : turn + 1, :] = row
    copies[2].wait()

    picks = [(turn, step) for turn in range(n_render) for step in range(cap // 128)]

    def shade(step):
        lanes = slice(step * width, step * width + width)
        copies[3 + step].wait()
        dense_ref[0:8, lanes] = params_ref[8:16, lanes]
        away = [params_ref[a : a + 1, lanes] + origin[a] for a in range(3)]
        inverse = lax.rsqrt(away[0] * away[0] + away[1] * away[1] + away[2] * away[2])
        basis = harmonic_basis(*[part * inverse for part in away])
        for channel in range(3):
            base = GEOMETRY + 16 * channel
            colour = 0.5 + basis[0] * params_ref[base : base + 1, lanes]
            for level in range(1, 16):
                colour += basis[level] * params_ref[base + level : base + level + 1, lanes]
            first = COLOUR_ROW + channel * views - 8
            dense_ref[first : first + views, lanes] = colour

    def pick(source, groups, skip, turn, step):
        lanes = slice(128 * step, 128 * step + 128)
        index = jnp.broadcast_to(order_ref[turn : turn + 1, lanes], (8, 128))
        lane, block = index & 127, index >> 7
        found = [jnp.zeros((8, 128), F32) for _ in range(groups)]
        for b in range(gaussians // 128):
            here = block == b
            for s in range(groups):
                piece = source[8 * s : 8 * s + 8, 128 * b : 128 * b + 128]
                found[s] = jnp.where(here, lane_pick(piece, lane), found[s])
        for s in range(groups):
            outs[turn][8 * (s + skip) : 8 * (s + skip) + 8, lanes] = found[s]

    for step in range(shades):
        shade(step)
        for turn, at in picks[step * len(picks) // shades : (step + 1) * len(picks) // shades]:
            pick(params_ref, 1, 0, turn, at)
    for turn, at in picks:
        pick(dense_ref, rows // 8 - 1, 1, turn, at)


def entry_coefficients(raw, cam):
    px, py, pz = raw[0], raw[1], raw[2]
    extent = [jnp.exp(raw[3 + a]) for a in range(3)]
    norm = lax.rsqrt(raw[6] * raw[6] + raw[7] * raw[7] + raw[8] * raw[8] + raw[9] * raw[9])
    qw, qx, qy, qz = [raw[6 + a] * norm for a in range(4)]
    turn = [[cam[3 * a + b] for b in range(3)] for a in range(3)]
    x, y, z = [turn[a][0] * px + turn[a][1] * py + turn[a][2] * pz + cam[9 + a] for a in range(3)]
    scale = cam[12] / z
    slope_x, slope_y = x / z, y / z
    u = cam[12] * slope_x + cam[13]
    v = cam[12] * slope_y + cam[14]
    quat = [
        [1.0 - 2.0 * (qy * qy + qz * qz), 2.0 * (qx * qy - qw * qz), 2.0 * (qx * qz + qw * qy)],
        [2.0 * (qx * qy + qw * qz), 1.0 - 2.0 * (qx * qx + qz * qz), 2.0 * (qy * qz - qw * qx)],
        [2.0 * (qx * qz - qw * qy), 2.0 * (qy * qz + qw * qx), 1.0 - 2.0 * (qx * qx + qy * qy)],
    ]
    screen = [
        [scale * (turn[a][b] - slope * turn[2][b]) for b in range(3)]
        for a, slope in ((0, slope_x), (1, slope_y))
    ]
    foot = [
        [sum(screen[a][m] * quat[m][b] for m in range(3)) * extent[b] for b in range(3)]
        for a in range(2)
    ]
    cov_a = sum(foot[0][b] * foot[0][b] for b in range(3)) + dilation
    cov_b = sum(foot[0][b] * foot[1][b] for b in range(3))
    cov_c = sum(foot[1][b] * foot[1][b] for b in range(3)) + dilation
    inverse = 1.0 / (cov_a * cov_c - cov_b * cov_b)
    conic_a, conic_b, conic_c = cov_c * inverse, -cov_b * inverse, cov_a * inverse
    log_opacity = -jnp.log(1.0 + jnp.exp(-raw[10]))
    pull_x = conic_a * u + conic_b * v
    pull_y = conic_c * v + conic_b * u
    return [
        -0.5 * conic_a,
        -conic_b,
        -0.5 * conic_c,
        pull_x,
        pull_y,
        log_opacity - 0.5 * (pull_x * u + pull_y * v),
    ]


def monomials(shape, axis):
    number = lax.broadcasted_iota(jnp.int32, shape, axis)
    pixel = lax.broadcasted_iota(jnp.int32, shape, 1 - axis)
    x = (pixel & 15).astype(F32) - 7.5
    y = (pixel >> 4).astype(F32) - 7.5
    value = jnp.zeros(shape, F32)
    for at, term in enumerate((x * x, x * y, y * y, x, y, jnp.ones_like(x))):
        value = jnp.where((number & 7) == at, term, value)
    return value, number


def fetch(slot, view, views, blocks, turns, found):
    me = lax.axis_index("render")
    per_block = blocks[0].shape[1] // 128
    lane, block = slot & 127, slot >> 7
    found = list(found)
    for ref, turn in zip(blocks, turns):
        first = (me ^ turn) * per_block
        for j in range(per_block):
            hit = block == first + j
            cut = slice(128 * j, 128 * j + 128)
            for p in range(GEOMETRY):
                piece = jnp.broadcast_to(ref[p : p + 1, cut], (8, 128))
                found[p] = jnp.where(hit, lane_pick(piece, lane), found[p])
            for w in range(views):
                seen = hit & (view == w)
                for channel in range(3):
                    p = COLOUR_ROW + channel * views + w
                    piece = jnp.broadcast_to(ref[p : p + 1, cut], (8, 128))
                    at = GEOMETRY + channel
                    found[at] = jnp.where(seen, lane_pick(piece, lane), found[at])
    return found


def meet_kernel(camera_ref, code_ref, live_ref, list_ref, *refs):
    blocks, (slot_ref, cam_ref, part_ref, origin_ref) = refs[:NEAR], refs[NEAR:]
    tiles, length = list_ref.shape
    segments = 128 // tiles
    steps = length // segments
    lists = list_ref[...].astype(F32)
    turned = []
    for segment in range(segments):
        begin = segment * steps
        base = lists[:, begin // 128 * 128 : begin // 128 * 128 + 128]
        turned.append(pltpu.roll(base, 128 - begin % 128, 1) if begin % 128 else base)
    slot_ref[...] = jnp.concatenate(turned, axis=0).T[0:steps, :].astype(jnp.int32)

    views = camera_ref.shape[0]
    lane = lax.broadcasted_iota(jnp.int32, (8, 128), 1)
    by_tile = lax.broadcasted_iota(jnp.int32, (8, 128), 0) < 4
    code, live = jnp.zeros((8, 128), jnp.int32), jnp.zeros((8, 128), jnp.int32)
    for t in range(tiles):
        here = (lane & (tiles - 1)) == t
        code = jnp.where(here, code_ref[0, t], code)
        live = jnp.where(here, live_ref[0, t], live)
    view = code // (CROP * CROP)
    cell = code - view * (CROP * CROP)
    down = cell // CROP
    place = jnp.where(by_tile, view, lane)
    cameras = []
    for c in range(7):
        value = jnp.full((8, 128), camera_ref[0, c])
        for w in range(1, views):
            value = jnp.where(place == w, camera_ref[w, c], value)
        cameras.append(value)
    parts = camera_parts(cameras[0:3], cameras[3:6], cameras[6])
    for c in range(13):
        cam_ref[c : c + 1, :] = parts[c][0:1, :]
    cam_ref[13:14, :] = (8 * CROP - 8 - 16 * (cell - down * CROP)).astype(F32)[0:1, :]
    cam_ref[14:15, :] = (8 * CROP - 8 - 16 * down).astype(F32)[0:1, :]
    cam_ref[15:16, :] = view.astype(F32)[0:1, :]
    cam_ref[16:17, :] = live.astype(F32)[0:1, :]
    row = jnp.where(lane < 32, parts[13], 0.0)
    for a in (1, 2):
        row = row + pltpu.roll(jnp.where(lane < 32, parts[13 + a], 0.0), 32 * a, 1)
    origin_ref[...] = row[4:5, :]

    def group_work(group, _):
        here = pl.ds(pl.multiple_of(group * 8, 8), 8)
        found = [jnp.zeros((8, 128), F32) for _ in range(GEOMETRY + 3)]
        found = fetch(slot_ref[here, :], view, views, blocks, range(NEAR), found)
        for p in range(GEOMETRY + 3):
            part_ref[p, here, :] = found[p]
        return 0

    lax.fori_loop(0, steps // 8, group_work, 0)


def render_kernel(n_render, views, *refs):
    blocks, refs = refs[: n_render - NEAR], refs[n_render - NEAR :]
    slot_ref, cam_ref, part_ref, target_ref, refs = *refs[0:4], refs[4:]
    image_ref, outs, refs = refs[0], refs[1 : 1 + n_render], refs[1 + n_render :]
    raw_ref, stack_ref, wide_ref, alpha_ref, weight_ref, shown_ref, pass_ref, enter_ref, behind_ref, right_ref, sums_ref, lhs_ref, hot_ref, acc_ref = refs
    tiles = target_ref.shape[0]
    entry_rows = slot_ref.shape[0]
    entries = entry_rows * 128
    rows, cap = blocks[0].shape
    me = lax.axis_index("render")
    groups = entry_rows // 8

    def complete(group, _):
        here = pl.ds(pl.multiple_of(group * 8, 8), 8)
        view = jnp.broadcast_to(cam_ref[15:16, :], (8, 128)).astype(jnp.int32)
        found = [part_ref[p, here, :] for p in range(GEOMETRY + 3)]
        found = fetch(slot_ref[here, :], view, views, blocks, range(NEAR, n_render), found)
        for p in range(GEOMETRY + 3):
            raw_ref[p, here, :] = found[p]
        return 0

    lax.fori_loop(0, groups, complete, 0)

    def cam_rows():
        return [jnp.broadcast_to(cam_ref[i : i + 1, :], (8, 128)) for i in range(15)]

    stack_ref[...] = jnp.zeros_like(stack_ref)

    def forward_entries(group, _):
        here = pl.ds(pl.multiple_of(group * 8, 8), 8)
        coefficient = entry_coefficients([raw_ref[p, here, :] for p in range(GEOMETRY)], cam_rows())
        row = lax.broadcasted_iota(jnp.int32, (8, 128), 0) + group * 8
        lane = lax.broadcasted_iota(jnp.int32, (8, 128), 1)
        order = (lane // tiles) * entry_rows + row
        live = order < jnp.broadcast_to(cam_ref[16:17, :], (8, 128)).astype(jnp.int32)
        for c in range(6):
            value = coefficient[c] * LOG2_E
            if c == 5:
                value = jnp.where(live, value, DEAD)
            at = pl.ds(pl.multiple_of(c * entry_rows + group * 8, 8), 8)
            stack_ref[at, :] = value
        for channel in range(3):
            at = pl.ds(pl.multiple_of((8 + channel) * entry_rows + group * 8, 8), 8)
            stack_ref[at, :] = raw_ref[GEOMETRY + channel, here, :]
        return 0

    lax.fori_loop(0, groups, forward_entries, 0)

    chunks = entries // CHUNK

    def chunk_of(chunk):
        return pl.ds(pl.multiple_of(chunk * CHUNK, CHUNK), CHUNK)

    lane = lax.broadcasted_iota(jnp.int32, (8, 128), 1)
    own_tile = (lane & (tiles - 1)) == lax.broadcasted_iota(jnp.int32, (8, 128), 0)

    def widen(row, _):
        value = stack_ref[pl.ds(row, 16, stride=entry_rows), :]
        high, rest = high_low(value)
        middle, low = high_low(rest)

        def spread(part):
            return [
                jnp.where(own_tile, jnp.broadcast_to(part[8 + ch : 9 + ch, :], (8, 128)), 0.0)
                for ch in range(3)
            ]

        zero = jnp.zeros((8, 128), F32)
        bright = spread(high)
        pieces = [high[0:8], middle[0:8], low[0:8], zero] + bright + spread(middle) + bright + [zero]
        lanes = pl.ds(pl.multiple_of(row * 128, 128), 128)
        wide_ref[:, lanes] = jnp.concatenate(pieces, axis=0).astype(BF16)
        return 0

    lax.fori_loop(0, entry_rows, widen, 0)

    value, number = monomials((PIXELS, 32), 1)
    left = jnp.where(number < 24, value, 0.0).astype(BF16)
    segment = lax.broadcasted_iota(jnp.int32, (PIXELS, 128), 1) // tiles
    last = 128 // tiles - 1

    def expose(chunk, _):
        alpha = jnp.exp2(dot_plain(left, wide_ref[0:32, chunk_of(chunk)]))
        for k in range(CHUNK // 128):
            alpha_ref[chunk * (CHUNK // 128) + k] = alpha[:, 128 * k : 128 * k + 128]
        return 0

    lax.fori_loop(0, chunks, expose, 0)

    def colour_rows(row):
        return [
            jnp.broadcast_to(stack_ref[(8 + ch) * entry_rows + row : (8 + ch) * entry_rows + row + 1, :], (8, 128))
            for ch in range(3)
        ]

    def strip_of(strip, part):
        return pl.ds(pl.multiple_of(strip * STRIP + 8 * part, 8), 8)

    parts = STRIP // 8

    def attenuate(strip, _):
        passing = [jnp.ones((8, 128), F32) for _ in range(parts)]
        shown = [[None] * parts for _ in range(3)]
        for row in range(entry_rows):
            colours = colour_rows(row)
            for part in range(parts):
                weight = passing[part] * alpha_ref[row, strip_of(strip, part), :]
                passing[part] = passing[part] - weight
                weight_ref[row, strip_of(strip, part), :] = weight
                for ch in range(3):
                    term = weight * colours[ch]
                    shown[ch][part] = term if row == 0 else shown[ch][part] + term
        for part in range(parts):
            pass_ref[strip_of(strip, part), :] = passing[part]
            for ch in range(3):
                shown_ref[ch, strip_of(strip, part), :] = shown[ch][part]
        return 0

    lax.fori_loop(0, PIXELS // STRIP, attenuate, 0)

    through = pass_ref[...]
    hop = 1
    while hop <= last:
        through = through * jnp.where(segment >= hop, pltpu.roll(through, tiles * hop, 1), 1.0)
        hop *= 2
    enter = jnp.where(segment >= 1, pltpu.roll(through, tiles, 1), 1.0)
    enter_ref[...] = enter
    remain = jnp.where(segment == last, backdrop * through, 0.0)
    open_end = jnp.zeros((PIXELS, 128), F32)
    add = jnp.zeros((PIXELS, 128), F32)
    right = jnp.zeros((PIXELS, 128), F32)
    for channel in range(3):
        alone = shown_ref[channel]
        total = alone * enter + remain
        hop = 1
        while hop <= last:
            total = total + pltpu.roll(total, tiles * hop, 1)
            hop *= 2
        image_ref[:, channel, :] = total.T[0:tiles, :]
        wanted = jnp.concatenate([target_ref[:, channel, :]] * (last + 1), axis=0).T
        residual = total - wanted
        high, low = high_low(residual)
        right = jnp.where((segment == channel) | (segment == 3 + channel), high, right)
        right = jnp.where(segment == 6 + channel, low, right)
        shown_ref[channel] = residual
        open_end = open_end + backdrop * residual
        add = add + residual * alone

    right_ref[...] = right.astype(BF16)

    keep = pass_ref[...]
    hop = 1
    while hop <= last:
        inside = segment + hop <= last
        add = add + keep * jnp.where(inside, pltpu.roll(add, 128 - tiles * hop, 1), 0.0)
        keep = keep * jnp.where(inside, pltpu.roll(keep, 128 - tiles * hop, 1), 1.0)
        hop *= 2
    behind_ref[...] = jnp.where(
        segment < last, pltpu.roll(add + keep * open_end, 128 - tiles, 1), open_end
    )

    def sums_at(strip, number, row):
        return pl.ds(pl.multiple_of(((strip * 9 + number) * entry_rows + row) * 8, 8), 8)

    def descend(strip, _):
        behind = [behind_ref[strip_of(strip, part), :] for part in range(parts)]
        enter = [enter_ref[strip_of(strip, part), :] for part in range(parts)]
        residual = [[shown_ref[ch, strip_of(strip, part), :] for part in range(parts)] for ch in range(3)]
        facing = right_ref[pl.ds(pl.multiple_of(strip * STRIP, STRIP), STRIP), 0:80]
        for row in reversed(range(entry_rows)):
            if row % 2:
                shade = dot_plain(facing, wide_ref[32:112, 128 * row - 128 : 128 * row + 128])
            side = slice(128 * (row % 2), 128 * (row % 2) + 128)
            tint = [None] * 3
            tall = [[None] * 3, [None] * 3]
            for part in range(parts):
                here = [residual[ch][part] for ch in range(3)]
                gap = shade[8 * part : 8 * part + 8, side] - behind[part]
                behind[part] = behind[part] + alpha_ref[row, strip_of(strip, part), :] * gap
                weight = weight_ref[row, strip_of(strip, part), :] * enter[part]
                slope = weight * gap
                for ch in range(3):
                    term = weight * here[ch]
                    tint[ch] = term if part == 0 else tint[ch] + term
                half, up = part % 2, float(part // 2)
                terms = [slope, slope * up, slope * (up * up)] if up else [slope, None, None]
                for power in range(3):
                    if terms[power] is None:
                        continue
                    known = tall[half][power]
                    tall[half][power] = terms[power] if known is None else known + terms[power]
            base = (strip * (STRIP // 16)).astype(F32) - 7.5
            for half in range(2):
                level, rise, bend = tall[half]
                bend = bend + (2.0 * base) * rise + (base * base) * level
                rise = rise + base * level
                for power, value in ((0, level), (1, rise), (2, bend)):
                    at = 3 * half + power
                    sums_ref[sums_at(strip, at, row), :] = value
            for ch in range(3):
                sums_ref[sums_at(strip, 6 + ch, row), :] = tint[ch]
        return 0

    lax.fori_loop(0, PIXELS // STRIP, descend, 0)

    def gather_sums(group, _):
        def summed(number, sub):
            return sum(
                sums_ref[pl.ds((strip * 9 + number) * 8 * entry_rows + group * 64 + sub, 8, stride=8), :]
                for strip in range(PIXELS // STRIP)
            )

        values = [0.0] * 9
        for sub in range(8):
            for half in range(2):
                x = 8.0 * half + sub - 7.5
                level, rise, bend = [summed(3 * half + power, sub) for power in range(3)]
                terms = [(x * x) * level, x * rise, bend, x * level, rise, level]
                for c in range(6):
                    values[c] = values[c] + terms[c]
            for ch in range(3):
                values[6 + ch] = values[6 + ch] + summed(6 + ch, sub)
        for c, value in enumerate(values):
            line = c * entry_rows if c < 6 else (c + 2) * entry_rows
            stack_ref[pl.ds(pl.multiple_of(line + group * 8, 8), 8), :] = value
        return 0

    lax.fori_loop(0, groups, gather_sums, 0)

    def backward_entries(group, _):
        here = pl.ds(pl.multiple_of(group * 8, 8), 8)
        cam = cam_rows()
        given = [
            stack_ref[pl.ds(pl.multiple_of(c * entry_rows + group * 8, 8), 8), :] for c in range(6)
        ]
        _, pull = jax.vjp(
            lambda raw: entry_coefficients(raw, cam), [raw_ref[p, here, :] for p in range(GEOMETRY)]
        )
        (grads,) = pull(given)
        for channel in range(3):
            at = pl.ds(pl.multiple_of((8 + channel) * entry_rows + group * 8, 8), 8)
            grads.append(stack_ref[at, :])
        for p in range(GEOMETRY + 3):
            high, low = high_low(grads[p])
            raw_ref[p, here, :] = high
            raw_ref[GEOMETRY + 3 + p, here, :] = low
        return 0

    lax.fori_loop(0, groups, backward_entries, 0)

    spans = n_render * cap // SPAN
    half_rows = rows * spans
    view = cam_ref[15:16, :].astype(jnp.int32)

    def spread_out(row, _):
        at_lanes = pl.ds(pl.multiple_of(row * 128, 128), 128)
        slot = slot_ref[pl.ds(row, 1), :]
        span, lane = slot // SPAN, slot & (SPAN - 1)
        lanes_of = lax.broadcasted_iota(jnp.int32, (SPAN, 128), 0) == jnp.broadcast_to(lane, (SPAN, 128))
        hot_ref[:, at_lanes] = jnp.where(lanes_of, 1.0, 0.0).astype(BF16)
        in_span = lax.broadcasted_iota(jnp.int32, (spans, 128), 0) == jnp.broadcast_to(span, (spans, 128))
        key = view * spans + span
        in_view = lax.broadcasted_iota(jnp.int32, (views * spans, 128), 0) == jnp.broadcast_to(
            key, (views * spans, 128)
        )
        for part in range(2):
            base = part * half_rows
            pieces = []
            for p in range(COLOUR_ROW):
                if p < GEOMETRY:
                    value = raw_ref[part * (GEOMETRY + 3) + p, pl.ds(row, 1), :]
                    pieces.append(jnp.where(in_span, jnp.broadcast_to(value, (spans, 128)), 0.0))
                else:
                    pieces.append(jnp.zeros((spans, 128), F32))
                if len(pieces) == 2:
                    at = base + (p - 1) * spans
                    lhs_ref[at : at + 2 * spans, at_lanes] = jnp.concatenate(pieces, axis=0).astype(BF16)
                    pieces = []
            for channel in range(3):
                value = raw_ref[part * (GEOMETRY + 3) + GEOMETRY + channel, pl.ds(row, 1), :]
                value = jnp.where(in_view, jnp.broadcast_to(value, (views * spans, 128)), 0.0)
                at = base + (COLOUR_ROW + channel * views) * spans
                lhs_ref[at : at + views * spans, at_lanes] = value.astype(BF16)

    def spread_rows(step, _):
        for i in range(4):
            spread_out(step * 4 + i, 0)
        return 0

    lax.fori_loop(0, entry_rows // 4, spread_rows, 0)
    product = dot_lanes(lhs_ref[...], hot_ref[...])
    for half in range(SPAN // 128):
        at = slice(half * 2 * half_rows, (half + 1) * 2 * half_rows)
        acc_ref[at, :] = product[:, 128 * half : 128 * half + 128]
    for turn in range(n_render):
        for part in range(cap // SPAN):
            span = (me ^ turn) * (cap // SPAN) + part
            for half in range(SPAN // 128):
                cut = slice(128 * half, 128 * half + 128)
                total = (
                    acc_ref[pl.ds(half * 2 * rows * spans + span, rows, stride=spans), :]
                    + acc_ref[pl.ds(half * 2 * rows * spans + rows * spans + span, rows, stride=spans), :]
                )
                first = part * SPAN + 128 * half
                outs[turn][:, first : first + 128] = total


def collect_kernel(n_render, n_view, own, turns, *refs):
    final = turns[-1] == n_render - 1
    blocks, refs = refs[: len(turns)], refs[len(turns) :]
    index_ref, refs = refs[0], refs[1:]
    rows, cap = blocks[0].shape
    spans = own * n_view // SPAN
    if final:
        origin_ref, before_ref, refs = refs[0], refs[1], refs[2:]
        outs, (lhs_ref, hot_ref, acc_ref) = refs[:n_view], refs[n_view:]
    else:
        acc_ref, lhs_ref, hot_ref = refs
    column = lax.axis_index("view")
    order = partner_rows(index_ref, n_render)
    for place, turn in enumerate(turns):
        lanes = slice(place * cap, (place + 1) * cap)
        index = order[turn]
        span, lane = index // SPAN, index & (SPAN - 1)
        hot = lax.broadcasted_iota(jnp.int32, (SPAN, cap), 0) == jnp.broadcast_to(lane, (SPAN, cap))
        hot_ref[:, lanes] = jnp.where(hot, 1.0, 0.0).astype(BF16)
        in_span = lax.broadcasted_iota(jnp.int32, (spans, cap), 0) == jnp.broadcast_to(span, (spans, cap))
        high, low = high_low(blocks[place][...])
        for part, value in ((0, high), (1, low)):
            for p in range(rows):
                at = (part * rows + p) * spans
                piece = jnp.broadcast_to(value[p : p + 1, :], (spans, cap))
                lhs_ref[at : at + spans, lanes] = jnp.where(in_span, piece, 0.0).astype(BF16)
    product = dot_lanes(lhs_ref[...], hot_ref[...])
    for half in range(2):
        at = slice(half * 2 * rows * spans, (half + 1) * 2 * rows * spans)
        piece = product[:, 128 * half : 128 * half + 128]
        acc_ref[at, :] = piece + before_ref[at, :] if final else piece
    if not final:
        return
    strips = own // 128
    for turn in range(n_view):
        for strip in range(strips):
            span = (column ^ turn) * (own // SPAN) + strip // 2
            first = (strip % 2) * 2 * rows * spans
            for p, count, to in ((0, GEOMETRY, 0), (COLOUR_ROW, rows - COLOUR_ROW, GEOMETRY)):
                begin = first + p * spans + span
                outs[turn][pl.ds(to * strips + strip, count, stride=strips), :] = (
                    acc_ref[pl.ds(begin, count, stride=spans), :]
                    + acc_ref[pl.ds(begin + rows * spans, count, stride=spans), :]
                )
        outs[turn][TURN_ROW * strips : TURN_ROW * strips + 1, :] = origin_ref[...]


def owner_kernel(views, n_blocks, final, *refs):
    blocks, refs = refs[:n_blocks], refs[n_blocks:]
    own_ref, refs = refs[0], refs[1:]
    if final:
        before_ref, out_ref, sum_ref = refs
        strips = out_ref.shape[1] // 128
    else:
        (sum_ref,) = refs
        strips = sum_ref.shape[0] // (GEOMETRY + 48)

    def of(ref, p):
        return ref[p * strips : (p + 1) * strips, :]

    def known(p):
        return of(before_ref, p) if final else None

    def plus(total, term):
        return term if total is None else total + term

    position = [of(own_ref, a) for a in range(3)]
    levels = [[known(GEOMETRY + 16 * ch + b) for b in range(16)] for ch in range(3)]
    moved = [known(a) for a in range(3)]
    for block in blocks:
        for w in range(views):
            away = []
            for a in range(3):
                at = 32 * a + w
                offset = block[TURN_ROW * strips : TURN_ROW * strips + 1, at : at + 1]
                away.append(position[a] + jnp.broadcast_to(offset, (strips, 128)))
            inverse = lax.rsqrt(away[0] * away[0] + away[1] * away[1] + away[2] * away[2])
            direction = [part * inverse for part in away]
            basis, pull = jax.vjp(harmonic_basis, *direction)
            tint = [of(block, GEOMETRY + ch * views + w) for ch in range(3)]
            for ch in range(3):
                for b in range(16):
                    levels[ch][b] = plus(levels[ch][b], tint[ch] * basis[b])
            given = [
                sum(tint[ch] * of(own_ref, GEOMETRY + 16 * ch + b) for ch in range(3)) for b in range(16)
            ]
            turned = pull(given)
            along = sum(turned[a] * direction[a] for a in range(3))
            for a in range(3):
                moved[a] = plus(moved[a], inverse * (turned[a] - direction[a] * along))
    totals = [moved[p] if p < 3 else known(p) for p in range(GEOMETRY)]
    for p in range(GEOMETRY):
        for block in blocks:
            totals[p] = plus(totals[p], of(block, p))
    along = sum(totals[TURN_ROW + a] * of(own_ref, TURN_ROW + a) for a in (1, 2, 3))
    totals[TURN_ROW] = -along / of(own_ref, TURN_ROW)
    for p in range(GEOMETRY):
        sum_ref[p * strips : (p + 1) * strips, :] = totals[p]
    for ch in range(3):
        for b in range(16):
            p = GEOMETRY + 16 * ch + b
            sum_ref[p * strips : (p + 1) * strips, :] = levels[ch][b]
    if final:
        count = out_ref.shape[0]
        for strip in range(strips):
            out_ref[:, 128 * strip : 128 * strip + 128] = sum_ref[pl.ds(strip, count, stride=strips), :]


def swap(blocks, axis):
    n = len(blocks)
    return [blocks[0]] + [
        lax.ppermute(blocks[turn], axis, [(i, i ^ turn) for i in range(n)]) for turn in range(1, n)
    ]


def call(kernel, out_shape, scratch, space, *args):
    return pl.pallas_call(
        kernel,
        out_shape=out_shape,
        in_specs=[
            pl.BlockSpec(memory_space=space[i] if isinstance(space, list) else space)
            for i in range(len(args))
        ],
        out_specs=[pl.BlockSpec(memory_space=pltpu.VMEM)] * len(out_shape),
        scratch_shapes=scratch,
        compiler_params=pltpu.CompilerParams(vmem_limit_bytes=(64 if space == pl.ANY else 48) * 1024 * 1024),
    )(*args)


def meet(arrived, cameras, code, live, lists):
    tiles, length = lists.shape
    entry_rows = tiles * length // 128
    return call(
        meet_kernel,
        [
            jax.ShapeDtypeStruct((entry_rows, 128), jnp.int32),
            jax.ShapeDtypeStruct((24, 128), F32),
            jax.ShapeDtypeStruct((GEOMETRY + 3, entry_rows, 128), F32),
            jax.ShapeDtypeStruct((1, 128), F32),
        ],
        [],
        [pltpu.SMEM] * 3 + [pltpu.VMEM] * (1 + NEAR),
        cameras,
        code,
        live,
        lists,
        *arrived[:NEAR],
    )


def render(n_render, views, arrived, slot_lanes, lane_table, part, wanted):
    rows, cap = arrived[0].shape
    entry_rows = slot_lanes.shape[0]
    entries = entry_rows * 128
    spans = n_render * cap // SPAN
    return call(
        partial(render_kernel, n_render, views),
        [jax.ShapeDtypeStruct(wanted.shape, F32)]
        + [jax.ShapeDtypeStruct((rows, cap), F32)] * n_render,
        [
            pltpu.VMEM((2 * (GEOMETRY + 3), entry_rows, 128), F32),
            pltpu.VMEM((16 * entry_rows, 128), F32),
            pltpu.VMEM((112, entries), BF16),
            pltpu.VMEM((entry_rows, PIXELS, 128), F32),
            pltpu.VMEM((entry_rows, PIXELS, 128), F32),
            pltpu.VMEM((3, PIXELS, 128), F32),
            pltpu.VMEM((PIXELS, 128), F32),
            pltpu.VMEM((PIXELS, 128), F32),
            pltpu.VMEM((PIXELS, 128), F32),
            pltpu.VMEM((PIXELS, 128), BF16),
            pltpu.VMEM((9 * PIXELS // STRIP * 8 * entry_rows, 128), F32),
            pltpu.VMEM((2 * rows * spans, entries), BF16),
            pltpu.VMEM((SPAN, entries), BF16),
            pltpu.VMEM((4 * rows * spans, 128), F32),
        ],
        pltpu.VMEM,
        *arrived[NEAR:],
        slot_lanes,
        lane_table,
        part,
        wanted,
    )


def slab(n_render, params, cameras, index):
    views, (count, gaussians), cap = cameras.shape[0], params.shape, index.shape[1]
    rows = -(-(COLOUR_ROW + 3 * views) // 8) * 8
    return call(
        partial(slab_kernel, n_render, views),
        [jax.ShapeDtypeStruct((rows, cap), F32)] * n_render,
        [
            pltpu.VMEM((count, gaussians), F32),
            pltpu.VMEM(cameras.shape, F32),
            pltpu.VMEM((n_render, cap), jnp.int32),
            pltpu.VMEM((n_render, cap), jnp.int32),
            pltpu.VMEM((rows - 8, gaussians), F32),
            pltpu.SemaphoreType.DMA((3 + gaussians // 512,)),
        ],
        pl.ANY,
        params,
        cameras,
        index,
    )


def collect(n_render, n_view, homed, index, origin, own):
    rows, cap = homed[0].shape
    spans = n_view * own // SPAN
    total = jax.ShapeDtypeStruct((4 * rows * spans, 128), F32)

    def scratch(turns):
        return [
            pltpu.VMEM((2 * rows * spans, len(turns) * cap), BF16),
            pltpu.VMEM((SPAN, len(turns) * cap), BF16),
        ]

    near, far = tuple(range(2)), tuple(range(2, n_render))
    (early,) = call(
        partial(collect_kernel, n_render, n_view, own, near),
        [total],
        scratch(near),
        pltpu.VMEM,
        *homed[:2],
        index,
    )
    return call(
        partial(collect_kernel, n_render, n_view, own, far),
        [jax.ShapeDtypeStruct(((rows - 1) * own // 128, 128), F32)] * n_view,
        scratch(far) + [pltpu.VMEM(total.shape, F32)],
        pltpu.VMEM,
        *homed[2:],
        index,
        origin,
        early,
    )


def body(n_render, n_view, params, cameras, send_index, tile_id, tile_count, tile_slot, targets):
    index = send_index[0, 0]
    views = cameras.shape[0]
    own = params.shape[1] // n_view
    mine = lax.dynamic_slice_in_dim(params, lax.axis_index("view") * own, own, 1).reshape(-1, 128)

    arrived = swap(list(slab(n_render, params, cameras, index)), "render")
    slot_lanes, lane_table, part, origin = meet(
        arrived, cameras, tile_id[0], tile_count[0], tile_slot[0, 0]
    )
    image, *returned = render(n_render, views, arrived, slot_lanes, lane_table, part, targets[0, 0])
    homed = swap(returned, "render")
    owned = swap(list(collect(n_render, n_view, homed, index, origin, own)), "view")
    (early,) = call(
        partial(owner_kernel, views, 2, False),
        [jax.ShapeDtypeStruct(mine.shape, F32)],
        [],
        pltpu.VMEM,
        *owned[:2],
        mine,
    )
    (gradients,) = call(
        partial(owner_kernel, views, n_view - 2, True),
        [jax.ShapeDtypeStruct((params.shape[0], own), F32)],
        [pltpu.VMEM(mine.shape, F32)],
        pltpu.VMEM,
        *owned[2:],
        mine,
        early,
    )
    return (image[None, None], gradients)


def solution(mesh):
    in_specs = (
        P(None, ("groups", "render")),
        P(("groups", "view"), None),
        P(("groups", "render"), "view", None, None),
        P(("groups", "render"), "view", None),
        P(("groups", "render"), "view", None),
        P(("groups", "render"), "view", None, None),
        P(("groups", "render"), "view", None, None, None),
    )
    out_specs = (
        P(("groups", "render"), "view", None, None, None),
        P(None, ("groups", "render", "view")),
    )
    work = partial(body, mesh.shape["render"], mesh.shape["view"])
    return jax.shard_map(work, mesh=mesh, in_specs=in_specs, out_specs=out_specs, check_vma=False)
```

```python
from functools import partial

import jax
import jax.numpy as jnp
from jax import lax
from jax.experimental import pallas as pl
from jax.experimental.pallas import tpu as pltpu
from jax.sharding import PartitionSpec as P

CROP = 2
PIXELS = 256
GEOMETRY = 11
COLOUR_ROW = 12
TURN_ROW = 6
SPAN = 256
CHUNK = 4096
STRIP = 256
NEAR = 2
LOG2_E = 1.4426950408889634
DEAD = -1e30

dilation = 0.3
backdrop = 1.0
band_zero = 0.28209479177387814
band_one = 0.4886025119029199
band_two = [
    1.0925484305920792,
    -1.0925484305920792,
    0.31539156525252005,
    -1.0925484305920792,
    0.5462742152960396,
]
band_three = [
    -0.5900435899266435,
    2.890611442640554,
    -0.4570457994644658,
    0.3731763325901154,
    -0.4570457994644658,
    1.445305721320277,
    -0.5900435899266435,
]

F32 = jnp.float32
BF16 = jnp.bfloat16


def harmonic_basis(along_x, along_y, along_z):
    square_x = along_x * along_x
    square_y = along_y * along_y
    square_z = along_z * along_z
    return [
        jnp.full_like(along_x, band_zero),
        -band_one * along_y,
        band_one * along_z,
        -band_one * along_x,
        band_two[0] * along_x * along_y,
        band_two[1] * along_y * along_z,
        band_two[2] * (2.0 * square_z - square_x - square_y),
        band_two[3] * along_x * along_z,
        band_two[4] * (square_x - square_y),
        band_three[0] * along_y * (3.0 * square_x - square_y),
        band_three[1] * along_x * along_y * along_z,
        band_three[2] * along_y * (4.0 * square_z - square_x - square_y),
        band_three[3] * along_z * (2.0 * square_z - 3.0 * square_x - 3.0 * square_y),
        band_three[4] * along_x * (4.0 * square_z - square_x - square_y),
        band_three[5] * along_z * (square_x - square_y),
        band_three[6] * along_x * (square_x - 3.0 * square_y),
    ]


def high_low(value):
    high = value.astype(BF16).astype(F32)
    return high, value - high


def dot_plain(left, right):
    return lax.dot_general(left, right, (((1,), (0,)), ((), ())), preferred_element_type=F32)


def dot_lanes(left, right):
    return lax.dot_general(left, right, (((1,), (1,)), ((), ())), preferred_element_type=F32)


def camera_parts(angles, shift, focal):
    c0, c1, c2 = [jnp.cos(angle) for angle in angles]
    s0, s1, s2 = [jnp.sin(angle) for angle in angles]
    rotation = [
        [c1 * c2, s0 * s1 * c2 - c0 * s2, c0 * s1 * c2 + s0 * s2],
        [c1 * s2, s0 * s1 * s2 + c0 * c2, c0 * s1 * s2 - s0 * c2],
        [-s1, s0 * c1, c0 * c1],
    ]
    origin = [sum(rotation[m][a] * shift[m] for m in range(3)) for a in range(3)]
    return [e for row in rotation for e in row] + shift + [focal] + origin


def lane_pick(source, lanes):
    return jnp.take_along_axis(source, lanes, axis=1, mode="promise_in_bounds")


def partner_rows(index_ref, n_render):
    me = lax.axis_index("render")
    rows = [index_ref[o : o + 1, :] for o in range(n_render)]
    return [
        sum(jnp.where((me ^ turn) == o, rows[o], 0) for o in range(n_render)) for turn in range(n_render)
    ]


def slab_kernel(n_render, views, params_hbm, cameras_hbm, index_hbm, *rest):
    outs, refs = rest[:n_render], rest[n_render:]
    params_ref, cameras_ref, index_ref, order_ref, dense_ref, arrival = refs
    rows, gaussians = outs[0].shape[0], params_ref.shape[1]
    cap = index_ref.shape[1]
    width = 512
    shades = gaussians // width
    count = params_ref.shape[0]
    copies = [
        pltpu.make_async_copy(cameras_hbm, cameras_ref, arrival.at[0]),
        pltpu.make_async_copy(index_hbm, index_ref, arrival.at[1]),
        pltpu.make_async_copy(params_hbm.at[0:8, :], params_ref.at[0:8, :], arrival.at[2]),
    ]
    for step in range(shades):
        lanes = pl.ds(step * width, width)
        copies.append(
            pltpu.make_async_copy(
                params_hbm.at[8:count, lanes], params_ref.at[8:count, lanes], arrival.at[3 + step]
            )
        )
    for copy in copies:
        copy.start()
    copies[0].wait()
    cameras = [cameras_ref[:, a : a + 1] for a in range(7)]
    origin = camera_parts(cameras[0:3], cameras[3:6], cameras[6])[13:16]
    copies[1].wait()
    for turn, row in enumerate(partner_rows(index_ref, n_render)):
        order_ref[turn : turn + 1, :] = row
    copies[2].wait()

    picks = [(turn, step) for turn in range(n_render) for step in range(cap // 128)]

    def shade(step):
        lanes = slice(step * width, step * width + width)
        copies[3 + step].wait()
        dense_ref[0:8, lanes] = params_ref[8:16, lanes]
        away = [params_ref[a : a + 1, lanes] + origin[a] for a in range(3)]
        inverse = lax.rsqrt(away[0] * away[0] + away[1] * away[1] + away[2] * away[2])
        basis = harmonic_basis(*[part * inverse for part in away])
        for channel in range(3):
            base = GEOMETRY + 16 * channel
            colour = 0.5 + basis[0] * params_ref[base : base + 1, lanes]
            for level in range(1, 16):
                colour += basis[level] * params_ref[base + level : base + level + 1, lanes]
            first = COLOUR_ROW + channel * views - 8
            dense_ref[first : first + views, lanes] = colour

    def pick(source, groups, skip, turn, step):
        lanes = slice(128 * step, 128 * step + 128)
        index = jnp.broadcast_to(order_ref[turn : turn + 1, lanes], (8, 128))
        lane, block = index & 127, index >> 7
        found = [jnp.zeros((8, 128), F32) for _ in range(groups)]
        for b in range(gaussians // 128):
            here = block == b
            for s in range(groups):
                piece = source[8 * s : 8 * s + 8, 128 * b : 128 * b + 128]
                found[s] = jnp.where(here, lane_pick(piece, lane), found[s])
        for s in range(groups):
            outs[turn][8 * (s + skip) : 8 * (s + skip) + 8, lanes] = found[s]

    for step in range(shades):
        shade(step)
        for turn, at in picks[step * len(picks) // shades : (step + 1) * len(picks) // shades]:
            pick(params_ref, 1, 0, turn, at)
    for turn, at in picks:
        pick(dense_ref, rows // 8 - 1, 1, turn, at)


def entry_coefficients(raw, cam):
    px, py, pz = raw[0], raw[1], raw[2]
    extent = [jnp.exp(raw[3 + a]) for a in range(3)]
    norm = lax.rsqrt(raw[6] * raw[6] + raw[7] * raw[7] + raw[8] * raw[8] + raw[9] * raw[9])
    qw, qx, qy, qz = [raw[6 + a] * norm for a in range(4)]
    turn = [[cam[3 * a + b] for b in range(3)] for a in range(3)]
    x, y, z = [turn[a][0] * px + turn[a][1] * py + turn[a][2] * pz + cam[9 + a] for a in range(3)]
    scale = cam[12] / z
    slope_x, slope_y = x / z, y / z
    u = cam[12] * slope_x + cam[13]
    v = cam[12] * slope_y + cam[14]
    quat = [
        [1.0 - 2.0 * (qy * qy + qz * qz), 2.0 * (qx * qy - qw * qz), 2.0 * (qx * qz + qw * qy)],
        [2.0 * (qx * qy + qw * qz), 1.0 - 2.0 * (qx * qx + qz * qz), 2.0 * (qy * qz - qw * qx)],
        [2.0 * (qx * qz - qw * qy), 2.0 * (qy * qz + qw * qx), 1.0 - 2.0 * (qx * qx + qy * qy)],
    ]
    screen = [
        [scale * (turn[a][b] - slope * turn[2][b]) for b in range(3)]
        for a, slope in ((0, slope_x), (1, slope_y))
    ]
    foot = [
        [sum(screen[a][m] * quat[m][b] for m in range(3)) * extent[b] for b in range(3)]
        for a in range(2)
    ]
    cov_a = sum(foot[0][b] * foot[0][b] for b in range(3)) + dilation
    cov_b = sum(foot[0][b] * foot[1][b] for b in range(3))
    cov_c = sum(foot[1][b] * foot[1][b] for b in range(3)) + dilation
    inverse = 1.0 / (cov_a * cov_c - cov_b * cov_b)
    conic_a, conic_b, conic_c = cov_c * inverse, -cov_b * inverse, cov_a * inverse
    log_opacity = -jnp.log(1.0 + jnp.exp(-raw[10]))
    pull_x = conic_a * u + conic_b * v
    pull_y = conic_c * v + conic_b * u
    return [
        -0.5 * conic_a,
        -conic_b,
        -0.5 * conic_c,
        pull_x,
        pull_y,
        log_opacity - 0.5 * (pull_x * u + pull_y * v),
    ]


def monomials(shape, axis):
    number = lax.broadcasted_iota(jnp.int32, shape, axis)
    pixel = lax.broadcasted_iota(jnp.int32, shape, 1 - axis)
    x = (pixel & 15).astype(F32) - 7.5
    y = (pixel >> 4).astype(F32) - 7.5
    value = jnp.zeros(shape, F32)
    for at, term in enumerate((x * x, x * y, y * y, x, y, jnp.ones_like(x))):
        value = jnp.where((number & 7) == at, term, value)
    return value, number


def fetch(slot, view, views, blocks, turns, found):
    me = lax.axis_index("render")
    per_block = blocks[0].shape[1] // 128
    lane, block = slot & 127, slot >> 7
    found = list(found)
    for ref, turn in zip(blocks, turns):
        first = (me ^ turn) * per_block
        for j in range(per_block):
            hit = block == first + j
            cut = slice(128 * j, 128 * j + 128)
            for p in range(GEOMETRY):
                piece = jnp.broadcast_to(ref[p : p + 1, cut], (8, 128))
                found[p] = jnp.where(hit, lane_pick(piece, lane), found[p])
            for w in range(views):
                seen = hit & (view == w)
                for channel in range(3):
                    p = COLOUR_ROW + channel * views + w
                    piece = jnp.broadcast_to(ref[p : p + 1, cut], (8, 128))
                    at = GEOMETRY + channel
                    found[at] = jnp.where(seen, lane_pick(piece, lane), found[at])
    return found


def meet_kernel(camera_ref, code_ref, live_ref, list_ref, *refs):
    blocks, (slot_ref, cam_ref, part_ref, origin_ref) = refs[:NEAR], refs[NEAR:]
    tiles, length = list_ref.shape
    segments = 128 // tiles
    steps = length // segments
    lists = list_ref[...].astype(F32)
    turned = []
    for segment in range(segments):
        begin = segment * steps
        base = lists[:, begin // 128 * 128 : begin // 128 * 128 + 128]
        turned.append(pltpu.roll(base, 128 - begin % 128, 1) if begin % 128 else base)
    slot_ref[...] = jnp.concatenate(turned, axis=0).T[0:steps, :].astype(jnp.int32)

    views = camera_ref.shape[0]
    lane = lax.broadcasted_iota(jnp.int32, (8, 128), 1)
    by_tile = lax.broadcasted_iota(jnp.int32, (8, 128), 0) < 4
    code, live = jnp.zeros((8, 128), jnp.int32), jnp.zeros((8, 128), jnp.int32)
    for t in range(tiles):
        here = (lane & (tiles - 1)) == t
        code = jnp.where(here, code_ref[0, t], code)
        live = jnp.where(here, live_ref[0, t], live)
    view = code // (CROP * CROP)
    cell = code - view * (CROP * CROP)
    down = cell // CROP
    place = jnp.where(by_tile, view, lane)
    cameras = []
    for c in range(7):
        value = jnp.full((8, 128), camera_ref[0, c])
        for w in range(1, views):
            value = jnp.where(place == w, camera_ref[w, c], value)
        cameras.append(value)
    parts = camera_parts(cameras[0:3], cameras[3:6], cameras[6])
    for c in range(13):
        cam_ref[c : c + 1, :] = parts[c][0:1, :]
    cam_ref[13:14, :] = (8 * CROP - 8 - 16 * (cell - down * CROP)).astype(F32)[0:1, :]
    cam_ref[14:15, :] = (8 * CROP - 8 - 16 * down).astype(F32)[0:1, :]
    cam_ref[15:16, :] = view.astype(F32)[0:1, :]
    cam_ref[16:17, :] = live.astype(F32)[0:1, :]
    row = jnp.where(lane < 32, parts[13], 0.0)
    for a in (1, 2):
        row = row + pltpu.roll(jnp.where(lane < 32, parts[13 + a], 0.0), 32 * a, 1)
    origin_ref[...] = row[4:5, :]

    def group_work(group, _):
        here = pl.ds(pl.multiple_of(group * 8, 8), 8)
        found = [jnp.zeros((8, 128), F32) for _ in range(GEOMETRY + 3)]
        found = fetch(slot_ref[here, :], view, views, blocks, range(NEAR), found)
        for p in range(GEOMETRY + 3):
            part_ref[p, here, :] = found[p]
        return 0

    lax.fori_loop(0, steps // 8, group_work, 0)


def render_kernel(n_render, views, *refs):
    blocks, refs = refs[: n_render - NEAR], refs[n_render - NEAR :]
    slot_ref, cam_ref, part_ref, target_ref, refs = *refs[0:4], refs[4:]
    image_ref, outs, refs = refs[0], refs[1 : 1 + n_render], refs[1 + n_render :]
    raw_ref, stack_ref, wide_ref, alpha_ref, weight_ref, shown_ref, pass_ref, enter_ref, behind_ref, right_ref, sums_ref, lhs_ref, hot_ref, acc_ref = refs
    tiles = target_ref.shape[0]
    entry_rows = slot_ref.shape[0]
    entries = entry_rows * 128
    rows, cap = blocks[0].shape
    me = lax.axis_index("render")
    groups = entry_rows // 8

    def complete(group, _):
        here = pl.ds(pl.multiple_of(group * 8, 8), 8)
        view = jnp.broadcast_to(cam_ref[15:16, :], (8, 128)).astype(jnp.int32)
        found = [part_ref[p, here, :] for p in range(GEOMETRY + 3)]
        found = fetch(slot_ref[here, :], view, views, blocks, range(NEAR, n_render), found)
        for p in range(GEOMETRY + 3):
            raw_ref[p, here, :] = found[p]
        return 0

    lax.fori_loop(0, groups, complete, 0)

    def cam_rows():
        return [jnp.broadcast_to(cam_ref[i : i + 1, :], (8, 128)) for i in range(15)]

    stack_ref[...] = jnp.zeros_like(stack_ref)

    def forward_entries(group, _):
        here = pl.ds(pl.multiple_of(group * 8, 8), 8)
        coefficient = entry_coefficients([raw_ref[p, here, :] for p in range(GEOMETRY)], cam_rows())
        row = lax.broadcasted_iota(jnp.int32, (8, 128), 0) + group * 8
        lane = lax.broadcasted_iota(jnp.int32, (8, 128), 1)
        order = (lane // tiles) * entry_rows + row
        live = order < jnp.broadcast_to(cam_ref[16:17, :], (8, 128)).astype(jnp.int32)
        for c in range(6):
            value = coefficient[c] * LOG2_E
            if c == 5:
                value = jnp.where(live, value, DEAD)
            at = pl.ds(pl.multiple_of(c * entry_rows + group * 8, 8), 8)
            stack_ref[at, :] = value
        for channel in range(3):
            at = pl.ds(pl.multiple_of((8 + channel) * entry_rows + group * 8, 8), 8)
            stack_ref[at, :] = raw_ref[GEOMETRY + channel, here, :]
        return 0

    lax.fori_loop(0, groups, forward_entries, 0)

    chunks = entries // CHUNK

    def chunk_of(chunk):
        return pl.ds(pl.multiple_of(chunk * CHUNK, CHUNK), CHUNK)

    lane = lax.broadcasted_iota(jnp.int32, (8, 128), 1)
    own_tile = (lane & (tiles - 1)) == lax.broadcasted_iota(jnp.int32, (8, 128), 0)

    def widen(row, _):
        value = stack_ref[pl.ds(row, 16, stride=entry_rows), :]
        high, rest = high_low(value)
        middle, low = high_low(rest)

        def spread(part):
            return [
                jnp.where(own_tile, jnp.broadcast_to(part[8 + ch : 9 + ch, :], (8, 128)), 0.0)
                for ch in range(3)
            ]

        zero = jnp.zeros((8, 128), F32)
        bright = spread(high)
        pieces = [high[0:8], middle[0:8], low[0:8], zero] + bright + spread(middle) + bright + [zero]
        lanes = pl.ds(pl.multiple_of(row * 128, 128), 128)
        wide_ref[:, lanes] = jnp.concatenate(pieces, axis=0).astype(BF16)
        return 0

    lax.fori_loop(0, entry_rows, widen, 0)

    value, number = monomials((PIXELS, 32), 1)
    left = jnp.where(number < 24, value, 0.0).astype(BF16)
    segment = lax.broadcasted_iota(jnp.int32, (PIXELS, 128), 1) // tiles
    last = 128 // tiles - 1

    def expose(chunk, _):
        alpha = jnp.exp2(dot_plain(left, wide_ref[0:32, chunk_of(chunk)]))
        for k in range(CHUNK // 128):
            alpha_ref[chunk * (CHUNK // 128) + k] = alpha[:, 128 * k : 128 * k + 128]
        return 0

    lax.fori_loop(0, chunks, expose, 0)

    def colour_rows(row):
        return [
            jnp.broadcast_to(stack_ref[(8 + ch) * entry_rows + row : (8 + ch) * entry_rows + row + 1, :], (8, 128))
            for ch in range(3)
        ]

    def strip_of(strip, part):
        return pl.ds(pl.multiple_of(strip * STRIP + 8 * part, 8), 8)

    parts = STRIP // 8

    def attenuate(strip, _):
        passing = [jnp.ones((8, 128), F32) for _ in range(parts)]
        shown = [[None] * parts for _ in range(3)]
        for row in range(entry_rows):
            colours = colour_rows(row)
            for part in range(parts):
                weight = passing[part] * alpha_ref[row, strip_of(strip, part), :]
                passing[part] = passing[part] - weight
                weight_ref[row, strip_of(strip, part), :] = weight
                for ch in range(3):
                    term = weight * colours[ch]
                    shown[ch][part] = term if row == 0 else shown[ch][part] + term
        for part in range(parts):
            pass_ref[strip_of(strip, part), :] = passing[part]
            for ch in range(3):
                shown_ref[ch, strip_of(strip, part), :] = shown[ch][part]
        return 0

    lax.fori_loop(0, PIXELS // STRIP, attenuate, 0)

    through = pass_ref[...]
    hop = 1
    while hop <= last:
        through = through * jnp.where(segment >= hop, pltpu.roll(through, tiles * hop, 1), 1.0)
        hop *= 2
    enter = jnp.where(segment >= 1, pltpu.roll(through, tiles, 1), 1.0)
    enter_ref[...] = enter
    remain = jnp.where(segment == last, backdrop * through, 0.0)
    open_end = jnp.zeros((PIXELS, 128), F32)
    add = jnp.zeros((PIXELS, 128), F32)
    right = jnp.zeros((PIXELS, 128), F32)
    for channel in range(3):
        alone = shown_ref[channel]
        total = alone * enter + remain
        hop = 1
        while hop <= last:
            total = total + pltpu.roll(total, tiles * hop, 1)
            hop *= 2
        image_ref[:, channel, :] = total.T[0:tiles, :]
        wanted = jnp.concatenate([target_ref[:, channel, :]] * (last + 1), axis=0).T
        residual = total - wanted
        high, low = high_low(residual)
        right = jnp.where((segment == channel) | (segment == 3 + channel), high, right)
        right = jnp.where(segment == 6 + channel, low, right)
        shown_ref[channel] = residual
        open_end = open_end + backdrop * residual
        add = add + residual * alone

    right_ref[...] = right.astype(BF16)

    keep = pass_ref[...]
    hop = 1
    while hop <= last:
        inside = segment + hop <= last
        add = add + keep * jnp.where(inside, pltpu.roll(add, 128 - tiles * hop, 1), 0.0)
        keep = keep * jnp.where(inside, pltpu.roll(keep, 128 - tiles * hop, 1), 1.0)
        hop *= 2
    behind_ref[...] = jnp.where(
        segment < last, pltpu.roll(add + keep * open_end, 128 - tiles, 1), open_end
    )

    def sums_at(strip, number, row):
        return pl.ds(pl.multiple_of(((strip * 9 + number) * entry_rows + row) * 8, 8), 8)

    def descend(strip, _):
        behind = [behind_ref[strip_of(strip, part), :] for part in range(parts)]
        enter = [enter_ref[strip_of(strip, part), :] for part in range(parts)]
        residual = [[shown_ref[ch, strip_of(strip, part), :] for part in range(parts)] for ch in range(3)]
        facing = right_ref[pl.ds(pl.multiple_of(strip * STRIP, STRIP), STRIP), 0:80]
        for row in reversed(range(entry_rows)):
            if row % 2:
                shade = dot_plain(facing, wide_ref[32:112, 128 * row - 128 : 128 * row + 128])
            side = slice(128 * (row % 2), 128 * (row % 2) + 128)
            tint = [None] * 3
            tall = [[None] * 3, [None] * 3]
            for part in range(parts):
                here = [residual[ch][part] for ch in range(3)]
                gap = shade[8 * part : 8 * part + 8, side] - behind[part]
                behind[part] = behind[part] + alpha_ref[row, strip_of(strip, part), :] * gap
                weight = weight_ref[row, strip_of(strip, part), :] * enter[part]
                slope = weight * gap
                for ch in range(3):
                    term = weight * here[ch]
                    tint[ch] = term if part == 0 else tint[ch] + term
                half, up = part % 2, float(part // 2)
                terms = [slope, slope * up, slope * (up * up)] if up else [slope, None, None]
                for power in range(3):
                    if terms[power] is None:
                        continue
                    known = tall[half][power]
                    tall[half][power] = terms[power] if known is None else known + terms[power]
            base = (strip * (STRIP // 16)).astype(F32) - 7.5
            for half in range(2):
                level, rise, bend = tall[half]
                bend = bend + (2.0 * base) * rise + (base * base) * level
                rise = rise + base * level
                for power, value in ((0, level), (1, rise), (2, bend)):
                    at = 3 * half + power
                    sums_ref[sums_at(strip, at, row), :] = value
            for ch in range(3):
                sums_ref[sums_at(strip, 6 + ch, row), :] = tint[ch]
        return 0

    lax.fori_loop(0, PIXELS // STRIP, descend, 0)

    def gather_sums(group, _):
        def summed(number, sub):
            return sum(
                sums_ref[pl.ds((strip * 9 + number) * 8 * entry_rows + group * 64 + sub, 8, stride=8), :]
                for strip in range(PIXELS // STRIP)
            )

        values = [0.0] * 9
        for sub in range(8):
            for half in range(2):
                x = 8.0 * half + sub - 7.5
                level, rise, bend = [summed(3 * half + power, sub) for power in range(3)]
                terms = [(x * x) * level, x * rise, bend, x * level, rise, level]
                for c in range(6):
                    values[c] = values[c] + terms[c]
            for ch in range(3):
                values[6 + ch] = values[6 + ch] + summed(6 + ch, sub)
        for c, value in enumerate(values):
            line = c * entry_rows if c < 6 else (c + 2) * entry_rows
            stack_ref[pl.ds(pl.multiple_of(line + group * 8, 8), 8), :] = value
        return 0

    lax.fori_loop(0, groups, gather_sums, 0)

    def backward_entries(group, _):
        here = pl.ds(pl.multiple_of(group * 8, 8), 8)
        cam = cam_rows()
        given = [
            stack_ref[pl.ds(pl.multiple_of(c * entry_rows + group * 8, 8), 8), :] for c in range(6)
        ]
        _, pull = jax.vjp(
            lambda raw: entry_coefficients(raw, cam), [raw_ref[p, here, :] for p in range(GEOMETRY)]
        )
        (grads,) = pull(given)
        for channel in range(3):
            at = pl.ds(pl.multiple_of((8 + channel) * entry_rows + group * 8, 8), 8)
            grads.append(stack_ref[at, :])
        for p in range(GEOMETRY + 3):
            high, low = high_low(grads[p])
            raw_ref[p, here, :] = high
            raw_ref[GEOMETRY + 3 + p, here, :] = low
        return 0

    lax.fori_loop(0, groups, backward_entries, 0)

    spans = n_render * cap // SPAN
    half_rows = rows * spans
    view = cam_ref[15:16, :].astype(jnp.int32)

    def spread_out(row, _):
        at_lanes = pl.ds(pl.multiple_of(row * 128, 128), 128)
        slot = slot_ref[pl.ds(row, 1), :]
        span, lane = slot // SPAN, slot & (SPAN - 1)
        lanes_of = lax.broadcasted_iota(jnp.int32, (SPAN, 128), 0) == jnp.broadcast_to(lane, (SPAN, 128))
        hot_ref[:, at_lanes] = jnp.where(lanes_of, 1.0, 0.0).astype(BF16)
        in_span = lax.broadcasted_iota(jnp.int32, (spans, 128), 0) == jnp.broadcast_to(span, (spans, 128))
        key = view * spans + span
        in_view = lax.broadcasted_iota(jnp.int32, (views * spans, 128), 0) == jnp.broadcast_to(
            key, (views * spans, 128)
        )
        for part in range(2):
            base = part * half_rows
            pieces = []
            for p in range(COLOUR_ROW):
                if p < GEOMETRY:
                    value = raw_ref[part * (GEOMETRY + 3) + p, pl.ds(row, 1), :]
                    pieces.append(jnp.where(in_span, jnp.broadcast_to(value, (spans, 128)), 0.0))
                else:
                    pieces.append(jnp.zeros((spans, 128), F32))
                if len(pieces) == 2:
                    at = base + (p - 1) * spans
                    lhs_ref[at : at + 2 * spans, at_lanes] = jnp.concatenate(pieces, axis=0).astype(BF16)
                    pieces = []
            for channel in range(3):
                value = raw_ref[part * (GEOMETRY + 3) + GEOMETRY + channel, pl.ds(row, 1), :]
                value = jnp.where(in_view, jnp.broadcast_to(value, (views * spans, 128)), 0.0)
                at = base + (COLOUR_ROW + channel * views) * spans
                lhs_ref[at : at + views * spans, at_lanes] = value.astype(BF16)

    def spread_rows(step, _):
        for i in range(8):
            spread_out(step * 8 + i, 0)
        return 0

    lax.fori_loop(0, entry_rows // 8, spread_rows, 0)
    product = dot_lanes(lhs_ref[...], hot_ref[...])
    for half in range(SPAN // 128):
        at = slice(half * 2 * half_rows, (half + 1) * 2 * half_rows)
        acc_ref[at, :] = product[:, 128 * half : 128 * half + 128]
    for turn in range(n_render):
        for part in range(cap // SPAN):
            span = (me ^ turn) * (cap // SPAN) + part
            for half in range(SPAN // 128):
                cut = slice(128 * half, 128 * half + 128)
                total = (
                    acc_ref[pl.ds(half * 2 * rows * spans + span, rows, stride=spans), :]
                    + acc_ref[pl.ds(half * 2 * rows * spans + rows * spans + span, rows, stride=spans), :]
                )
                first = part * SPAN + 128 * half
                outs[turn][:, first : first + 128] = total


def collect_kernel(n_render, n_view, own, turns, *refs):
    final = turns[-1] == n_render - 1
    blocks, refs = refs[: len(turns)], refs[len(turns) :]
    index_ref, refs = refs[0], refs[1:]
    rows, cap = blocks[0].shape
    spans = own * n_view // SPAN
    if final:
        origin_ref, before_ref, refs = refs[0], refs[1], refs[2:]
        outs, (lhs_ref, hot_ref, acc_ref) = refs[:n_view], refs[n_view:]
    else:
        acc_ref, lhs_ref, hot_ref = refs
    column = lax.axis_index("view")
    order = partner_rows(index_ref, n_render)
    for place, turn in enumerate(turns):
        lanes = slice(place * cap, (place + 1) * cap)
        index = order[turn]
        span, lane = index // SPAN, index & (SPAN - 1)
        hot = lax.broadcasted_iota(jnp.int32, (SPAN, cap), 0) == jnp.broadcast_to(lane, (SPAN, cap))
        hot_ref[:, lanes] = jnp.where(hot, 1.0, 0.0).astype(BF16)
        in_span = lax.broadcasted_iota(jnp.int32, (spans, cap), 0) == jnp.broadcast_to(span, (spans, cap))
        high, low = high_low(blocks[place][...])
        for part, value in ((0, high), (1, low)):
            for p in range(rows):
                at = (part * rows + p) * spans
                piece = jnp.broadcast_to(value[p : p + 1, :], (spans, cap))
                lhs_ref[at : at + spans, lanes] = jnp.where(in_span, piece, 0.0).astype(BF16)
    product = dot_lanes(lhs_ref[...], hot_ref[...])
    for half in range(2):
        at = slice(half * 2 * rows * spans, (half + 1) * 2 * rows * spans)
        piece = product[:, 128 * half : 128 * half + 128]
        acc_ref[at, :] = piece + before_ref[at, :] if final else piece
    if not final:
        return
    strips = own // 128
    for turn in range(n_view):
        for strip in range(strips):
            span = (column ^ turn) * (own // SPAN) + strip // 2
            first = (strip % 2) * 2 * rows * spans
            for p, count, to in ((0, GEOMETRY, 0), (COLOUR_ROW, rows - COLOUR_ROW, GEOMETRY)):
                begin = first + p * spans + span
                outs[turn][pl.ds(to * strips + strip, count, stride=strips), :] = (
                    acc_ref[pl.ds(begin, count, stride=spans), :]
                    + acc_ref[pl.ds(begin + rows * spans, count, stride=spans), :]
                )
        outs[turn][TURN_ROW * strips : TURN_ROW * strips + 1, :] = origin_ref[...]


def owner_kernel(views, n_blocks, final, *refs):
    blocks, refs = refs[:n_blocks], refs[n_blocks:]
    own_ref, refs = refs[0], refs[1:]
    if final:
        before_ref, out_ref, sum_ref = refs
        strips = out_ref.shape[1] // 128
    else:
        (sum_ref,) = refs
        strips = sum_ref.shape[0] // (GEOMETRY + 48)

    def of(ref, p):
        return ref[p * strips : (p + 1) * strips, :]

    def known(p):
        return of(before_ref, p) if final else None

    def plus(total, term):
        return term if total is None else total + term

    position = [of(own_ref, a) for a in range(3)]
    levels = [[known(GEOMETRY + 16 * ch + b) for b in range(16)] for ch in range(3)]
    moved = [known(a) for a in range(3)]
    for block in blocks:
        for w in range(views):
            away = []
            for a in range(3):
                at = 32 * a + w
                offset = block[TURN_ROW * strips : TURN_ROW * strips + 1, at : at + 1]
                away.append(position[a] + jnp.broadcast_to(offset, (strips, 128)))
            inverse = lax.rsqrt(away[0] * away[0] + away[1] * away[1] + away[2] * away[2])
            direction = [part * inverse for part in away]
            basis, pull = jax.vjp(harmonic_basis, *direction)
            tint = [of(block, GEOMETRY + ch * views + w) for ch in range(3)]
            for ch in range(3):
                for b in range(16):
                    levels[ch][b] = plus(levels[ch][b], tint[ch] * basis[b])
            given = [
                sum(tint[ch] * of(own_ref, GEOMETRY + 16 * ch + b) for ch in range(3)) for b in range(16)
            ]
            turned = pull(given)
            along = sum(turned[a] * direction[a] for a in range(3))
            for a in range(3):
                moved[a] = plus(moved[a], inverse * (turned[a] - direction[a] * along))
    totals = [moved[p] if p < 3 else known(p) for p in range(GEOMETRY)]
    for p in range(GEOMETRY):
        for block in blocks:
            totals[p] = plus(totals[p], of(block, p))
    along = sum(totals[TURN_ROW + a] * of(own_ref, TURN_ROW + a) for a in (1, 2, 3))
    totals[TURN_ROW] = -along / of(own_ref, TURN_ROW)
    for p in range(GEOMETRY):
        sum_ref[p * strips : (p + 1) * strips, :] = totals[p]
    for ch in range(3):
        for b in range(16):
            p = GEOMETRY + 16 * ch + b
            sum_ref[p * strips : (p + 1) * strips, :] = levels[ch][b]
    if final:
        count = out_ref.shape[0]
        for strip in range(strips):
            out_ref[:, 128 * strip : 128 * strip + 128] = sum_ref[pl.ds(strip, count, stride=strips), :]


def swap(blocks, axis):
    n = len(blocks)
    return [blocks[0]] + [
        lax.ppermute(blocks[turn], axis, [(i, i ^ turn) for i in range(n)]) for turn in range(1, n)
    ]


def call(kernel, out_shape, scratch, space, *args):
    return pl.pallas_call(
        kernel,
        out_shape=out_shape,
        in_specs=[
            pl.BlockSpec(memory_space=space[i] if isinstance(space, list) else space)
            for i in range(len(args))
        ],
        out_specs=[pl.BlockSpec(memory_space=pltpu.VMEM)] * len(out_shape),
        scratch_shapes=scratch,
        compiler_params=pltpu.CompilerParams(vmem_limit_bytes=(64 if space == pl.ANY else 48) * 1024 * 1024),
    )(*args)


def meet(arrived, cameras, code, live, lists):
    tiles, length = lists.shape
    entry_rows = tiles * length // 128
    return call(
        meet_kernel,
        [
            jax.ShapeDtypeStruct((entry_rows, 128), jnp.int32),
            jax.ShapeDtypeStruct((24, 128), F32),
            jax.ShapeDtypeStruct((GEOMETRY + 3, entry_rows, 128), F32),
            jax.ShapeDtypeStruct((1, 128), F32),
        ],
        [],
        [pltpu.SMEM] * 3 + [pltpu.VMEM] * (1 + NEAR),
        cameras,
        code,
        live,
        lists,
        *arrived[:NEAR],
    )


def render(n_render, views, arrived, slot_lanes, lane_table, part, wanted):
    rows, cap = arrived[0].shape
    entry_rows = slot_lanes.shape[0]
    entries = entry_rows * 128
    spans = n_render * cap // SPAN
    return call(
        partial(render_kernel, n_render, views),
        [jax.ShapeDtypeStruct(wanted.shape, F32)]
        + [jax.ShapeDtypeStruct((rows, cap), F32)] * n_render,
        [
            pltpu.VMEM((2 * (GEOMETRY + 3), entry_rows, 128), F32),
            pltpu.VMEM((17 * entry_rows, 128), F32),
            pltpu.VMEM((112, entries), BF16),
            pltpu.VMEM((entry_rows, PIXELS, 128), F32),
            pltpu.VMEM((entry_rows, PIXELS, 128), F32),
            pltpu.VMEM((3, PIXELS, 128), F32),
            pltpu.VMEM((PIXELS, 128), F32),
            pltpu.VMEM((PIXELS, 128), F32),
            pltpu.VMEM((PIXELS, 128), F32),
            pltpu.VMEM((PIXELS, 128), BF16),
            pltpu.VMEM((9 * PIXELS // STRIP * 8 * entry_rows, 128), F32),
            pltpu.VMEM((2 * rows * spans, entries), BF16),
            pltpu.VMEM((SPAN, entries), BF16),
            pltpu.VMEM((4 * rows * spans + spans, 128), F32),
        ],
        pltpu.VMEM,
        *arrived[NEAR:],
        slot_lanes,
        lane_table,
        part,
        wanted,
    )


def slab(n_render, params, cameras, index):
    views, (count, gaussians), cap = cameras.shape[0], params.shape, index.shape[1]
    rows = -(-(COLOUR_ROW + 3 * views) // 8) * 8
    return call(
        partial(slab_kernel, n_render, views),
        [jax.ShapeDtypeStruct((rows, cap), F32)] * n_render,
        [
            pltpu.VMEM((count, gaussians), F32),
            pltpu.VMEM(cameras.shape, F32),
            pltpu.VMEM((n_render, cap), jnp.int32),
            pltpu.VMEM((n_render, cap), jnp.int32),
            pltpu.VMEM((rows - 8, gaussians), F32),
            pltpu.SemaphoreType.DMA((3 + gaussians // 512,)),
        ],
        pl.ANY,
        params,
        cameras,
        index,
    )


def collect(n_render, n_view, homed, index, origin, own):
    rows, cap = homed[0].shape
    spans = n_view * own // SPAN
    total = jax.ShapeDtypeStruct((4 * rows * spans, 128), F32)

    def scratch(turns):
        return [
            pltpu.VMEM((2 * rows * spans, len(turns) * cap), BF16),
            pltpu.VMEM((SPAN, len(turns) * cap), BF16),
        ]

    near, far = tuple(range(2)), tuple(range(2, n_render))
    (early,) = call(
        partial(collect_kernel, n_render, n_view, own, near),
        [total],
        scratch(near),
        pltpu.VMEM,
        *homed[:2],
        index,
    )
    return call(
        partial(collect_kernel, n_render, n_view, own, far),
        [jax.ShapeDtypeStruct(((rows - 1) * own // 128, 128), F32)] * n_view,
        scratch(far) + [pltpu.VMEM(total.shape, F32)],
        pltpu.VMEM,
        *homed[2:],
        index,
        origin,
        early,
    )


def body(n_render, n_view, params, cameras, send_index, tile_id, tile_count, tile_slot, targets):
    index = send_index[0, 0]
    views = cameras.shape[0]
    own = params.shape[1] // n_view
    mine = lax.dynamic_slice_in_dim(params, lax.axis_index("view") * own, own, 1).reshape(-1, 128)

    arrived = swap(list(slab(n_render, params, cameras, index)), "render")
    slot_lanes, lane_table, part, origin = meet(
        arrived, cameras, tile_id[0], tile_count[0], tile_slot[0, 0]
    )
    image, *returned = render(n_render, views, arrived, slot_lanes, lane_table, part, targets[0, 0])
    homed = swap(returned, "render")
    owned = swap(list(collect(n_render, n_view, homed, index, origin, own)), "view")
    (early,) = call(
        partial(owner_kernel, views, 2, False),
        [jax.ShapeDtypeStruct(mine.shape, F32)],
        [],
        pltpu.VMEM,
        *owned[:2],
        mine,
    )
    (gradients,) = call(
        partial(owner_kernel, views, n_view - 2, True),
        [jax.ShapeDtypeStruct((params.shape[0], own), F32)],
        [pltpu.VMEM(mine.shape, F32)],
        pltpu.VMEM,
        *owned[2:],
        mine,
        early,
    )
    return (image[None, None], gradients)


def solution(mesh):
    in_specs = (
        P(None, ("groups", "render")),
        P(("groups", "view"), None),
        P(("groups", "render"), "view", None, None),
        P(("groups", "render"), "view", None),
        P(("groups", "render"), "view", None),
        P(("groups", "render"), "view", None, None),
        P(("groups", "render"), "view", None, None, None),
    )
    out_specs = (
        P(("groups", "render"), "view", None, None, None),
        P(None, ("groups", "render", "view")),
    )
    work = partial(body, mesh.shape["render"], mesh.shape["view"])
    return jax.shard_map(work, mesh=mesh, in_specs=in_specs, out_specs=out_specs, check_vma=False)
```
